128 devices in a mesh: dom: 32 (over z, y, core), sub: 4 (over x).
Axes of the slice: x: 4, y: 4, z: 4, core: 2. Of those that a mesh axis runs over, the one named last changes fastest.
Arguments:
- velocity: float32 [5, 1048576], P(None, ('dom', 'sub')), may hold values from -6 to 6
- position: float32 [3, 1048576], P(None, ('dom', 'sub')), may hold values from 0 to 1
- inv_mass: float32 [1048576], P(('dom', 'sub')), may hold values from 0.05 to 0.3
- connectivity: int32 [4, 1048576], P(None, ('dom', 'sub')), may hold values from 0 to 8447, as said below
- shape_grad: float32 [2, 4, 1048576], P(None, None, ('dom', 'sub')), may hold values from -3 to 3
- area: float32 [1048576], P(('dom', 'sub')), may hold values from 0.5 to 2
- thickness: float32 [1048576], P(('dom', 'sub')), may hold values from 0.5 to 1.5
- yield_stress: float32 [1048576], P(('dom', 'sub')), may hold values from 0.5 to 3
- stress: float32 [5, 5, 1048576], P(None, None, ('dom', 'sub')), may hold values from -6 to 6
- contact_owner: int32 [1048576, 1], P(('dom', 'sub')), may hold values from 0 to 127; in each aligned block of 8192 rows (0 to 8191, 8192 to 16383, ...) at most 128 rows name the same one
- face_center: float32 [3, 262144], P(None, ('dom', 'sub')), may hold values from 0 to 1
- face_angle: float32 [2, 262144], P(None, ('dom', 'sub')), may hold values from -3.140625 to 3.140625
- face_stiffness: float32 [262144], P(('dom', 'sub')), may hold values from 1 to 10
- ghost_list: int32 [65536], P(('dom', 'sub')), may hold values from 0 to 2047
- pair_node: int32 [16384], P(('dom', 'sub')), may hold values from 0 to 127
- pair_face: int32 [16384], P(('dom', 'sub')), may hold values from 0 to 19
- pair_count: int32 [128], P(('dom', 'sub')), may hold values from 16 to 128, as said below
Outputs:
- new_velocity: float32 [5, 1048576], P(None, ('dom', 'sub'))
- new_stress: float32 [5, 5, 1048576], P(None, None, ('dom', 'sub'))
The draws below stay inside these ranges and needn't reach their ends.
Inputs may be any that keep to these rules, and one draw needn't show every extreme that they name: `connectivity`: the corners of the element at local index e of a device lie in e .. e + 256; on the first device at least 128, on the last below 8320. `contact_owner`: the 8192 nodes of one device name any one contact device at most 128 times; some device reaches 128. `pair_count`: some device's count is 128 in every draw.
All inputs are finite; a program needn't handle non-finite values.
Results may differ from the reference program's by a relative error of at most 0.0003.
Values sent between devices are 32-bit elements; how exact they have to be, the bound alone decides.
A program may use at most 128 MiB of HBM per device.

```python
import math
import jax
import jax.numpy as jnp
import numpy as np
from jax import lax

NODE_DEV = 8192
TILE = 128
NODES = 1048576
ELEMS = 1048576
HALO = 128
CAP = 128
FACE_DEV = 2048
FACES = 262144
GHOST = 256
NODE_TILES = 128
FACE_TILES = 20
PAIRS = 128
N_DOM = 32
N_SUB = 4
DEVICES = 128


def draw_connectivity(key, part):
    groups = ELEMS // NODE_DEV
    owner_dev = jnp.arange(ELEMS, dtype=jnp.int32) // NODE_DEV
    local = jnp.arange(ELEMS, dtype=jnp.int32) % NODE_DEV
    lower = jnp.where(owner_dev == 0, jnp.maximum(HALO - local, 0), 0)
    upper = jnp.where(owner_dev == groups - 1, jnp.minimum(2 * HALO - 2, NODE_DEV + HALO - 3 - local), 2 * HALO - 2)
    offset = jax.random.randint(key, (ELEMS,), lower, upper)
    base = local + offset
    corners = jnp.array([0, 1, 2, 3], dtype=jnp.int32)
    return (base[None, :] + corners[:, None]).astype(jnp.int32)


def draw_pair_count(key, part):
    groups = N_DOM * N_SUB
    halving = jax.random.randint(jax.random.fold_in(key, 11), (groups,), 0, 4)
    counts = PAIRS // 2 ** halving
    fullest = jax.random.randint(jax.random.fold_in(key, 12), (), 0, groups)
    return counts.at[fullest].set(PAIRS).astype(jnp.int32)


def with_ends(values, own_key, low, top_value):
    spot = [jax.random.randint(jax.random.fold_in(own_key, axis), (), 0, length) for axis, length in enumerate(values.shape)]
    main_axis = values.shape.index(max(values.shape))
    beside = spot[:main_axis] + [(spot[main_axis] + 1) % values.shape[main_axis]] + spot[main_axis + 1:]
    return values.at[tuple(spot)].set(low).at[tuple(beside)].set(top_value)


def shard_levels(own_key, dims, split, least, high):
    factor_of, own = 1.0, jax.random.fold_in(own_key, 6)
    for axis_at, blocks in split:
        heights = jnp.exp(jax.random.uniform(jax.random.fold_in(own, axis_at), (blocks,), jnp.float32, least / len(split), high / len(split)))
        factor_of = factor_of * jnp.repeat(heights, dims[axis_at] // blocks).reshape([-1 if axis == axis_at else 1 for axis in range(len(dims))])
    return factor_of


def shared_out(own_key, own, number, rows, amount, top, most, skew):
    sequence = jax.random.permutation(own_key, amount)
    heavy_load, ordinary = portions_of(amount, rows * top, most, skew, True), portions_of(amount, rows * top, most, skew, False)
    places = jnp.arange(amount)

    def named(lengths, turn):
        used = int((lengths > 0).sum())
        fixed = max(1, used // 4)
        shifted = fixed + (places - fixed + turn * (used - fixed)) % max(1, amount - fixed)
        return jnp.zeros((amount,), jnp.int32).at[sequence[jnp.where(places < fixed, places, shifted)]].set(jnp.asarray(lengths, jnp.int32))

    lengths = jnp.where(number % 4 == 0, named(heavy_load, number // 4), named(ordinary, number - number // 4 - 1))
    mixed = jax.random.permutation(jax.random.fold_in(own, 3), amount)
    donor, receiver = mixed[0:amount // 2 * 2:2], mixed[1:amount // 2 * 2:2]
    room = jnp.minimum(lengths[donor] - 1, most - lengths[receiver]) // 2
    room = jnp.where((donor == sequence[0]) | (receiver == sequence[0]) | (lengths[receiver] == 0), 0, jnp.maximum(room, 0))
    shifted = jax.random.randint(jax.random.fold_in(own, 4), (amount // 2,), 0, 1 << 20) % (room + 1)
    lengths = lengths.at[donor].add(-shifted).at[receiver].add(shifted)
    members = jnp.searchsorted(jnp.cumsum(lengths), jnp.arange(rows * top), side="right").astype(jnp.int32)
    listing = members.reshape(top, rows).T
    listing = listing[jax.random.permutation(jax.random.fold_in(own, 1), rows)]
    turn = jax.random.randint(jax.random.fold_in(own, 2), (rows, 1), 0, top)
    return jnp.take_along_axis(listing, (jnp.arange(top)[None, :] + turn) % top, axis=1)


def portions_of(count, total, most, skew, full):
    portions = [(1 << 20) // math.isqrt(grade ** skew) + 1 for grade in range(1, count + 1)]
    largest = most if full else min(most, max(-(-total // count), total * portions[0] // sum(portions)))
    least = 1 if total - largest >= count - 1 else 0
    given, spare = [largest] + [least] * (count - 1), total - largest - least * (count - 1)
    while spare > 0:
        movable = [i for i in range(1, count) if given[i] < largest] or [i for i in range(1, count) if given[i] < most]
        whole, budget = sum([portions[i] for i in movable]), spare
        for i in movable:
            addition = min(most - given[i], max(1, budget * portions[i] // whole), spare)
            given[i] = given[i] + addition
            spare = spare - addition
    return np.array(given)


def centred(rng, shape, spread, limit, pieces=(), kind=jnp.bfloat16):
    result = jax.random.normal(rng, shape, jnp.float32) * spread
    if len(pieces) > 0:
        result = shard_levels(rng, shape, pieces, -0.22, 0.18) * result
    return jnp.clip(result, min=-limit, max=limit).astype(kind)


def setup_inputs(seed: int = 0) -> dict:
    key_of = jax.random.split(jax.random.key(seed), 18)
    velocity = centred(key_of[0], (5, NODES), 1.0, 6.0, ((1, 128),), jnp.float32)
    position = jnp.clip(1.0 * jax.random.uniform(key_of[1], (3, NODES), jnp.float32) ** shard_levels(key_of[1], (3, NODES), ((1, 128),), -0.2, 0.2), 0.0, 1.0)
    inv_mass = jnp.clip(jnp.exp(math.log(0.3) - 1.7917595 * jax.random.uniform(key_of[2], (NODES,), jnp.float32) ** shard_levels(key_of[2], (NODES,), ((0, 128),), -0.2, 0.2)), 0.05, 0.3)
    connectivity = draw_connectivity(jax.random.fold_in(key_of[17], 71), 0)
    shape_grad = centred(key_of[4], (2, 4, ELEMS), 0.5, 3.0, ((2, 128),), jnp.float32)
    area = jnp.clip(jnp.exp(math.log(2.0) - 1.3862944 * jax.random.uniform(key_of[5], (ELEMS,), jnp.float32) ** shard_levels(key_of[5], (ELEMS,), ((0, 128),), -0.2, 0.2)), 0.5, 2.0)
    thickness = jnp.clip(0.5 + 1.0 * jax.random.uniform(key_of[6], (ELEMS,), jnp.float32) ** shard_levels(key_of[6], (ELEMS,), ((0, 128),), -0.2, 0.2), 0.5, 1.5)
    yield_stress = jnp.clip(jnp.exp(math.log(3.0) - 1.7917595 * jax.random.uniform(key_of[7], (ELEMS,), jnp.float32) ** shard_levels(key_of[7], (ELEMS,), ((0, 128),), -0.2, 0.2)), 0.5, 3.0)
    stress = centred(key_of[8], (5, 5, ELEMS), 1.0, 6.0, ((2, 128),), jnp.float32)
    contact_owner_keys = jax.random.split(jax.random.fold_in(key_of[9], 1), NODES // NODE_DEV)
    contact_owner_turns = jax.random.permutation(jax.random.fold_in(key_of[9], 3), NODES // NODE_DEV)
    contact_owner = jax.vmap(lambda own, number: shared_out(jax.random.fold_in(key_of[9], 2), own, number, NODE_DEV, DEVICES, 1, CAP, 2))(contact_owner_keys, contact_owner_turns).reshape((NODES, 1))
    face_center = jnp.clip(1.0 * jax.random.uniform(key_of[10], (3, FACES), jnp.float32) ** shard_levels(key_of[10], (3, FACES), ((1, 128),), -0.2, 0.2), 0.0, 1.0)
    face_angle = jnp.clip(jax.random.uniform(key_of[11], (2, FACES), jnp.float32, -3.140625, 3.140625), -3.140625, 3.140625)
    face_stiffness = jnp.clip(jnp.exp(math.log(10.0) - 2.3025851 * jax.random.uniform(key_of[12], (FACES,), jnp.float32) ** shard_levels(key_of[12], (FACES,), ((0, 128),), -0.2, 0.2)), 1.0, 10.0)
    ghost_list = with_ends(jax.random.randint(key_of[13], (2 * GHOST * DEVICES,), 0, FACE_DEV), jax.random.fold_in(key_of[13], 1), 0, FACE_DEV - 1).astype(jnp.int32)
    pair_node = with_ends(jax.random.randint(key_of[14], (PAIRS * DEVICES,), 0, NODE_TILES), jax.random.fold_in(key_of[14], 1), 0, NODE_TILES - 1).astype(jnp.int32)
    pair_face = with_ends(jax.random.randint(key_of[15], (PAIRS * DEVICES,), 0, FACE_TILES), jax.random.fold_in(key_of[15], 1), 0, FACE_TILES - 1).astype(jnp.int32)
    pair_count = draw_pair_count(jax.random.fold_in(key_of[17], 71), 0)
    return dict(velocity=velocity, position=position, inv_mass=inv_mass, connectivity=connectivity, shape_grad=shape_grad, area=area, thickness=thickness, yield_stress=yield_stress, stress=stress, contact_owner=contact_owner, face_center=face_center, face_angle=face_angle, face_stiffness=face_stiffness, ghost_list=ghost_list, pair_node=pair_node, pair_face=pair_face, pair_count=pair_count)


LOBATTO_POINTS = (-1.0, -0.6546536707079771, 0.0, 0.6546536707079771, 1.0)
LOBATTO_WEIGHTS = (0.1, 49.0 / 90.0, 32.0 / 45.0, 49.0 / 90.0, 0.1)
PLANE_MODULUS = 1.0 / 0.91
POISSON = 0.3
SHEAR_MODULUS = 5.0 / 6.0 / 2.6
DAMPING = 0.3
REACH_SQ = 0.5

def element_forces(corner, grads, area, thickness, yield_stress, old_stress):
    vel_x, vel_y, vel_z, rot_x, rot_y = (corner[0], corner[1], corner[2], corner[3], corner[4])
    grad_x, grad_y = (grads[0], grads[1])
    memb_xx = lax.optimization_barrier(jnp.sum(grad_x * vel_x, axis=0))
    bend_xx = lax.optimization_barrier(jnp.sum(grad_x * rot_y, axis=0))
    memb_yy = lax.optimization_barrier(jnp.sum(grad_y * vel_y, axis=0))
    bend_yy = -lax.optimization_barrier(jnp.sum(grad_y * rot_x, axis=0))
    memb_xy = lax.optimization_barrier(jnp.sum(grad_y * vel_x + grad_x * vel_y, axis=0))
    bend_xy = lax.optimization_barrier(jnp.sum(grad_y * rot_y - grad_x * rot_x, axis=0))
    shear_xz = lax.optimization_barrier(jnp.sum(grad_x * vel_z, axis=0)) + 0.25 * lax.optimization_barrier(jnp.sum(rot_y, axis=0))
    shear_yz = lax.optimization_barrier(jnp.sum(grad_y * vel_z, axis=0)) - 0.25 * lax.optimization_barrier(jnp.sum(rot_x, axis=0))
    layers = []
    membrane = []
    moments = []
    for layer in range(5):
        height = 0.5 * thickness * LOBATTO_POINTS[layer]
        strain_xx = memb_xx + height * bend_xx
        strain_yy = memb_yy + height * bend_yy
        strain_xy = memb_xy + height * bend_xy
        trial_xx = old_stress[layer, 0] + PLANE_MODULUS * (strain_xx + POISSON * strain_yy)
        trial_yy = old_stress[layer, 1] + PLANE_MODULUS * (strain_yy + POISSON * strain_xx)
        trial_xy = old_stress[layer, 2] + PLANE_MODULUS * 0.5 * (1.0 - POISSON) * strain_xy
        trial_xz = old_stress[layer, 3] + SHEAR_MODULUS * shear_xz
        trial_yz = old_stress[layer, 4] + SHEAR_MODULUS * shear_yz
        mises = jnp.sqrt(0.25 * (trial_xx + trial_yy) ** 2 + 0.75 * (trial_xx - trial_yy) ** 2 + 3.0 * (trial_xy ** 2 + trial_xz ** 2 + trial_yz ** 2))
        factor = yield_stress / jnp.maximum(mises, yield_stress)
        updated = jnp.stack([trial_xx, trial_yy, trial_xy, trial_xz, trial_yz]) * factor
        layers.append(updated)
        weight = LOBATTO_WEIGHTS[layer] * 0.5 * thickness * area
        membrane.append(weight * updated)
        moments.append(weight * height * updated[0:3])
    new_stress = jnp.stack(layers)
    force_sum = sum(membrane)
    moment_sum = sum(moments)
    force_x = grad_x * force_sum[0] + grad_y * force_sum[2]
    force_y = grad_y * force_sum[1] + grad_x * force_sum[2]
    force_z = grad_x * force_sum[3] + grad_y * force_sum[4]
    moment_x = -(grad_y * moment_sum[1] + grad_x * moment_sum[2]) - 0.25 * force_sum[4]
    moment_y = grad_x * moment_sum[0] + grad_y * moment_sum[2] + 0.25 * force_sum[3]
    return (jnp.stack([force_x, force_y, force_z, moment_x, moment_y]), new_stress)

def slot_ranks(target, number):
    ordering = jnp.argsort(target, stable=True).astype(jnp.int32)
    ordered = target[ordering]
    totals = jnp.bincount(target, length=number).astype(jnp.int32)
    starts = jnp.cumsum(totals).astype(jnp.int32) - totals
    within = jnp.arange(target.shape[0], dtype=jnp.int32) - starts[ordered]
    return jnp.zeros(target.shape[0], jnp.int32).at[ordering].set(within)

def face_normals(face_angle):
    azimuth, elevation = (face_angle[0], face_angle[1])
    return jnp.stack([jnp.cos(azimuth) * jnp.cos(elevation), jnp.sin(azimuth) * jnp.cos(elevation), jnp.sin(elevation)])

def pair_forces(node_block, face_block, live):
    offset = node_block[0:3, :, :, None] - face_block[0:3, :, None, :]
    normal = face_block[3:6, :, None, :]
    depth = jnp.maximum(-lax.optimization_barrier(jnp.sum(normal * offset, axis=0)), 0.0)
    reach = jnp.exp(-lax.optimization_barrier(jnp.sum(offset * offset, axis=0)) / REACH_SQ)
    along = lax.optimization_barrier(jnp.sum(normal * node_block[3:6, :, :, None], axis=0))
    magnitude = face_block[6][:, None, :] * reach * depth * (1.0 - DAMPING * along)
    magnitude = magnitude * node_block[6][:, :, None] * live[:, None, None]
    return jnp.einsum('bij,cbj->cbi', magnitude, face_block[3:6], precision=lax.Precision.HIGHEST)

def reference(velocity, position, inv_mass, connectivity, shape_grad, area, thickness, yield_stress, stress, contact_owner, face_center, face_angle, face_stiffness, ghost_list, pair_node, pair_face, pair_count):
    devices = N_DOM * N_SUB
    capacity = 2 * NODE_DEV // devices
    ftype = velocity.dtype
    owner_dev = (jnp.arange(ELEMS, dtype=jnp.int32) // NODE_DEV).astype(jnp.int32)
    gnode = (owner_dev[None, :] * NODE_DEV + connectivity - HALO).astype(jnp.int32)

    def per_device(inputs):
        nodes_of, grads, area_of, thick_of, yield_of, stress_of = inputs
        return element_forces(velocity[:, nodes_of], grads, area_of, thick_of, yield_of, stress_of)
    forces, new_stress = lax.map(per_device, (gnode.reshape(4, devices, NODE_DEV).transpose(1, 0, 2), shape_grad.reshape(2, 4, devices, NODE_DEV).transpose(2, 0, 1, 3), area.reshape(devices, NODE_DEV), thickness.reshape(devices, NODE_DEV), yield_stress.reshape(devices, NODE_DEV), stress.reshape(5, 5, devices, NODE_DEV).transpose(2, 0, 1, 3)))
    forces = forces.transpose(1, 2, 0, 3).reshape(5, 4, ELEMS)
    new_stress = new_stress.transpose(1, 2, 0, 3).reshape(5, 5, ELEMS)
    internal = jnp.zeros_like(velocity).at[:, gnode].add(forces)
    owner = contact_owner[:, 0].reshape(devices, NODE_DEV)
    ranks = lax.map(lambda target: slot_ranks(target, devices), owner)
    source = jnp.arange(devices, dtype=jnp.int32)[:, None]
    gslot = (owner * (devices * capacity) + source * capacity + ranks).reshape(-1)
    payload = jnp.concatenate([position, velocity[0:3], jnp.ones((1, NODES), ftype)], axis=0)
    received = jnp.zeros((7, devices * devices * capacity), ftype).at[:, gslot].set(payload)
    received = received.reshape(7, devices, devices * capacity).transpose(1, 0, 2)
    face_data = jnp.concatenate([face_center, face_normals(face_angle), face_stiffness[None, :]], axis=0)
    by_dev = face_data.reshape(7, devices, FACE_DEV)
    lists = ghost_list.reshape(devices, 2 * GHOST)
    lent = jnp.take_along_axis(by_dev, lists[None, :, :], axis=2)
    blank = jnp.zeros((7, 1, GHOST), ftype)
    from_prev = jnp.concatenate([blank, lent[:, :-1, GHOST:]], axis=1)
    from_next = jnp.concatenate([lent[:, 1:, :GHOST], blank], axis=1)
    faces_all = jnp.concatenate([from_prev, by_dev, from_next], axis=2).transpose(1, 0, 2)
    block = 64 if PAIRS % 64 == 0 else 8
    node_pairs = pair_node.reshape(devices, PAIRS)
    face_pairs = pair_face.reshape(devices, PAIRS)

    def contact_device(inputs):
        nodes_of, faces_of, pnodes, pfaces, live_count = inputs
        node_tiles = nodes_of.reshape(7, NODE_TILES, TILE)
        face_tiles = faces_of.reshape(7, FACE_TILES, TILE)

        def per_block(index):
            start = index * block
            pn = lax.dynamic_slice_in_dim(pnodes, start, block)
            pf = lax.dynamic_slice_in_dim(pfaces, start, block)
            live = (start + jnp.arange(block, dtype=jnp.int32) < live_count).astype(ftype)
            return pair_forces(jnp.take(node_tiles, pn, axis=1), jnp.take(face_tiles, pf, axis=1), live)
        parts = lax.map(per_block, jnp.arange(PAIRS // block, dtype=jnp.int32))
        parts = parts.transpose(0, 2, 1, 3).reshape(PAIRS, 3, TILE)
        summed = jax.ops.segment_sum(parts, pnodes, num_segments=NODE_TILES)
        return summed.transpose(1, 0, 2).reshape(3, NODE_TILES * TILE)
    contact_all = lax.map(contact_device, (received, faces_all, node_pairs, face_pairs, pair_count))
    contact = contact_all.transpose(1, 0, 2).reshape(3, -1)[:, gslot]
    total = (-internal).at[0:3].add(contact)
    new_velocity = velocity + inv_mass[None, :] * total
    return (new_velocity, new_stress)
```

```python
import functools

import jax
import jax.numpy as jnp
from jax import lax
from jax.experimental import pallas as pl
from jax.experimental.pallas import tpu as pltpu
from jax.sharding import PartitionSpec as P

TILE = 128
HALO = 128
GHOST = 256
NODE_DEV = 8192
ROWS = NODE_DEV // 128
FACE_DEV = 2048
FACE_TILES = 20
DEVICES = 128
PAIRS = 128
EXT = ROWS + 8

LOBATTO_POINTS = (-1.0, -0.6546536707079771, 0.0, 0.6546536707079771, 1.0)
LOBATTO_WEIGHTS = (0.1, 49.0 / 90.0, 32.0 / 45.0, 49.0 / 90.0, 0.1)
PLANE_MODULUS = 1.0 / 0.91
POISSON = 0.3
SHEAR_MODULUS = 5.0 / 6.0 / 2.6
DAMPING = 0.3
REACH_SQ = 0.5
LOG2E = 1.4426950408889634

BF = jnp.bfloat16
F32 = jnp.float32
NT = (((1,), (1,)), ((), ()))
NN = (((1,), (0,)), ((), ()))


def dot(a, b, dims):
    return lax.dot_general(a, b, dims, preferred_element_type=F32)


def onehot(count, row):
    where = lax.broadcasted_iota(jnp.int32, (count, row.shape[1]), 0)
    return jnp.where(where == row, 1.0, 0.0).astype(BF)


def split(x, parts):
    out = []
    for _ in range(parts - 1):
        head = x.astype(BF)
        out.append(head)
        x = x - head.astype(F32)
    out.append(x.astype(BF))
    return out


def lane_aligned(x, size):
    return pl.ds(pl.multiple_of(x * size, size), size)


NODE_PARTS = 3


def slots_kernel(owner_ref, pos_ref, vel_ref, rank_ref, out_ref, run, acc, tri):
    later = lax.broadcasted_iota(jnp.int32, (256, 384), 0)
    column = lax.broadcasted_iota(jnp.int32, (256, 384), 1)
    tri[...] = jnp.where((later < column) | (column >= 256), 1.0, 0.0).astype(BF)
    run[...] = jnp.zeros_like(run)

    def rank_block(b):
        at = lane_aligned(b, 256)
        own = owner_ref[0:1, at]
        where = lax.broadcasted_iota(jnp.int32, (DEVICES, 256), 0)
        hot = jnp.where(where == own, 1.0, 0.0)
        counts = dot(hot.astype(BF), tri[...], NN)
        base = run[...]
        seen = counts[:, :256] + jnp.concatenate([base, base], axis=1)
        rank_ref[0:1, at] = jnp.sum(hot * seen, axis=0, keepdims=True)
        run[...] = base + counts[:, 256:]

    def rank_step(b, _):
        rank_block(2 * b)
        rank_block(2 * b + 1)
        return 0

    lax.fori_loop(0, NODE_DEV // 512, rank_step, 0)
    acc[...] = jnp.zeros_like(acc)

    def place(b, _):
        at = lane_aligned(b, 1024)
        own = owner_ref[0:1, at]
        column = (own & 1) * 128 + rank_ref[0:1, at].astype(jnp.int32)
        hot = onehot(256, column)
        group = onehot(64, own // 2)
        rows = []
        for c in range(6):
            value = pos_ref[c : c + 1, at] if c < 3 else vel_ref[c - 3 : c - 2, at]
            rows += [group * part for part in split(value, NODE_PARTS)]
        rows.append(group)
        placed = dot(jnp.concatenate(rows, axis=0), hot, NT)
        for c in range(6):
            first = c * NODE_PARTS * 64
            total = placed[first : first + 64]
            for part in range(1, NODE_PARTS):
                total = total + placed[first + part * 64 : first + part * 64 + 64]
            acc[c * 64 : c * 64 + 64, :] += total
        acc[384:448, :] += placed[6 * NODE_PARTS * 64 :]
        return 0

    lax.fori_loop(0, NODE_DEV // 1024, place, 0)
    for first in range(0, 64, 8):
        for low in range(2):
            for c in range(8):
                rows = pl.ds(first * 16 + low * 8 + c, 8, stride=16)
                if c < 7:
                    part = acc[c * 64 + first : c * 64 + first + 8, low * 128 : low * 128 + 128]
                else:
                    part = jnp.zeros((8, 128), F32)
                out_ref[rows, :] = part


def slots(owner, position, velocity):
    return pl.pallas_call(
        slots_kernel,
        out_shape=(
            jax.ShapeDtypeStruct((1, NODE_DEV), F32),
            jax.ShapeDtypeStruct((DEVICES * 8, 128), F32),
        ),
        scratch_shapes=[
            pltpu.VMEM((DEVICES, 128), F32),
            pltpu.VMEM((448, 256), F32),
            pltpu.VMEM((256, 384), BF),
        ],
        compiler_params=pltpu.CompilerParams(vmem_limit_bytes=40 * 2**20),
        name="slots",
    )(owner, position, velocity)


def lend_kernel(list_ref, face_ref, out_ref):
    for g in range(4):
        index = jnp.broadcast_to(list_ref[:, 128 * g : 128 * g + 128], (8, 128))
        low, high = index & 127, index >> 7
        found = jnp.zeros((8, 128), F32)
        for t in range(FACE_DEV // 128):
            part = jnp.take_along_axis(face_ref[:, 128 * t : 128 * t + 128], low, axis=1)
            found = jnp.where(high == t, part, found)
        out_ref[:, 128 * g : 128 * g + 128] = found


def lend(ghost_list, faces):
    return pl.pallas_call(
        lend_kernel,
        out_shape=jax.ShapeDtypeStruct((8, 2 * GHOST), F32),
        name="lend",
    )(ghost_list, faces)


def constitutive(corner, grad_x, grad_y, area, thickness, limit, old):
    def over(f):
        total = f(0)
        for a in range(1, 4):
            total = total + f(a)
        return total

    vx, vy, vz, rx, ry = corner
    memb_xx = over(lambda a: grad_x[a] * vx[a])
    bend_xx = over(lambda a: grad_x[a] * ry[a])
    memb_yy = over(lambda a: grad_y[a] * vy[a])
    bend_yy = -over(lambda a: grad_y[a] * rx[a])
    memb_xy = over(lambda a: grad_y[a] * vx[a] + grad_x[a] * vy[a])
    bend_xy = over(lambda a: grad_y[a] * ry[a] - grad_x[a] * rx[a])
    shear_xz = over(lambda a: grad_x[a] * vz[a]) + 0.25 * over(lambda a: ry[a])
    shear_yz = over(lambda a: grad_y[a] * vz[a]) - 0.25 * over(lambda a: rx[a])
    add_xz, add_yz = SHEAR_MODULUS * shear_xz, SHEAR_MODULUS * shear_yz
    half = 0.5 * thickness
    volume = half * area
    new, force, moment = [], [0.0] * 5, [0.0] * 3
    for layer in range(5):
        height = half * LOBATTO_POINTS[layer]
        exx = memb_xx + height * bend_xx
        eyy = memb_yy + height * bend_yy
        exy = memb_xy + height * bend_xy
        t0 = old(layer, 0) + PLANE_MODULUS * (exx + POISSON * eyy)
        t1 = old(layer, 1) + PLANE_MODULUS * (eyy + POISSON * exx)
        t2 = old(layer, 2) + PLANE_MODULUS * 0.5 * (1.0 - POISSON) * exy
        t3 = old(layer, 3) + add_xz
        t4 = old(layer, 4) + add_yz
        plus, minus = t0 + t1, t0 - t1
        mises = jnp.sqrt(
            0.25 * (plus * plus) + 0.75 * (minus * minus) + 3.0 * (t2 * t2 + t3 * t3 + t4 * t4)
        )
        factor = limit / jnp.maximum(mises, limit)
        updated = [t * factor for t in (t0, t1, t2, t3, t4)]
        new.append(updated)
        weight = LOBATTO_WEIGHTS[layer] * volume
        weighted = [weight * u for u in updated]
        force = [f + w for f, w in zip(force, weighted)]
        moment = [m + height * w for m, w in zip(moment, weighted)]
    corners = []
    for a in range(4):
        gx, gy = grad_x[a], grad_y[a]
        corners.append(
            [
                gx * force[0] + gy * force[2],
                gy * force[1] + gx * force[2],
                gx * force[3] + gy * force[4],
                -(gy * moment[1] + gx * moment[2]) - 0.25 * force[4],
                gx * moment[0] + gy * moment[2] + 0.25 * force[3],
            ]
        )
    return new, corners


def elements_kernel(
    vel_ref, low_ref, high_ref, conn_ref, grad_ref, area_ref, thick_ref, limit_ref, stress_ref,
    new_ref, sum_ref, vel, conn, grad, stress, spread,
):
    vel[pl.ds(0, 5, stride=EXT), :] = low_ref[...]
    vel[pl.ds(ROWS + 1, 5, stride=EXT), :] = high_ref[...]

    def unpack(j, _):
        at = lane_aligned(j, 128)
        vel[pl.ds(j + 1, 5, stride=EXT), :] = vel_ref[:, at]
        conn[pl.ds(j, 4, stride=ROWS), :] = conn_ref[:, at] - 128 * j
        for axis in range(2):
            grad[pl.ds(axis * 4 * ROWS + j, 4, stride=ROWS), :] = grad_ref[axis, :, at]
        for layer in range(5):
            stress[pl.ds(layer * 5 * ROWS + j, 5, stride=ROWS), :] = stress_ref[layer, :, at]
        return 0

    lax.fori_loop(0, ROWS, unpack, 0, unroll=8)
    spread[...] = jnp.zeros_like(spread)

    def group(g, _):
        def rows(field):
            return pl.ds(pl.multiple_of(field * ROWS + 8 * g, 8), 8)

        here = pl.ds(pl.multiple_of(8 * g, 8), 8)
        index = [conn[rows(a), :] for a in range(4)]
        low = [i & 127 for i in index]
        part_of = [i >> 7 for i in index]
        corner = []
        for c in range(5):
            window = [vel[pl.ds(c * EXT + 8 * g + k, 8), :] for k in range(3)]
            values = []
            for a in range(4):
                got = [jnp.take_along_axis(w, low[a], axis=1) for w in window]
                values.append(
                    jnp.where(part_of[a] == 0, got[0], jnp.where(part_of[a] == 1, got[1], got[2]))
                )
            corner.append(values)
        grad_x = [grad[rows(a), :] for a in range(4)]
        grad_y = [grad[rows(4 + a), :] for a in range(4)]
        new, forces = constitutive(
            corner, grad_x, grad_y, area_ref[here, :], thick_ref[here, :], limit_ref[here, :],
            lambda layer, c: stress[rows(5 * layer + c), :],
        )
        for layer in range(5):
            for c in range(5):
                stress[rows(5 * layer + c), :] = new[layer][c]
        for a in range(4):
            for c in range(5):
                spread[a, pl.ds(64 * g + c, 8, stride=8), :] = forces[a][c]
        return 0

    lax.fori_loop(0, 8, group, 0)

    def pack(j, _):
        at = lane_aligned(j, 128)
        for layer in range(5):
            new_ref[layer, :, at] = stress[pl.ds(layer * 5 * ROWS + j, 5, stride=ROWS), :]
        return 0

    lax.fori_loop(0, ROWS, pack, 0, unroll=8)
    sum_ref[...] = jnp.zeros_like(sum_ref)

    def scatter(b):
        at = lane_aligned(b, 256)
        index = jnp.concatenate([conn_ref[a : a + 1, at] for a in range(4)], axis=1) - 256 * b
        hot = onehot(256, index & 255)
        upper = (index >> 8).astype(F32)
        value = jnp.concatenate(
            [
                spread[a, pl.ds(pl.multiple_of(16 * b + 8 * h, 8), 8), :]
                for a in range(4)
                for h in range(2)
            ],
            axis=1,
        )
        high = value * upper
        both = split(value - high, 2) + split(high, 2)
        found = dot(jnp.concatenate(both, axis=0), hot, NT)
        sum_ref[:, at] += found[0:8] + found[8:16]
        sum_ref[:, lane_aligned(b + 1, 256)] += found[16:24] + found[24:32]

    def scatter_step(b, _):
        scatter(2 * b)
        scatter(2 * b + 1)
        return 0

    lax.fori_loop(0, ROWS // 4, scatter_step, 0)


def elements(velocity, low, high, connectivity, shape_grad, area, thickness, limit, stress):
    return pl.pallas_call(
        elements_kernel,
        out_shape=(
            jax.ShapeDtypeStruct((5, 5, NODE_DEV), F32),
            jax.ShapeDtypeStruct((8, NODE_DEV + 256), F32),
        ),
        scratch_shapes=[
            pltpu.VMEM((5 * EXT, 128), F32),
            pltpu.VMEM((4 * ROWS, 128), jnp.int32),
            pltpu.VMEM((8 * ROWS, 128), F32),
            pltpu.VMEM((25 * ROWS, 128), F32),
            pltpu.VMEM((4, 8 * ROWS, 128), F32),
        ],
        compiler_params=pltpu.CompilerParams(vmem_limit_bytes=40 * 2**20),
        name="elements",
    )(velocity, low, high, connectivity, shape_grad, area, thickness, limit, stress)


def contact_kernel(count_ref, node_ref, face_of_ref, faces_ref, nodes_ref, out_ref, table):
    def expand(f, _):
        x = faces_ref[:, lane_aligned(f, 128)]
        r, m, stiff = [x[i : i + 1] for i in range(3)], [x[i : i + 1] for i in range(3, 6)], x[6:7]
        apart = m[0] * r[0] + m[1] * r[1] + m[2] * r[2]
        square = r[0] * r[0] + r[1] * r[1] + r[2] * r[2]
        scaled = [(2.0 / REACH_SQ * LOG2E) * v for v in r]
        strength = stiff * jnp.exp2((-LOG2E / REACH_SQ) * square)
        stacked = jnp.concatenate([*m, apart, *scaled, strength], axis=0).T
        for q in range(8):
            table[f, q] = jnp.broadcast_to(stacked[:, q : q + 1], (128, 128))
        return 0

    lax.fori_loop(0, FACE_TILES, expand, 0)
    out_ref[...] = jnp.zeros_like(out_ref)

    def pair(q, _):
        n, f = node_ref[q], face_of_ref[q]
        x = nodes_ref[n]
        p = [jnp.broadcast_to(x[i : i + 1], (8, 128)) for i in range(3)]
        u = [jnp.broadcast_to(-DAMPING * x[i : i + 1], (8, 128)) for i in range(3, 6)]
        square = x[0:1] * x[0:1] + x[1:2] * x[1:2] + x[2:3] * x[2:3]
        scale = x[6:7] * jnp.exp2((-LOG2E / REACH_SQ) * square)
        total = [jnp.zeros((8, 128), F32) for _ in range(3)]
        for k in range(16):
            mx, my, mz, apart, rx, ry, rz, stiff = [table[f, i, 8 * k : 8 * k + 8] for i in range(8)]
            depth = jnp.maximum(apart - (mx * p[0] + my * p[1] + mz * p[2]), 0.0)
            reach = jnp.exp2(rx * p[0] + ry * p[1] + rz * p[2])
            along = 1.0 + (mx * u[0] + my * u[1] + mz * u[2])
            size = (stiff * reach) * (depth * along)
            total = [t + size * m for t, m in zip(total, (mx, my, mz))]
        force = [scale * jnp.sum(t, axis=0, keepdims=True) for t in total]
        out_ref[n, 0:3] += jnp.concatenate(force, axis=0)
        return 0

    lax.fori_loop(0, count_ref[0], pair, 0)


def contact_forces(count, node, face, faces, nodes):
    smem = pl.BlockSpec(memory_space=pltpu.SMEM)
    vmem = pl.BlockSpec(memory_space=pltpu.VMEM)
    return pl.pallas_call(
        contact_kernel,
        out_shape=jax.ShapeDtypeStruct((DEVICES, 4, 128), F32),
        in_specs=[smem, smem, smem, vmem, vmem],
        scratch_shapes=[pltpu.VMEM((FACE_TILES, 8, 128, 128), F32)],
        compiler_params=pltpu.CompilerParams(vmem_limit_bytes=40 * 2**20),
        name="contact",
    )(count, node, face, faces, nodes)


def finish_kernel(back_ref, owner_ref, rank_ref, sum_ref, low_ref, high_ref, vel_ref, mass_ref, out_ref, side):
    for c in range(3):
        turned = back_ref[pl.ds(c, 128, stride=4), :].T
        for i, part in enumerate(split(turned, 2)):
            side[128 * c : 128 * c + 128, 128 * i : 128 * i + 128] = part

    def block(b):
        at = lane_aligned(b, 256)
        own = onehot(128, owner_ref[0:1, at])
        found = dot(side[...], jnp.concatenate([own, own], axis=0), NN)
        rank = rank_ref[0:1, at].astype(jnp.int32)
        mine = lax.broadcasted_iota(jnp.int32, (128, 256), 0) == rank
        contact = [
            jnp.sum(jnp.where(mine, found[128 * c : 128 * c + 128], 0.0), axis=0, keepdims=True)
            for c in range(3)
        ]
        contact = jnp.concatenate([*contact, jnp.zeros((2, 256), F32)], axis=0)
        inner = sum_ref[0:5, pl.ds(pl.multiple_of(b * 256 + 128, 128), 256)]
        out_ref[:, at] = vel_ref[:, at] + mass_ref[0:1, at] * (contact - inner)

    def step(b, _):
        block(2 * b)
        block(2 * b + 1)
        return 0

    lax.fori_loop(0, NODE_DEV // 512, step, 0)
    for ref, at in ((low_ref, pl.ds(0, 128)), (high_ref, pl.ds(NODE_DEV - 128, 128))):
        out_ref[:, at] -= mass_ref[0:1, at] * ref[0:5, :]


def finish(back, owner, rank, summed, low, high, velocity, inv_mass):
    return pl.pallas_call(
        finish_kernel,
        out_shape=jax.ShapeDtypeStruct((5, NODE_DEV), F32),
        scratch_shapes=[pltpu.VMEM((384, 256), BF)],
        compiler_params=pltpu.CompilerParams(vmem_limit_bytes=40 * 2**20),
        name="finish",
    )(back, owner, rank, summed, low, high, velocity, inv_mass)


AXES = ("dom", "sub")


def neighbours(first, last):
    count = lax.axis_size("dom") * lax.axis_size("sub")
    up = [(i, i + 1) for i in range(count - 1)]
    return lax.ppermute(last, AXES, up), lax.ppermute(first, AXES, [(b, a) for a, b in up])


def body(
    velocity, position, inv_mass, connectivity, shape_grad, area, thickness, yield_stress, stress,
    contact_owner, face_center, face_angle, face_stiffness, ghost_list, pair_node, pair_face,
    pair_count,
):
    owner = contact_owner.reshape(1, NODE_DEV)
    rank, outgoing = slots(owner, position, velocity)
    incoming = lax.all_to_all(outgoing.reshape(DEVICES, 8, 128), AXES, 0, 0, tiled=True)
    azimuth, elevation = face_angle[0], face_angle[1]
    flat = jnp.cos(elevation)
    normal = [jnp.cos(azimuth) * flat, jnp.sin(azimuth) * flat, jnp.sin(elevation)]
    faces = jnp.concatenate(
        [face_center, jnp.stack([*normal, face_stiffness, jnp.zeros_like(face_stiffness)])]
    )
    lent = lend(ghost_list.reshape(1, 2 * GHOST), faces)
    before, after = neighbours(lent[:, :GHOST], lent[:, GHOST:])
    all_faces = jnp.concatenate([before, faces, after], axis=1)
    low, high = neighbours(velocity[:, :HALO], velocity[:, NODE_DEV - HALO :])
    square = (ROWS, 128)
    new_stress, summed = elements(
        velocity, low, high, connectivity, shape_grad, area.reshape(square),
        thickness.reshape(square), yield_stress.reshape(square), stress,
    )
    below, above = neighbours(summed[:, :HALO], summed[:, HALO + NODE_DEV :])
    forces = contact_forces(pair_count, pair_node, pair_face, all_faces, incoming)
    back = lax.all_to_all(forces, AXES, 0, 0, tiled=True)
    new_velocity = finish(
        back.reshape(DEVICES * 4, 128), owner, rank, summed, below, above, velocity,
        inv_mass.reshape(1, NODE_DEV),
    )
    return new_velocity, new_stress


def solution(mesh):
    nodes, rows = P(AXES), P(None, AXES)
    in_specs = (
        rows, rows, nodes, rows, P(None, None, AXES), nodes, nodes, nodes, P(None, None, AXES),
        P(AXES, None), rows, rows, nodes, nodes, nodes, nodes, nodes,
    )
    out_specs = (rows, P(None, None, AXES))
    return jax.shard_map(body, mesh=mesh, in_specs=in_specs, out_specs=out_specs, check_vma=False)
```

```python
import functools

import jax
import jax.numpy as jnp
from jax import lax
from jax.experimental import pallas as pl
from jax.experimental.pallas import tpu as pltpu
from jax.sharding import PartitionSpec as P

TILE = 128
HALO = 128
GHOST = 256
NODE_DEV = 8192
ROWS = NODE_DEV // 128
FACE_DEV = 2048
FACE_TILES = 20
DEVICES = 128
PAIRS = 128
EXT = ROWS + 8

LOBATTO_POINTS = (-1.0, -0.6546536707079771, 0.0, 0.6546536707079771, 1.0)
LOBATTO_WEIGHTS = (0.1, 49.0 / 90.0, 32.0 / 45.0, 49.0 / 90.0, 0.1)
PLANE_MODULUS = 1.0 / 0.91
POISSON = 0.3
SHEAR_MODULUS = 5.0 / 6.0 / 2.6
DAMPING = 0.3
REACH_SQ = 0.5
LOG2E = 1.4426950408889634

BF = jnp.bfloat16
F32 = jnp.float32
NT = (((1,), (1,)), ((), ()))
NN = (((1,), (0,)), ((), ()))


def dot(a, b, dims):
    return lax.dot_general(a, b, dims, preferred_element_type=F32)


def onehot(count, row):
    where = lax.broadcasted_iota(jnp.int32, (count, row.shape[1]), 0)
    return jnp.where(where == row, 1.0, 0.0).astype(BF)


def split(x, parts):
    out = []
    for _ in range(parts - 1):
        head = x.astype(BF)
        out.append(head)
        x = x - head.astype(F32)
    out.append(x.astype(BF))
    return out


def lane_aligned(x, size):
    return pl.ds(pl.multiple_of(x * size, size), size)


NODE_PARTS = 3
MESH = pl.DeviceIdType.MESH


def constitutive(corner, grad_x, grad_y, area, thickness, limit, old):
    def over(f):
        total = f(0)
        for a in range(1, 4):
            total = total + f(a)
        return total

    vx, vy, vz, rx, ry = corner
    memb_xx = over(lambda a: grad_x[a] * vx[a])
    bend_xx = over(lambda a: grad_x[a] * ry[a])
    memb_yy = over(lambda a: grad_y[a] * vy[a])
    bend_yy = -over(lambda a: grad_y[a] * rx[a])
    memb_xy = over(lambda a: grad_y[a] * vx[a] + grad_x[a] * vy[a])
    bend_xy = over(lambda a: grad_y[a] * ry[a] - grad_x[a] * rx[a])
    shear_xz = over(lambda a: grad_x[a] * vz[a]) + 0.25 * over(lambda a: ry[a])
    shear_yz = over(lambda a: grad_y[a] * vz[a]) - 0.25 * over(lambda a: rx[a])
    add_xz, add_yz = SHEAR_MODULUS * shear_xz, SHEAR_MODULUS * shear_yz
    half = 0.5 * thickness
    volume = half * area
    new, force, moment = [], [0.0] * 5, [0.0] * 3
    for layer in range(5):
        height = half * LOBATTO_POINTS[layer]
        exx = memb_xx + height * bend_xx
        eyy = memb_yy + height * bend_yy
        exy = memb_xy + height * bend_xy
        t0 = old(layer, 0) + PLANE_MODULUS * (exx + POISSON * eyy)
        t1 = old(layer, 1) + PLANE_MODULUS * (eyy + POISSON * exx)
        t2 = old(layer, 2) + PLANE_MODULUS * 0.5 * (1.0 - POISSON) * exy
        t3 = old(layer, 3) + add_xz
        t4 = old(layer, 4) + add_yz
        plus, minus = t0 + t1, t0 - t1
        mises = jnp.sqrt(
            0.25 * (plus * plus) + 0.75 * (minus * minus) + 3.0 * (t2 * t2 + t3 * t3 + t4 * t4)
        )
        factor = limit / jnp.maximum(mises, limit)
        updated = [t * factor for t in (t0, t1, t2, t3, t4)]
        new.append(updated)
        weight = LOBATTO_WEIGHTS[layer] * volume
        weighted = [weight * u for u in updated]
        force = [f + w for f, w in zip(force, weighted)]
        moment = [m + height * w for m, w in zip(moment, weighted)]
    corners = []
    for a in range(4):
        gx, gy = grad_x[a], grad_y[a]
        corners.append(
            [
                gx * force[0] + gy * force[2],
                gy * force[1] + gx * force[2],
                gx * force[3] + gy * force[4],
                -(gy * moment[1] + gx * moment[2]) - 0.25 * force[4],
                gx * moment[0] + gy * moment[2] + 0.25 * force[3],
            ]
        )
    return new, corners


def slots(owner_ref, pos_ref, vel_ref, rank_ref, out_ref, run, acc, tri):
    later = lax.broadcasted_iota(jnp.int32, (256, 384), 0)
    column = lax.broadcasted_iota(jnp.int32, (256, 384), 1)
    tri[...] = jnp.where((later < column) | (column >= 256), 1.0, 0.0).astype(BF)
    run[...] = jnp.zeros_like(run)

    def rank_block(b):
        at = lane_aligned(b, 256)
        own = owner_ref[0:1, at]
        where = lax.broadcasted_iota(jnp.int32, (DEVICES, 256), 0)
        hot = jnp.where(where == own, 1.0, 0.0)
        counts = dot(hot.astype(BF), tri[...], NN)
        base = run[...]
        seen = counts[:, :256] + jnp.concatenate([base, base], axis=1)
        rank_ref[0:1, at] = jnp.sum(hot * seen, axis=0, keepdims=True)
        run[...] = base + counts[:, 256:]

    def rank_step(b, _):
        rank_block(2 * b)
        rank_block(2 * b + 1)
        return 0

    lax.fori_loop(0, NODE_DEV // 512, rank_step, 0)
    acc[...] = jnp.zeros_like(acc)

    def place(b, _):
        at = lane_aligned(b, 1024)
        own = owner_ref[0:1, at]
        column = (own & 1) * 128 + rank_ref[0:1, at].astype(jnp.int32)
        hot = onehot(256, column)
        group = onehot(64, own >> 1)
        rows = []
        for c in range(6):
            value = pos_ref[c : c + 1, at] if c < 3 else vel_ref[c - 3 : c - 2, at]
            rows += [group * part for part in split(value, NODE_PARTS)]
        rows.append(group)
        placed = dot(jnp.concatenate(rows, axis=0), hot, NT)
        for c in range(6):
            first = c * NODE_PARTS * 64
            total = placed[first : first + 64]
            for part in range(1, NODE_PARTS):
                total = total + placed[first + part * 64 : first + part * 64 + 64]
            acc[c * 64 : c * 64 + 64, :] += total
        acc[384:448, :] += placed[6 * NODE_PARTS * 64 :]
        return 0

    lax.fori_loop(0, NODE_DEV // 1024, place, 0)
    for first in range(0, 64, 8):
        for low in range(2):
            for c in range(8):
                rows = pl.ds(first * 16 + low * 8 + c, 8, stride=16)
                if c < 7:
                    part = acc[c * 64 + first : c * 64 + first + 8, low * 128 : low * 128 + 128]
                else:
                    part = jnp.zeros((8, 128), F32)
                out_ref[rows, :] = part


def lend(list_ref, face_ref, out_ref):
    for g in range(4):
        index = jnp.broadcast_to(list_ref[:, 128 * g : 128 * g + 128], (8, 128))
        low, high = index & 127, index >> 7
        found = jnp.zeros((8, 128), F32)
        for t in range(FACE_DEV // 128):
            part = jnp.take_along_axis(face_ref[:, 128 * t : 128 * t + 128], low, axis=1)
            found = jnp.where(high == t, part, found)
        out_ref[:, 128 * g : 128 * g + 128] = found


def unpack(vel_ref, conn_ref, grad_ref, stress_ref, vel, conn, grad, stress):
    def step(j, _):
        at = lane_aligned(j, 128)
        vel[pl.ds(j + 1, 5, stride=EXT), :] = vel_ref[:, at]
        conn[pl.ds(j, 4, stride=ROWS), :] = conn_ref[:, at] - 128 * j
        for axis in range(2):
            grad[pl.ds(axis * 4 * ROWS + j, 4, stride=ROWS), :] = grad_ref[axis, :, at]
        for layer in range(5):
            stress[pl.ds(layer * 5 * ROWS + j, 5, stride=ROWS), :] = stress_ref[layer, :, at]
        return 0

    lax.fori_loop(0, ROWS, step, 0, unroll=8)


def elements(vel, conn, grad, area_ref, thick_ref, limit_ref, stress, spread):
    spread[...] = jnp.zeros_like(spread)

    def group(g, _):
        def rows(field):
            return pl.ds(pl.multiple_of(field * ROWS + 8 * g, 8), 8)

        here = pl.ds(pl.multiple_of(8 * g, 8), 8)
        index = [conn[rows(a), :] for a in range(4)]
        low = [i & 127 for i in index]
        part_of = [i >> 7 for i in index]
        corner = []
        for c in range(5):
            window = [vel[pl.ds(c * EXT + 8 * g + k, 8), :] for k in range(3)]
            values = []
            for a in range(4):
                got = [jnp.take_along_axis(w, low[a], axis=1) for w in window]
                values.append(
                    jnp.where(part_of[a] == 0, got[0], jnp.where(part_of[a] == 1, got[1], got[2]))
                )
            corner.append(values)
        grad_x = [grad[rows(a), :] for a in range(4)]
        grad_y = [grad[rows(4 + a), :] for a in range(4)]
        new, forces = constitutive(
            corner, grad_x, grad_y, area_ref[here, :], thick_ref[here, :], limit_ref[here, :],
            lambda layer, c: stress[rows(5 * layer + c), :],
        )
        for layer in range(5):
            for c in range(5):
                stress[rows(5 * layer + c), :] = new[layer][c]
        for a in range(4):
            for c in range(5):
                spread[a, pl.ds(64 * g + c, 8, stride=8), :] = forces[a][c]
        return 0

    lax.fori_loop(0, 8, group, 0)


def pack(stress, new_ref):
    def step(j, _):
        at = lane_aligned(j, 128)
        for layer in range(5):
            new_ref[layer, :, at] = stress[pl.ds(layer * 5 * ROWS + j, 5, stride=ROWS), :]
        return 0

    lax.fori_loop(0, ROWS, step, 0, unroll=8)


def scatter(b, conn_ref, spread, sum_ref):
    at = lane_aligned(b, 256)
    index = jnp.concatenate([conn_ref[a : a + 1, at] for a in range(4)], axis=1) - 256 * b
    hot = onehot(256, index & 255)
    upper = (index >> 8).astype(F32)
    value = jnp.concatenate(
        [spread[a, lane_aligned(2 * b + h, 8), :] for a in range(4) for h in range(2)], axis=1
    )
    high = value * upper
    both = split(value - high, 2) + split(high, 2)
    found = dot(jnp.concatenate(both, axis=0), hot, NT)
    sum_ref[:, at] += found[0:8] + found[8:16]
    sum_ref[:, lane_aligned(b + 1, 256)] += found[16:24] + found[24:32]


def expand(f, faces_ref, table):
    x = faces_ref[:, lane_aligned(f, 128)]
    r, m, stiff = [x[i : i + 1] for i in range(3)], [x[i : i + 1] for i in range(3, 6)], x[6:7]
    apart = m[0] * r[0] + m[1] * r[1] + m[2] * r[2]
    square = r[0] * r[0] + r[1] * r[1] + r[2] * r[2]
    scaled = [(2.0 / REACH_SQ * LOG2E) * v for v in r]
    strength = stiff * jnp.exp2((-LOG2E / REACH_SQ) * square)
    stacked = jnp.concatenate([*m, apart, *scaled, strength], axis=0).T
    for q in range(8):
        table[f, q] = jnp.broadcast_to(stacked[:, q : q + 1], (128, 128))


def pair_force(x, faces_of):
    p = [jnp.broadcast_to(x[i : i + 1], (8, 128)) for i in range(3)]
    u = [jnp.broadcast_to(-DAMPING * x[i : i + 1], (8, 128)) for i in range(3, 6)]
    square = x[0:1] * x[0:1] + x[1:2] * x[1:2] + x[2:3] * x[2:3]
    scale = x[6:7] * jnp.exp2((-LOG2E / REACH_SQ) * square)
    total = [jnp.zeros((8, 128), F32) for _ in range(3)]
    for k in range(16):
        mx, my, mz, apart, rx, ry, rz, stiff = [faces_of(i, k) for i in range(8)]
        depth = jnp.maximum(apart - (mx * p[0] + my * p[1] + mz * p[2]), 0.0)
        reach = jnp.exp2(rx * p[0] + ry * p[1] + rz * p[2])
        along = 1.0 + (mx * u[0] + my * u[1] + mz * u[2])
        size = (stiff * reach) * (depth * along)
        total = [t + size * m for t, m in zip(total, (mx, my, mz))]
    return [scale * jnp.sum(t, axis=0, keepdims=True) for t in total]


def finish(back_ref, owner_ref, rank_ref, sum_ref, vel_ref, mass_ref, out_ref, side):
    for c in range(3):
        turned = back_ref[pl.ds(c, 128, stride=8), :].T
        for i, part in enumerate(split(turned, 2)):
            side[128 * c : 128 * c + 128, 128 * i : 128 * i + 128] = part

    def block(b):
        at = lane_aligned(b, 256)
        own = onehot(128, owner_ref[0:1, at])
        found = dot(side[...], jnp.concatenate([own, own], axis=0), NN)
        rank = rank_ref[0:1, at].astype(jnp.int32)
        mine = lax.broadcasted_iota(jnp.int32, (128, 256), 0) == rank
        contact = [
            jnp.sum(jnp.where(mine, found[128 * c : 128 * c + 128], 0.0), axis=0, keepdims=True)
            for c in range(3)
        ]
        contact = jnp.concatenate([*contact, jnp.zeros((2, 256), F32)], axis=0)
        inner = sum_ref[0:5, pl.ds(pl.multiple_of(b * 256 + 128, 128), 256)]
        out_ref[:, at] = vel_ref[:, at] + mass_ref[0:1, at] * (contact - inner)

    def step(b, _):
        block(2 * b)
        block(2 * b + 1)
        return 0

    lax.fori_loop(0, NODE_DEV // 512, step, 0)


def step_kernel(
    count_ref, node_ref, face_of_ref, node_row_ref, owner_ref, pos_ref, vel_ref, list_ref, face_ref,
    mass_ref, area_ref, thick_ref, limit_ref, conn_hbm, grad_hbm, stress_hbm,
    out_ref, new_ref,
    conn_in, grad_in, stress_in, rank_ref, run, acc, tri, going, coming, faces, lent, ghost_in,
    vel_in, vel, conn, grad, stress, spread, sum_ref, rim_in, table, pairs, leaving, back, side,
    load_sem, send_sem, recv_sem, edge_send, edge_recv,
):
    sub_count = lax.axis_size("sub")
    me = lax.axis_index("dom") * sub_count + lax.axis_index("sub")

    def device(k):
        to = lax.rem(me + k, DEVICES)
        return to, (lax.div(to, sub_count), lax.rem(to, sub_count))

    loads = [
        pltpu.make_async_copy(src, dst, load_sem.at[i])
        for i, (src, dst) in enumerate(
            ((conn_hbm, conn_in), (grad_hbm, grad_in), (stress_hbm, stress_in))
        )
    ]
    for copy in loads:
        copy.start()
    barrier = pltpu.get_barrier_semaphore()

    def greet(k, _):
        pl.semaphore_signal(barrier, inc=1, device_id=device(k)[1], device_id_type=MESH)
        return 0

    lax.fori_loop(1, DEVICES, greet, 0)
    slots(owner_ref, pos_ref, vel_ref, rank_ref, going, run, acc, tri)
    lend(list_ref, face_ref, lent)
    pl.semaphore_wait(barrier, DEVICES - 1)

    def edges(i, first, last, land):
        pair = []
        for end, (src, k) in enumerate(((last, 1), (first, DEVICES - 1))):
            copy = pltpu.make_async_remote_copy(
                src, land.at[end], edge_send.at[i, end], edge_recv.at[i, end],
                device_id=device(k)[1], device_id_type=MESH,
            )
            copy.start()
            pair.append(copy)
        return pair

    def tile(i):
        return pl.ds(pl.multiple_of(8 * i, 8), 8)

    def exchange(i, src, dst):
        def send(k, _):
            to, where = device(k)
            pltpu.make_async_remote_copy(
                src.at[tile(to)], dst.at[tile(me)], send_sem.at[i], recv_sem.at[i],
                device_id=where, device_id_type=MESH,
            ).start()
            return 0

        lax.fori_loop(1, DEVICES, send, 0)
        dst[tile(me), :] = src[tile(me), :]
        others = pl.ds(0, (DEVICES - 1) * 8)
        return pltpu.make_async_remote_copy(
            src.at[others], dst.at[others], send_sem.at[i], recv_sem.at[i],
            device_id=device(1)[1], device_id_type=MESH,
        )

    halo = edges(0, vel_ref.at[:, 0:HALO], vel_ref.at[:, NODE_DEV - HALO : NODE_DEV], vel_in)
    ghosts = edges(1, lent.at[:, 0:GHOST], lent.at[:, GHOST : 2 * GHOST], ghost_in)
    nodes_move = exchange(0, going, coming)
    for copy in loads:
        copy.wait()
    unpack(vel_ref, conn_in, grad_in, stress_in, vel, conn, grad, stress)
    for copy in halo:
        copy.wait()
    vel[pl.ds(0, 5, stride=EXT), :] = vel_in[0]
    vel[pl.ds(ROWS + 1, 5, stride=EXT), :] = vel_in[1]
    elements(vel, conn, grad, area_ref, thick_ref, limit_ref, stress, spread)
    pack(stress, new_ref)
    for copy in ghosts:
        copy.wait()
    faces[:, 0:GHOST] = jnp.where(me > 0, ghost_in[0], 0.0)
    faces[:, GHOST : GHOST + FACE_DEV] = face_ref[...]
    faces[:, GHOST + FACE_DEV :] = jnp.where(me < DEVICES - 1, ghost_in[1], 0.0)

    def expand_step(f, _):
        expand(f, faces, table)
        return 0

    lax.fori_loop(0, FACE_TILES, expand_step, 0)
    nodes_move.wait()

    tiles = coming.reshape(DEVICES, 8, 128)

    def pair_step(q, _):
        x, f = tiles[node_ref[q]], face_of_ref[q]
        force = pair_force(x, lambda i, k: table[f, i, 8 * k : 8 * k + 8])
        for c in range(3):
            pairs[pl.ds(c * PAIRS + q, 1), :] = force[c]
        return 0

    lax.fori_loop(0, PAIRS, pair_step, 0)
    slot = lax.broadcasted_iota(jnp.int32, (1, PAIRS), 1)
    listed = onehot(DEVICES, jnp.where(slot < count_ref[...], node_row_ref[...], -1))
    listed = jnp.concatenate([listed] * 3, axis=1)
    leaving[...] = jnp.zeros_like(leaving)
    for c in range(3):
        parts = jnp.concatenate(split(pairs[c * PAIRS : (c + 1) * PAIRS, :], 3), axis=0)
        leaving[pl.ds(c, DEVICES, stride=8), :] = dot(listed, parts, NN)
    forces_move = exchange(1, leaving, back)

    sum_ref[...] = jnp.zeros_like(sum_ref)
    scatter(0, conn_in, spread, sum_ref)
    scatter(ROWS // 2 - 1, conn_in, spread, sum_ref)
    rims = edges(
        2, sum_ref.at[:, 0:HALO], sum_ref.at[:, HALO + NODE_DEV : 2 * HALO + NODE_DEV], rim_in
    )

    def scatter_step(b, _):
        scatter(2 * b + 1, conn_in, spread, sum_ref)
        scatter(2 * b + 2, conn_in, spread, sum_ref)
        return 0

    lax.fori_loop(0, ROWS // 4 - 1, scatter_step, 0)
    for copy in rims:
        copy.wait()
    sum_ref[:, HALO : 2 * HALO] += rim_in[0]
    sum_ref[:, NODE_DEV : NODE_DEV + HALO] += rim_in[1]
    forces_move.wait()
    finish(back, owner_ref, rank_ref, sum_ref, vel_ref, mass_ref, out_ref, side)


def body(
    velocity, position, inv_mass, connectivity, shape_grad, area, thickness, yield_stress, stress,
    contact_owner, face_center, face_angle, face_stiffness, ghost_list, pair_node, pair_face,
    pair_count,
):
    azimuth, elevation = face_angle[0], face_angle[1]
    flat = jnp.cos(elevation)
    normal = [jnp.cos(azimuth) * flat, jnp.sin(azimuth) * flat, jnp.sin(elevation)]
    faces = jnp.concatenate(
        [face_center, jnp.stack([*normal, face_stiffness, jnp.zeros_like(face_stiffness)])]
    )
    square = (ROWS, 128)
    smem = pl.BlockSpec(memory_space=pltpu.SMEM)
    vmem = pl.BlockSpec(memory_space=pltpu.VMEM)
    hbm = pl.BlockSpec(memory_space=pl.ANY)
    dma = pltpu.SemaphoreType.DMA
    scratch = [
        ((4, NODE_DEV), jnp.int32), ((2, 4, NODE_DEV), F32), ((5, 5, NODE_DEV), F32),
        ((1, NODE_DEV), F32), ((DEVICES, 128), F32), ((448, 256), F32), ((256, 384), BF),
        ((DEVICES * 8, 128), F32), ((DEVICES * 8, 128), F32), ((8, FACE_TILES * 128), F32),
        ((8, 2 * GHOST), F32), ((2, 8, GHOST), F32), ((2, 5, HALO), F32), ((5 * EXT, 128), F32),
        ((4 * ROWS, 128), jnp.int32), ((8 * ROWS, 128), F32), ((25 * ROWS, 128), F32),
        ((4, 8 * ROWS, 128), F32), ((8, NODE_DEV + 256), F32), ((2, 8, HALO), F32),
        ((FACE_TILES, 8, 128, 128), F32), ((3 * PAIRS, 128), F32), ((DEVICES * 8, 128), F32),
        ((DEVICES * 8, 128), F32), ((384, 256), BF),
    ]
    return pl.pallas_call(
        step_kernel,
        out_shape=(
            jax.ShapeDtypeStruct((5, NODE_DEV), F32),
            jax.ShapeDtypeStruct((5, 5, NODE_DEV), F32),
        ),
        in_specs=[vmem] + [smem] * 2 + [vmem] * 10 + [hbm] * 3,
        out_specs=(vmem, vmem),
        scratch_shapes=[
            *(pltpu.VMEM(shape, kind) for shape, kind in scratch),
            dma((3,)), dma((2,)), dma((2,)), dma((3, 2)), dma((3, 2)),
        ],
        compiler_params=pltpu.CompilerParams(
            vmem_limit_bytes=56 * 2**20, collective_id=0, has_side_effects=True
        ),
        name="crash_step",
    )(
        pair_count.reshape(1, 1), pair_node, pair_face, pair_node.reshape(1, PAIRS),
        contact_owner.reshape(1, NODE_DEV), position, velocity, ghost_list.reshape(1, 2 * GHOST),
        faces, inv_mass.reshape(1, NODE_DEV), area.reshape(square), thickness.reshape(square),
        yield_stress.reshape(square), connectivity, shape_grad, stress,
    )


def solution(mesh):
    axes = ("dom", "sub")
    nodes, rows, cells = P(axes), P(None, axes), P(None, None, axes)
    in_specs = (
        rows, rows, nodes, rows, cells, nodes, nodes, nodes, cells, P(axes, None), rows, rows,
        nodes, nodes, nodes, nodes, nodes,
    )
    return jax.shard_map(
        body, mesh=mesh, in_specs=in_specs, out_specs=(rows, cells), check_vma=False
    )
```

```python
import functools

import jax
import jax.numpy as jnp
from jax import lax
from jax.experimental import pallas as pl
from jax.experimental.pallas import tpu as pltpu
from jax.sharding import PartitionSpec as P

TILE = 128
HALO = 128
GHOST = 256
NODE_DEV = 8192
ROWS = NODE_DEV // 128
FACE_DEV = 2048
FACE_TILES = 20
DEVICES = 128
PAIRS = 128
EXT = ROWS + 8

LOBATTO_POINTS = (-1.0, -0.6546536707079771, 0.0, 0.6546536707079771, 1.0)
LOBATTO_WEIGHTS = (0.1, 49.0 / 90.0, 32.0 / 45.0, 49.0 / 90.0, 0.1)
PLANE_MODULUS = 1.0 / 0.91
POISSON = 0.3
SHEAR_MODULUS = 5.0 / 6.0 / 2.6
DAMPING = 0.3
REACH_SQ = 0.5
LOG2E = 1.4426950408889634

BF = jnp.bfloat16
F32 = jnp.float32
NT = (((1,), (1,)), ((), ()))
NN = (((1,), (0,)), ((), ()))


def dot(a, b, dims):
    return lax.dot_general(a, b, dims, preferred_element_type=F32)


def onehot(count, row):
    where = lax.broadcasted_iota(jnp.int32, (count, row.shape[1]), 0)
    return jnp.where(where == row, 1.0, 0.0).astype(BF)


def split(x, parts):
    out = []
    for _ in range(parts - 1):
        head = x.astype(BF)
        out.append(head)
        x = x - head.astype(F32)
    out.append(x.astype(BF))
    return out


def lane_aligned(x, size):
    return pl.ds(pl.multiple_of(x * size, size), size)


MESH = pl.DeviceIdType.MESH
RANK_STEP, PLACE_STEP, SPREAD_STEP, FACE_STEP, PAIR_STEP, FINISH_STEP = 8, 4, 8, 10, 8, 8
PARTS = (3, 3, 3, 2, 2, 2, 1)


def constitutive(corner, grad_x, grad_y, area, thickness, limit, old):
    def over(f):
        total = f(0)
        for a in range(1, 4):
            total = total + f(a)
        return total

    vx, vy, vz, rx, ry = corner
    memb_xx = over(lambda a: grad_x[a] * vx[a])
    bend_xx = over(lambda a: grad_x[a] * ry[a])
    memb_yy = over(lambda a: grad_y[a] * vy[a])
    bend_yy = -over(lambda a: grad_y[a] * rx[a])
    memb_xy = over(lambda a: grad_y[a] * vx[a] + grad_x[a] * vy[a])
    bend_xy = over(lambda a: grad_y[a] * ry[a] - grad_x[a] * rx[a])
    shear_xz = over(lambda a: grad_x[a] * vz[a]) + 0.25 * over(lambda a: ry[a])
    shear_yz = over(lambda a: grad_y[a] * vz[a]) - 0.25 * over(lambda a: rx[a])
    add_xz, add_yz = SHEAR_MODULUS * shear_xz, SHEAR_MODULUS * shear_yz
    half = 0.5 * thickness
    volume = half * area
    new, force, moment = [], [0.0] * 5, [0.0] * 3
    for layer in range(5):
        height = half * LOBATTO_POINTS[layer]
        exx = memb_xx + height * bend_xx
        eyy = memb_yy + height * bend_yy
        exy = memb_xy + height * bend_xy
        t0 = old(layer, 0) + PLANE_MODULUS * (exx + POISSON * eyy)
        t1 = old(layer, 1) + PLANE_MODULUS * (eyy + POISSON * exx)
        t2 = old(layer, 2) + PLANE_MODULUS * 0.5 * (1.0 - POISSON) * exy
        t3 = old(layer, 3) + add_xz
        t4 = old(layer, 4) + add_yz
        plus, minus = t0 + t1, t0 - t1
        mises = jnp.sqrt(
            0.25 * (plus * plus) + 0.75 * (minus * minus) + 3.0 * (t2 * t2 + t3 * t3 + t4 * t4)
        )
        factor = limit / jnp.maximum(mises, limit)
        updated = [t * factor for t in (t0, t1, t2, t3, t4)]
        new.append(updated)
        weight = LOBATTO_WEIGHTS[layer] * volume
        weighted = [weight * u for u in updated]
        force = [f + w for f, w in zip(force, weighted)]
        moment = [m + height * w for m, w in zip(moment, weighted)]
    corners = []
    for a in range(4):
        gx, gy = grad_x[a], grad_y[a]
        corners.append(
            [
                gx * force[0] + gy * force[2],
                gy * force[1] + gx * force[2],
                gx * force[3] + gy * force[4],
                -(gy * moment[1] + gx * moment[2]) - 0.25 * force[4],
                gx * moment[0] + gy * moment[2] + 0.25 * force[3],
            ]
        )
    return new, corners


def ranks(owner_ref, rank_ref, run, tri):
    row = lax.broadcasted_iota(jnp.int32, (256, 384), 0)
    column = lax.broadcasted_iota(jnp.int32, (256, 384), 1)
    tri[...] = jnp.where((row < column) | (column >= 256), 1.0, 0.0).astype(BF)
    run[...] = jnp.zeros_like(run)

    def step(b, _):
        spans = [lane_aligned(b * RANK_STEP + i, 256) for i in range(RANK_STEP)]
        where = lax.broadcasted_iota(jnp.int32, (DEVICES, 256), 0)
        hot = [jnp.where(where == owner_ref[0:1, at], 1.0, 0.0) for at in spans]
        counts = dot(jnp.concatenate([h.astype(BF) for h in hot], axis=0), tri[...], NN)
        base = run[...]
        for i, at in enumerate(spans):
            count = counts[DEVICES * i : DEVICES * i + DEVICES]
            seen = count[:, :256] + jnp.concatenate([base, base], axis=1)
            rank_ref[0:1, at] = jnp.sum(hot[i] * seen, axis=0, keepdims=True)
            base = base + count[:, 256:]
        run[...] = base
        return 0

    lax.fori_loop(0, NODE_DEV // (256 * RANK_STEP), step, 0)


def place(owner_ref, rank_ref, pos_ref, vel_ref, out_ref, acc):
    acc[...] = jnp.zeros_like(acc)

    def block(b):
        at = lane_aligned(b, 1024)
        own = owner_ref[0:1, at]
        hot = onehot(256, (own & 1) * 128 + rank_ref[0:1, at].astype(jnp.int32))
        group = onehot(64, own >> 1)
        rows = []
        for c in range(6):
            value = pos_ref[c : c + 1, at] if c < 3 else vel_ref[c - 3 : c - 2, at]
            rows += [group * part for part in split(value, PARTS[c])]
        return dot(jnp.concatenate([*rows, group], axis=0), hot, NT)

    def step(b, _):
        placed = [block(b * PLACE_STEP + i) for i in range(PLACE_STEP)]
        first = 0
        for c, parts in enumerate(PARTS):
            total = acc[c * 64 : c * 64 + 64, :]
            for _ in range(parts):
                for p in placed:
                    total = total + p[first : first + 64]
                first += 64
            acc[c * 64 : c * 64 + 64, :] = total
        return 0

    lax.fori_loop(0, NODE_DEV // (1024 * PLACE_STEP), step, 0)
    for first in range(0, 64, 8):
        for low in range(2):
            for c in range(8):
                if c < 7:
                    part = acc[c * 64 + first : c * 64 + first + 8, low * 128 : low * 128 + 128]
                else:
                    part = jnp.ones((8, 128), F32)
                out_ref[pl.ds(first * 16 + low * 8 + c, 8, stride=16), :] = part


def face_rows(center_ref, angle_ref, stiff_ref, angles, normals, out_ref):
    tiles = FACE_DEV // 128
    for j in range(tiles):
        angles[pl.ds(j, 2, stride=tiles), :] = angle_ref[:, 128 * j : 128 * j + 128]
    azimuth, elevation = angles[0:tiles, :], angles[tiles : 2 * tiles, :]
    flat = jnp.cos(elevation)
    for c, value in enumerate(
        (jnp.cos(azimuth) * flat, jnp.sin(azimuth) * flat, jnp.sin(elevation))
    ):
        normals[pl.ds(c, tiles, stride=8), :] = value
    for j in range(tiles):
        at = slice(128 * j, 128 * j + 128)
        out_ref[:, GHOST + 128 * j : GHOST + 128 * j + 128] = jnp.concatenate(
            [center_ref[:, at], normals[8 * j : 8 * j + 3, :], stiff_ref[:, at], jnp.zeros((1, 128), F32)],
            axis=0,
        )


def lend(list_ref, faces_ref, out_ref):
    for g in range(2 * GHOST // 128):
        index = jnp.broadcast_to(list_ref[:, 128 * g : 128 * g + 128], (8, 128))
        low, high = index & 127, index >> 7
        found = jnp.zeros((8, 128), F32)
        for t in range(FACE_DEV // 128):
            at = slice(GHOST + 128 * t, GHOST + 128 * t + 128)
            part = jnp.take_along_axis(faces_ref[:, at], low, axis=1)
            found = jnp.where(high == t, part, found)
        out_ref[:, 128 * g : 128 * g + 128] = found


def unpack(vel_ref, conn_ref, grad_ref, stress_ref, vel, conn, grad, stress):
    def step(j, _):
        at = lane_aligned(j, 128)
        vel[pl.ds(j + 1, 5, stride=EXT), :] = vel_ref[:, at]
        conn[pl.ds(j, 4, stride=ROWS), :] = conn_ref[:, at] - 128 * j
        for axis in range(2):
            grad[pl.ds(axis * 4 * ROWS + j, 4, stride=ROWS), :] = grad_ref[axis, :, at]
        for layer in range(5):
            stress[pl.ds(layer * 5 * ROWS + j, 5, stride=ROWS), :] = stress_ref[layer, :, at]
        return 0

    lax.fori_loop(0, ROWS, step, 0, unroll=8)


def elements(vel, conn, grad, area_ref, thick_ref, limit_ref, stress, spread):
    spread[...] = jnp.zeros_like(spread)

    def group(g, _):
        def rows(field):
            return pl.ds(pl.multiple_of(field * ROWS + 8 * g, 8), 8)

        here = pl.ds(pl.multiple_of(8 * g, 8), 8)
        index = [conn[rows(a), :] for a in range(4)]
        low = [i & 127 for i in index]
        part_of = [i >> 7 for i in index]
        corner = []
        for c in range(5):
            window = [vel[pl.ds(c * EXT + 8 * g + k, 8), :] for k in range(3)]
            values = []
            for a in range(4):
                got = [jnp.take_along_axis(w, low[a], axis=1) for w in window]
                values.append(
                    jnp.where(part_of[a] == 0, got[0], jnp.where(part_of[a] == 1, got[1], got[2]))
                )
            corner.append(values)
        grad_x = [grad[rows(a), :] for a in range(4)]
        grad_y = [grad[rows(4 + a), :] for a in range(4)]
        new, forces = constitutive(
            corner, grad_x, grad_y, area_ref[here, :], thick_ref[here, :], limit_ref[here, :],
            lambda layer, c: stress[rows(5 * layer + c), :],
        )
        for layer in range(5):
            for c in range(5):
                stress[rows(5 * layer + c), :] = new[layer][c]
        for a in range(4):
            for c in range(5):
                spread[a, pl.ds(64 * g + c, 8, stride=8), :] = forces[a][c]
        return 0

    lax.fori_loop(0, 8, group, 0)


def scatter(b, conn_ref, spread):
    at = lane_aligned(b, 256)
    index = jnp.concatenate([conn_ref[a : a + 1, at] for a in range(4)], axis=1) - 256 * b
    hot = onehot(128, index & 127)
    window = index >> 7
    value = jnp.concatenate(
        [spread[a, lane_aligned(2 * b + h, 8), :] for a in range(4) for h in range(2)], axis=1
    )
    parts = split(value, 2)
    rows = []
    for h in range(4):
        mine = jnp.where(window == h, 1.0, 0.0).astype(BF)
        rows += [part * mine for part in parts]
    found = dot(hot, jnp.concatenate(rows, axis=0), NT).T
    return [found[16 * h : 16 * h + 8] + found[16 * h + 8 : 16 * h + 16] for h in range(4)]


def scatter_blocks(blocks, conn_ref, spread, sum_ref):
    found = [scatter(b, conn_ref, spread) for b in blocks]
    for b, windows in zip(blocks, found):
        for h, window in enumerate(windows):
            sum_ref[:, lane_aligned(2 * b + h, 128)] += window


def six_terms(x):
    high, mid, low = (part.astype(F32) for part in split(x, 3))
    return jnp.concatenate([high, mid, high, mid, low, high], axis=0)


def face_tables(faces_ref, forms, pick, normals):
    row = lax.broadcasted_iota(jnp.int32, (24, 3 * TILE), 0)
    column = lax.broadcasted_iota(jnp.int32, (24, 3 * TILE), 1)
    pick[...] = jnp.where((row & 7) == (column >> 7), 1.0, 0.0).astype(BF)

    def tile(f):
        x = faces_ref[:, lane_aligned(f, TILE)]
        r, m = [x[i : i + 1] for i in range(3)], [x[i : i + 1] for i in range(3, 6)]
        apart = m[0] * r[0] + m[1] * r[1] + m[2] * r[2]
        square = r[0] * r[0] + r[1] * r[1] + r[2] * r[2]
        strength = x[6:7] * jnp.exp2((-LOG2E / REACH_SQ) * square)
        none = jnp.zeros_like(apart)
        depth = [*(-strength * v for v in m), none, none, none, none, strength * apart]
        along = [none, none, none, *(-DAMPING * v for v in m), none, jnp.ones_like(apart)]
        reach = [*((2.0 / REACH_SQ * LOG2E) * v for v in r), none, none, none, none, none]
        for i, form in enumerate((depth, along, reach)):
            terms = six_terms(jnp.concatenate(form, axis=0))
            forms[f, TILE * i : TILE * i + TILE, :] = terms.T.astype(BF)
        parts = [part.astype(F32) for part in split(jnp.concatenate([*m] + [none] * 5, axis=0), 3)]
        wide = dot(jnp.concatenate(parts, axis=0).T.astype(BF), pick[...], NN)
        for i in range(3):
            normals[f, i] = wide[:, TILE * i : TILE * i + TILE]

    def step(b, _):
        for i in range(FACE_STEP):
            tile(b * FACE_STEP + i)
        return 0

    lax.fori_loop(0, FACE_TILES // FACE_STEP, step, 0)


def pair_force(x, form, normal_of):
    high, mid, low = split(x, 3)
    products = dot(form, jnp.concatenate([high, high, mid, mid, high, low], axis=0), NN)
    square = x[0:1] * x[0:1] + x[1:2] * x[1:2] + x[2:3] * x[2:3]
    scale = x[6:7] * jnp.exp2((-LOG2E / REACH_SQ) * square)
    total = [jnp.zeros((8, TILE), F32) for _ in range(3)]
    for k in range(0, TILE, 8):
        depth = jnp.maximum(products[k : k + 8], 0.0)
        along = products[TILE + k : TILE + k + 8]
        size = depth * along * jnp.exp2(products[2 * TILE + k : 2 * TILE + k + 8])
        total = [t + size * normal_of(i, k) for i, t in enumerate(total)]
    return [scale * jnp.sum(t, axis=0, keepdims=True) for t in total]


def step_kernel(*refs):
    inputs, outputs, held, scratch = refs[:17], refs[17:19], refs[19:36], refs[36:]
    (
        owner_ref, pos_ref, vel_ref, center_ref, angle_ref, stiff_ref, list_ref, conn_in, grad_in,
        stress_in, area_ref, thick_ref, limit_ref, node_ref, face_of_ref, node_row_ref, count_ref,
    ) = held
    total_hbm, cells_hbm = outputs
    (
        back, sum_ref, rank_ref, stress, total, side, run, acc, tri, going, coming, angles, unit, faces, lent, ghost_in,
    vel_in, vel, conn, grad, spread, rim_in, forms, pick, normals, pairs, leaving,
    load_sem, out_sem, send_sem, recv_sem, edge_send, edge_recv,
    ) = scratch
    sub_count = lax.axis_size("sub")
    me = lax.axis_index("dom") * sub_count + lax.axis_index("sub")

    def device(k):
        to = lax.rem(me + k, DEVICES)
        return to, (lax.div(to, sub_count), lax.rem(to, sub_count))

    loads = [
        pltpu.make_async_copy(src, dst, load_sem.at[i])
        for i, (src, dst) in enumerate(zip(inputs, held))
    ]
    for copy in loads:
        copy.start()
    barrier = pltpu.get_barrier_semaphore()

    def greet(k, _):
        pl.semaphore_signal(barrier, inc=1, device_id=device(k)[1], device_id_type=MESH)
        return 0

    lax.fori_loop(1, DEVICES, greet, 0)
    for copy in loads[:3]:
        copy.wait()
    ranks(owner_ref, rank_ref, run, tri)
    place(owner_ref, rank_ref, pos_ref, vel_ref, going, acc)
    pl.semaphore_wait(barrier, DEVICES - 1)

    def edges(i, first, last, land):
        pair = []
        for end, (src, k) in enumerate(((last, 1), (first, DEVICES - 1))):
            copy = pltpu.make_async_remote_copy(
                src, land.at[end], edge_send.at[i, end], edge_recv.at[i, end],
                device_id=device(k)[1], device_id_type=MESH,
            )
            copy.start()
            pair.append(copy)
        return pair

    def tile(i):
        return pl.ds(pl.multiple_of(8 * i, 8), 8)

    def exchange(i, src, dst):
        def send(k, _):
            to, where = device(k)
            pltpu.make_async_remote_copy(
                src.at[tile(to)], dst.at[tile(me)], send_sem.at[i], recv_sem.at[i],
                device_id=where, device_id_type=MESH,
            ).start()
            return 0

        lax.fori_loop(1, DEVICES, send, 0)
        dst[tile(me), :] = src[tile(me), :]
        others = pl.ds(0, (DEVICES - 1) * 8)
        return pltpu.make_async_remote_copy(
            src.at[others], dst.at[others], send_sem.at[i], recv_sem.at[i],
            device_id=device(1)[1], device_id_type=MESH,
        )

    halo = edges(0, vel_ref.at[:, 0:HALO], vel_ref.at[:, NODE_DEV - HALO : NODE_DEV], vel_in)
    nodes_move = exchange(0, going, coming)
    for copy in loads[3:]:
        copy.wait()
    face_rows(center_ref, angle_ref, stiff_ref, angles, unit, faces)
    lend(list_ref, faces, lent)
    ghosts = edges(1, lent.at[:, 0:GHOST], lent.at[:, GHOST : 2 * GHOST], ghost_in)
    unpack(vel_ref, conn_in, grad_in, stress_in, vel, conn, grad, stress)
    for copy in halo:
        copy.wait()
    vel[pl.ds(0, 5, stride=EXT), :] = vel_in[0]
    vel[pl.ds(ROWS + 1, 5, stride=EXT), :] = vel_in[1]
    elements(vel, conn, grad, area_ref, thick_ref, limit_ref, stress, spread)
    leave = [
        pltpu.make_async_copy(src, dst, out_sem.at[i])
        for i, (src, dst) in enumerate(((stress, cells_hbm), (total, total_hbm)))
    ]
    leave[0].start()
    for copy in ghosts:
        copy.wait()
    faces[:, 0:GHOST] = jnp.where(me > 0, ghost_in[0], 0.0)
    faces[:, GHOST + FACE_DEV :] = jnp.where(me < DEVICES - 1, ghost_in[1], 0.0)
    face_tables(faces, forms, pick, normals)
    nodes_move.wait()

    tiles = coming.reshape(DEVICES, 8, 128)

    def pair_step(b, _):
        first = b * PAIR_STEP
        forces = []
        for i in range(PAIR_STEP):
            x, f = tiles[node_ref[first + i]], face_of_ref[first + i]
            forces.append(pair_force(x, forms[f], lambda c, k, f=f: normals[f, c, k : k + 8]))
        for i, force in enumerate(forces):
            for c in range(3):
                pairs[pl.ds(c * PAIRS + first + i, 1), :] = force[c]
        return 0

    lax.fori_loop(0, PAIRS // PAIR_STEP, pair_step, 0)
    slot = lax.broadcasted_iota(jnp.int32, (1, PAIRS), 1)
    listed = onehot(DEVICES, jnp.where(slot < count_ref[...], node_row_ref[...], -1))
    listed = jnp.concatenate([listed] * 3, axis=1)
    leaving[...] = jnp.zeros_like(leaving)
    for c in range(3):
        parts = jnp.concatenate(split(pairs[c * PAIRS : (c + 1) * PAIRS, :], 3), axis=0)
        leaving[pl.ds(c, DEVICES, stride=8), :] = dot(listed, parts, NN)
    forces_move = exchange(1, leaving, back)

    sum_ref[...] = jnp.zeros_like(sum_ref)
    last = NODE_DEV // 256 - 1
    scatter_blocks([0, last, *range(1, SPREAD_STEP - 1)], conn_in, spread, sum_ref)
    rims = edges(
        2, sum_ref.at[:, 0:HALO], sum_ref.at[:, HALO + NODE_DEV : 2 * HALO + NODE_DEV], rim_in
    )

    def scatter_step(b, _):
        first = b * SPREAD_STEP - 1
        scatter_blocks([first + i for i in range(SPREAD_STEP)], conn_in, spread, sum_ref)
        return 0

    lax.fori_loop(1, NODE_DEV // (256 * SPREAD_STEP), scatter_step, 0)
    for copy in rims:
        copy.wait()
    sum_ref[:, HALO : 2 * HALO] += rim_in[0]
    sum_ref[:, NODE_DEV : NODE_DEV + HALO] += rim_in[1]
    forces_move.wait()
    totals(back, owner_ref, rank_ref, sum_ref, total, side)
    leave[1].start()
    for copy in leave:
        copy.wait()


def totals(back_ref, owner_ref, rank_ref, sum_ref, out_ref, side):
    for c in range(3):
        turned = back_ref[pl.ds(c, DEVICES, stride=8), :].T
        for i, part in enumerate(split(turned, 2)):
            side[128 * c : 128 * c + 128, 128 * i : 128 * i + 128] = part

    def block(b):
        at = lane_aligned(b, 256)
        own = onehot(DEVICES, owner_ref[0:1, at])
        found = dot(side[...], jnp.concatenate([own, own], axis=0), NN)
        rank = rank_ref[0:1, at].astype(jnp.int32)
        mine = lax.broadcasted_iota(jnp.int32, (128, 256), 0) == rank
        contact = [
            jnp.sum(jnp.where(mine, found[128 * c : 128 * c + 128], 0.0), axis=0, keepdims=True)
            for c in range(3)
        ]
        contact = jnp.concatenate([*contact, jnp.zeros((2, 256), F32)], axis=0)
        return contact - sum_ref[0:5, pl.ds(pl.multiple_of(b * 256 + HALO, HALO), 256)]

    def step(b, _):
        done = [block(b * FINISH_STEP + i) for i in range(FINISH_STEP)]
        for i, value in enumerate(done):
            out_ref[:, lane_aligned(b * FINISH_STEP + i, 256)] = value
        return 0

    lax.fori_loop(0, NODE_DEV // (256 * FINISH_STEP), step, 0)


def finish_kernel(
    total_hbm, vel_hbm, mass_hbm, cells_hbm, out_hbm, new_hbm, total, vel, mass, cells, out, new,
    in_sem, out_sem,
):
    inside = [
        pltpu.make_async_copy(src, dst, in_sem.at[i])
        for i, (src, dst) in enumerate(
            ((cells_hbm, cells), (total_hbm, total), (vel_hbm, vel), (mass_hbm, mass))
        )
    ]
    for copy in inside:
        copy.start()
    inside[0].wait()

    def pack(j, _):
        at = lane_aligned(j, 128)
        for layer in range(5):
            new[layer, :, at] = cells[pl.ds(layer * 5 * ROWS + j, 5, stride=ROWS), :]
        return 0

    lax.fori_loop(0, ROWS, pack, 0, unroll=8)
    outside = [pltpu.make_async_copy(new, new_hbm, out_sem.at[0])]
    outside[0].start()
    for copy in inside[1:]:
        copy.wait()
    out[...] = vel[...] + mass[...] * total[...]
    outside.append(pltpu.make_async_copy(out, out_hbm, out_sem.at[1]))
    outside[1].start()
    for copy in outside:
        copy.wait()


def body(
    velocity, position, inv_mass, connectivity, shape_grad, area, thickness, yield_stress, stress,
    contact_owner, face_center, face_angle, face_stiffness, ghost_list, pair_node, pair_face,
    pair_count,
):
    square = (ROWS, 128)
    owner = contact_owner.reshape(1, NODE_DEV)
    hbm = pl.BlockSpec(memory_space=pltpu.HBM)
    args = (
        owner, position, velocity, face_center, face_angle, face_stiffness.reshape(1, FACE_DEV),
        ghost_list.reshape(1, 2 * GHOST), connectivity, shape_grad, stress, area.reshape(square),
        thickness.reshape(square), yield_stress.reshape(square), pair_node, pair_face,
        pair_node.reshape(1, PAIRS), pair_count.reshape(1, 1),
    )
    held = [
        (pltpu.SMEM if len(arg.shape) == 1 else pltpu.VMEM)(arg.shape, arg.dtype) for arg in args
    ]
    dma = pltpu.SemaphoreType.DMA
    scratch = [
        ((DEVICES * 8, 128), F32), ((8, NODE_DEV + 2 * HALO), F32), ((1, NODE_DEV), F32),
        ((25 * ROWS, 128), F32), ((5, NODE_DEV), F32), ((3 * 128, 256), BF),
        ((DEVICES, 128), F32), ((448, 256), F32), ((256, 384), BF),
        ((DEVICES * 8, 128), F32), ((DEVICES * 8, 128), F32), ((FACE_DEV // 64, 128), F32),
        ((FACE_DEV // 16, 128), F32), ((8, FACE_TILES * 128), F32), ((8, 2 * GHOST), F32),
        ((2, 8, GHOST), F32), ((2, 5, HALO), F32), ((5 * EXT, 128), F32),
        ((4 * ROWS, 128), jnp.int32), ((8 * ROWS, 128), F32), ((4, 8 * ROWS, 128), F32),
        ((2, 8, HALO), F32), ((FACE_TILES, 3 * TILE, 48), BF), ((24, 3 * TILE), BF),
        ((FACE_TILES, 3, TILE, TILE), F32), ((3 * PAIRS, 128), F32), ((DEVICES * 8, 128), F32),
    ]
    total, cells = pl.pallas_call(
        step_kernel,
        out_shape=(
            jax.ShapeDtypeStruct((5, NODE_DEV), F32),
            jax.ShapeDtypeStruct((25 * ROWS, 128), F32),
        ),
        in_specs=[hbm] * len(args),
        out_specs=(hbm, hbm),
        scratch_shapes=[
            *held,
            *(pltpu.VMEM(shape, kind) for shape, kind in scratch),
            dma((len(args),)), dma((2,)), dma((2,)), dma((2,)), dma((3, 2)), dma((3, 2)),
        ],
        compiler_params=pltpu.CompilerParams(
            vmem_limit_bytes=56 * 2**20, collective_id=0, has_side_effects=True
        ),
        name="crash_step",
    )(*args)
    last = (total, velocity, inv_mass.reshape(1, NODE_DEV), cells)
    results = (
        jax.ShapeDtypeStruct((5, NODE_DEV), F32),
        jax.ShapeDtypeStruct((5, 5, NODE_DEV), F32),
    )
    return pl.pallas_call(
        finish_kernel,
        out_shape=results,
        in_specs=[hbm] * len(last),
        out_specs=(hbm, hbm),
        scratch_shapes=[
            *(pltpu.VMEM(x.shape, x.dtype) for x in (*last, *results)), dma((len(last),)), dma((2,)),
        ],
        compiler_params=pltpu.CompilerParams(vmem_limit_bytes=56 * 2**20),
        name="finish",
    )(*last)


def solution(mesh):
    axes = ("dom", "sub")
    nodes, rows, cells = P(axes), P(None, axes), P(None, None, axes)
    in_specs = (
        rows, rows, nodes, rows, cells, nodes, nodes, nodes, cells, P(axes, None), rows, rows,
        nodes, nodes, nodes, nodes, nodes,
    )
    return jax.shard_map(
        body, mesh=mesh, in_specs=in_specs, out_specs=(rows, cells), check_vma=False
    )
```

```python
import functools

import jax
import jax.numpy as jnp
from jax import lax
from jax.experimental import pallas as pl
from jax.experimental.pallas import tpu as pltpu
from jax.sharding import PartitionSpec as P

TILE = 128
HALO = 128
GHOST = 256
NODE_DEV = 8192
ROWS = NODE_DEV // 128
FACE_DEV = 2048
FACE_TILES = 20
DEVICES = 128
PAIRS = 128
EXT = ROWS + 8

LOBATTO_POINTS = (-1.0, -0.6546536707079771, 0.0, 0.6546536707079771, 1.0)
LOBATTO_WEIGHTS = (0.1, 49.0 / 90.0, 32.0 / 45.0, 49.0 / 90.0, 0.1)
PLANE_MODULUS = 1.0 / 0.91
POISSON = 0.3
SHEAR_MODULUS = 5.0 / 6.0 / 2.6
DAMPING = 0.3
REACH_SQ = 0.5
LOG2E = 1.4426950408889634

BF = jnp.bfloat16
F32 = jnp.float32
NT = (((1,), (1,)), ((), ()))
NN = (((1,), (0,)), ((), ()))


def dot(a, b, dims):
    return lax.dot_general(a, b, dims, preferred_element_type=F32)


def onehot(count, row):
    where = lax.broadcasted_iota(jnp.int32, (count, row.shape[1]), 0)
    return jnp.where(where == row, 1.0, 0.0).astype(BF)


def split(x, parts):
    out = []
    for _ in range(parts - 1):
        head = x.astype(BF)
        out.append(head)
        x = x - head.astype(F32)
    out.append(x.astype(BF))
    return out


def lane_aligned(x, size):
    return pl.ds(pl.multiple_of(x * size, size), size)


MESH = pl.DeviceIdType.MESH
RANK_STEP, PLACE_STEP, SPREAD_STEP, FACE_STEP, PAIR_STEP, FINISH_STEP = 8, 4, 8, 10, 16, 8
PARTS = (3, 3, 3, 2, 2, 2, 1)


def constitutive(corner, grad_x, grad_y, area, thickness, limit, old):
    def over(f):
        total = f(0)
        for a in range(1, 4):
            total = total + f(a)
        return total

    vx, vy, vz, rx, ry = corner
    memb_xx = over(lambda a: grad_x[a] * vx[a])
    bend_xx = over(lambda a: grad_x[a] * ry[a])
    memb_yy = over(lambda a: grad_y[a] * vy[a])
    bend_yy = -over(lambda a: grad_y[a] * rx[a])
    memb_xy = over(lambda a: grad_y[a] * vx[a] + grad_x[a] * vy[a])
    bend_xy = over(lambda a: grad_y[a] * ry[a] - grad_x[a] * rx[a])
    shear_xz = over(lambda a: grad_x[a] * vz[a]) + 0.25 * over(lambda a: ry[a])
    shear_yz = over(lambda a: grad_y[a] * vz[a]) - 0.25 * over(lambda a: rx[a])
    add_xz, add_yz = SHEAR_MODULUS * shear_xz, SHEAR_MODULUS * shear_yz
    half = 0.5 * thickness
    volume = half * area
    new, force, moment = [], [0.0] * 5, [0.0] * 3
    for layer in range(5):
        height = half * LOBATTO_POINTS[layer]
        exx = memb_xx + height * bend_xx
        eyy = memb_yy + height * bend_yy
        exy = memb_xy + height * bend_xy
        t0 = old(layer, 0) + PLANE_MODULUS * (exx + POISSON * eyy)
        t1 = old(layer, 1) + PLANE_MODULUS * (eyy + POISSON * exx)
        t2 = old(layer, 2) + PLANE_MODULUS * 0.5 * (1.0 - POISSON) * exy
        t3 = old(layer, 3) + add_xz
        t4 = old(layer, 4) + add_yz
        plus, minus = t0 + t1, t0 - t1
        mises = jnp.sqrt(
            0.25 * (plus * plus) + 0.75 * (minus * minus) + 3.0 * (t2 * t2 + t3 * t3 + t4 * t4)
        )
        factor = limit / jnp.maximum(mises, limit)
        updated = [t * factor for t in (t0, t1, t2, t3, t4)]
        new.append(updated)
        weight = LOBATTO_WEIGHTS[layer] * volume
        weighted = [weight * u for u in updated]
        force = [f + w for f, w in zip(force, weighted)]
        moment = [m + height * w for m, w in zip(moment, weighted)]
    corners = []
    for a in range(4):
        gx, gy = grad_x[a], grad_y[a]
        corners.append(
            [
                gx * force[0] + gy * force[2],
                gy * force[1] + gx * force[2],
                gx * force[3] + gy * force[4],
                -(gy * moment[1] + gx * moment[2]) - 0.25 * force[4],
                gx * moment[0] + gy * moment[2] + 0.25 * force[3],
            ]
        )
    return new, corners


def ranks(owner_ref, rank_ref, run, tri):
    row = lax.broadcasted_iota(jnp.int32, (256, 384), 0)
    column = lax.broadcasted_iota(jnp.int32, (256, 384), 1)
    tri[...] = jnp.where((row < column) | (column >= 256), 1.0, 0.0).astype(BF)
    run[...] = jnp.zeros_like(run)

    def step(b, _):
        spans = [lane_aligned(b * RANK_STEP + i, 256) for i in range(RANK_STEP)]
        where = lax.broadcasted_iota(jnp.int32, (DEVICES, 256), 0)
        hot = [jnp.where(where == owner_ref[0:1, at], 1.0, 0.0) for at in spans]
        counts = dot(jnp.concatenate([h.astype(BF) for h in hot], axis=0), tri[...], NN)
        base = run[...]
        for i, at in enumerate(spans):
            count = counts[DEVICES * i : DEVICES * i + DEVICES]
            seen = count[:, :256] + jnp.concatenate([base, base], axis=1)
            rank_ref[0:1, at] = jnp.sum(hot[i] * seen, axis=0, keepdims=True)
            base = base + count[:, 256:]
        run[...] = base
        return 0

    lax.fori_loop(0, NODE_DEV // (256 * RANK_STEP), step, 0)


def place(owner_ref, rank_ref, pos_ref, vel_ref, out_ref, acc):
    acc[...] = jnp.zeros_like(acc)

    def block(b):
        at = lane_aligned(b, 1024)
        own = owner_ref[0:1, at]
        hot = onehot(256, (own & 1) * 128 + rank_ref[0:1, at].astype(jnp.int32))
        group = onehot(64, own >> 1)
        rows = []
        for c in range(6):
            value = pos_ref[c : c + 1, at] if c < 3 else vel_ref[c - 3 : c - 2, at]
            rows += [group * part for part in split(value, PARTS[c])]
        return dot(jnp.concatenate([*rows, group], axis=0), hot, NT)

    def step(b, _):
        placed = [block(b * PLACE_STEP + i) for i in range(PLACE_STEP)]
        first = 0
        for c, parts in enumerate(PARTS):
            total = acc[c * 64 : c * 64 + 64, :]
            for _ in range(parts):
                for p in placed:
                    total = total + p[first : first + 64]
                first += 64
            acc[c * 64 : c * 64 + 64, :] = total
        return 0

    lax.fori_loop(0, NODE_DEV // (1024 * PLACE_STEP), step, 0)
    for first in range(0, 64, 8):
        for low in range(2):
            for c in range(8):
                if c < 7:
                    part = acc[c * 64 + first : c * 64 + first + 8, low * 128 : low * 128 + 128]
                else:
                    part = jnp.ones((8, 128), F32)
                out_ref[pl.ds(first * 16 + low * 8 + c, 8, stride=16), :] = part


def face_rows(center_ref, angle_ref, stiff_ref, angles, normals, out_ref):
    tiles = FACE_DEV // 128
    for j in range(tiles):
        angles[pl.ds(j, 2, stride=tiles), :] = angle_ref[:, 128 * j : 128 * j + 128]
    azimuth, elevation = angles[0:tiles, :], angles[tiles : 2 * tiles, :]
    flat = jnp.cos(elevation)
    for c, value in enumerate(
        (jnp.cos(azimuth) * flat, jnp.sin(azimuth) * flat, jnp.sin(elevation))
    ):
        normals[pl.ds(c, tiles, stride=8), :] = value
    for j in range(tiles):
        at = slice(128 * j, 128 * j + 128)
        out_ref[:, GHOST + 128 * j : GHOST + 128 * j + 128] = jnp.concatenate(
            [center_ref[:, at], normals[8 * j : 8 * j + 3, :], stiff_ref[:, at], jnp.zeros((1, 128), F32)],
            axis=0,
        )


def lend(list_ref, faces_ref, out_ref):
    for g in range(2 * GHOST // 128):
        index = jnp.broadcast_to(list_ref[:, 128 * g : 128 * g + 128], (8, 128))
        low, high = index & 127, index >> 7
        found = jnp.zeros((8, 128), F32)
        for t in range(FACE_DEV // 128):
            at = slice(GHOST + 128 * t, GHOST + 128 * t + 128)
            part = jnp.take_along_axis(faces_ref[:, at], low, axis=1)
            found = jnp.where(high == t, part, found)
        out_ref[:, 128 * g : 128 * g + 128] = found


def unpack(vel_ref, conn_ref, grad_ref, stress_ref, vel, conn, grad, stress):
    def step(j, _):
        at = lane_aligned(j, 128)
        vel[pl.ds(j + 1, 5, stride=EXT), :] = vel_ref[:, at]
        conn[pl.ds(j, 4, stride=ROWS), :] = conn_ref[:, at] - 128 * j
        for axis in range(2):
            grad[pl.ds(axis * 4 * ROWS + j, 4, stride=ROWS), :] = grad_ref[axis, :, at]
        for layer in range(5):
            stress[pl.ds(layer * 5 * ROWS + j, 5, stride=ROWS), :] = stress_ref[layer, :, at]
        return 0

    lax.fori_loop(0, ROWS, step, 0, unroll=8)


def elements(vel, conn, grad, area_ref, thick_ref, limit_ref, stress, spread):
    spread[...] = jnp.zeros_like(spread)

    def group(g, _):
        def rows(field):
            return pl.ds(pl.multiple_of(field * ROWS + 8 * g, 8), 8)

        here = pl.ds(pl.multiple_of(8 * g, 8), 8)
        index = [conn[rows(a), :] for a in range(4)]
        low = [i & 127 for i in index]
        part_of = [i >> 7 for i in index]
        corner = []
        for c in range(5):
            window = [vel[pl.ds(c * EXT + 8 * g + k, 8), :] for k in range(3)]
            values = []
            for a in range(4):
                got = [jnp.take_along_axis(w, low[a], axis=1) for w in window]
                values.append(
                    jnp.where(part_of[a] == 0, got[0], jnp.where(part_of[a] == 1, got[1], got[2]))
                )
            corner.append(values)
        grad_x = [grad[rows(a), :] for a in range(4)]
        grad_y = [grad[rows(4 + a), :] for a in range(4)]
        new, forces = constitutive(
            corner, grad_x, grad_y, area_ref[here, :], thick_ref[here, :], limit_ref[here, :],
            lambda layer, c: stress[rows(5 * layer + c), :],
        )
        for layer in range(5):
            for c in range(5):
                stress[rows(5 * layer + c), :] = new[layer][c]
        for a in range(4):
            for c in range(5):
                spread[a, pl.ds(64 * g + c, 8, stride=8), :] = forces[a][c]
        return 0

    lax.fori_loop(0, 8, group, 0)


def scatter(b, conn_ref, spread):
    at = lane_aligned(b, 256)
    index = jnp.concatenate([conn_ref[a : a + 1, at] for a in range(4)], axis=1) - 256 * b
    hot = onehot(128, index & 127)
    window = index >> 7
    value = jnp.concatenate(
        [spread[a, lane_aligned(2 * b + h, 8), :] for a in range(4) for h in range(2)], axis=1
    )
    parts = split(value, 2)
    rows = []
    for h in range(4):
        mine = jnp.where(window == h, 1.0, 0.0).astype(BF)
        rows += [part * mine for part in parts]
    found = dot(hot, jnp.concatenate(rows, axis=0), NT).T
    return [found[16 * h : 16 * h + 8] + found[16 * h + 8 : 16 * h + 16] for h in range(4)]


def scatter_blocks(blocks, conn_ref, spread, sum_ref):
    found = [scatter(b, conn_ref, spread) for b in blocks]
    for b, windows in zip(blocks, found):
        for h, window in enumerate(windows):
            sum_ref[:, lane_aligned(2 * b + h, 128)] += window


def six_terms(x):
    high, mid, low = (part.astype(F32) for part in split(x, 3))
    return jnp.concatenate([high, mid, high, mid, low, high], axis=0)


def face_tables(faces_ref, forms, pick, normals):
    row = lax.broadcasted_iota(jnp.int32, (24, 3 * TILE), 0)
    column = lax.broadcasted_iota(jnp.int32, (24, 3 * TILE), 1)
    pick[...] = jnp.where((row & 7) == (column >> 7), 1.0, 0.0).astype(BF)

    def tile(f):
        x = faces_ref[:, lane_aligned(f, TILE)]
        r, m = [x[i : i + 1] for i in range(3)], [x[i : i + 1] for i in range(3, 6)]
        apart = m[0] * r[0] + m[1] * r[1] + m[2] * r[2]
        square = r[0] * r[0] + r[1] * r[1] + r[2] * r[2]
        strength = x[6:7] * jnp.exp2((-LOG2E / REACH_SQ) * square)
        none = jnp.zeros_like(apart)
        depth = [*(-strength * v for v in m), none, none, none, none, strength * apart]
        along = [none, none, none, *(-DAMPING * v for v in m), none, jnp.ones_like(apart)]
        reach = [*((2.0 / REACH_SQ * LOG2E) * v for v in r), none, none, none, none, none]
        for i, form in enumerate((depth, along, reach)):
            terms = six_terms(jnp.concatenate(form, axis=0))
            forms[f, TILE * i : TILE * i + TILE, :] = terms.T.astype(BF)
        parts = [part.astype(F32) for part in split(jnp.concatenate([*m] + [none] * 5, axis=0), 3)]
        wide = dot(jnp.concatenate(parts, axis=0).T.astype(BF), pick[...], NN)
        for i in range(3):
            normals[f, i] = wide[:, TILE * i : TILE * i + TILE]

    def step(b, _):
        for i in range(FACE_STEP):
            tile(b * FACE_STEP + i)
        return 0

    lax.fori_loop(0, FACE_TILES // FACE_STEP, step, 0)


def pair_force(x, form, normal_of):
    high, mid, low = split(x, 3)
    products = dot(form, jnp.concatenate([high, high, mid, mid, high, low], axis=0), NN)
    square = x[0:1] * x[0:1] + x[1:2] * x[1:2] + x[2:3] * x[2:3]
    scale = x[6:7] * jnp.exp2((-LOG2E / REACH_SQ) * square)
    total = [jnp.zeros((8, TILE), F32) for _ in range(3)]
    for k in range(0, TILE, 8):
        depth = jnp.maximum(products[k : k + 8], 0.0)
        along = products[TILE + k : TILE + k + 8]
        size = depth * along * jnp.exp2(products[2 * TILE + k : 2 * TILE + k + 8])
        total = [t + size * normal_of(i, k) for i, t in enumerate(total)]
    return [scale * jnp.sum(t, axis=0, keepdims=True) for t in total]


def step_kernel(*refs):
    inputs, outputs, held, scratch = refs[:17], refs[17:19], refs[19:36], refs[36:]
    (
        owner_ref, pos_ref, vel_ref, center_ref, angle_ref, stiff_ref, list_ref, conn_in, grad_in,
        stress_in, area_ref, thick_ref, limit_ref, node_ref, face_of_ref, node_row_ref, count_ref,
    ) = held
    total_hbm, cells_hbm = outputs
    (
        back, sum_ref, rank_ref, stress, total, side, run, acc, tri, going, coming, angles, unit,
        faces, lent, ghost_in, vel_in, vel, conn, grad, spread, rim_in, forms, pick, normals, pairs,
        leaving, load_sem, out_sem, send_sem, recv_sem, edge_send, edge_recv,
    ) = scratch
    sub_count = lax.axis_size("sub")
    me = lax.axis_index("dom") * sub_count + lax.axis_index("sub")

    def device(k):
        to = lax.rem(me + k, DEVICES)
        return to, (lax.div(to, sub_count), lax.rem(to, sub_count))

    loads = [
        pltpu.make_async_copy(src, dst, load_sem.at[i])
        for i, (src, dst) in enumerate(zip(inputs, held))
    ]
    for copy in loads:
        copy.start()
    coming[pl.ds(7, DEVICES, stride=8), :] = jnp.ones((DEVICES, 128), F32)
    barrier = pltpu.get_barrier_semaphore()

    def greet(k, _):
        pl.semaphore_signal(barrier, inc=1, device_id=device(k)[1], device_id_type=MESH)
        return 0

    lax.fori_loop(1, DEVICES, greet, 0)
    for copy in loads[:3]:
        copy.wait()
    ranks(owner_ref, rank_ref, run, tri)
    place(owner_ref, rank_ref, pos_ref, vel_ref, going, acc)
    pl.semaphore_wait(barrier, DEVICES - 1)

    def edges(i, first, last, land):
        pair = []
        for end, (src, k) in enumerate(((last, 1), (first, DEVICES - 1))):
            copy = pltpu.make_async_remote_copy(
                src, land.at[end], edge_send.at[i, end], edge_recv.at[i, end],
                device_id=device(k)[1], device_id_type=MESH,
            )
            copy.start()
            pair.append(copy)
        return pair

    def tile(i):
        return pl.ds(pl.multiple_of(8 * i, 8), 8)

    def exchange(i, src, dst, rows):
        def part(t):
            return pl.ds(pl.multiple_of(8 * t, 8), rows)

        def send(k, _):
            to, where = device(k)
            pltpu.make_async_remote_copy(
                src.at[part(to)], dst.at[part(me)], send_sem.at[i], recv_sem.at[i],
                device_id=where, device_id_type=MESH,
            ).start()
            return 0

        lax.fori_loop(1, DEVICES, send, 0)
        dst[tile(me), :] = src[tile(me), :]
        others = pl.ds(0, (DEVICES - 1) * rows)
        return pltpu.make_async_remote_copy(
            src.at[others], dst.at[others], send_sem.at[i], recv_sem.at[i],
            device_id=device(1)[1], device_id_type=MESH,
        )

    halo = edges(0, vel_ref.at[:, 0:HALO], vel_ref.at[:, NODE_DEV - HALO : NODE_DEV], vel_in)
    nodes_move = exchange(0, going, coming, 7)
    for copy in loads[3:]:
        copy.wait()
    face_rows(center_ref, angle_ref, stiff_ref, angles, unit, faces)
    lend(list_ref, faces, lent)
    ghosts = edges(1, lent.at[:, 0:GHOST], lent.at[:, GHOST : 2 * GHOST], ghost_in)
    unpack(vel_ref, conn_in, grad_in, stress_in, vel, conn, grad, stress)
    for copy in halo:
        copy.wait()
    vel[pl.ds(0, 5, stride=EXT), :] = vel_in[0]
    vel[pl.ds(ROWS + 1, 5, stride=EXT), :] = vel_in[1]
    elements(vel, conn, grad, area_ref, thick_ref, limit_ref, stress, spread)
    leave = [
        pltpu.make_async_copy(src, dst, out_sem.at[i])
        for i, (src, dst) in enumerate(((stress, cells_hbm), (total, total_hbm)))
    ]
    leave[0].start()
    for copy in ghosts:
        copy.wait()
    faces[:, 0:GHOST] = jnp.where(me > 0, ghost_in[0], 0.0)
    faces[:, GHOST + FACE_DEV :] = jnp.where(me < DEVICES - 1, ghost_in[1], 0.0)
    face_tables(faces, forms, pick, normals)
    nodes_move.wait()

    tiles = coming.reshape(DEVICES, 8, 128)

    def pair_step(b, _):
        first = b * PAIR_STEP
        forces = []
        for i in range(PAIR_STEP):
            x, f = tiles[node_ref[first + i]], face_of_ref[first + i]
            forces.append(pair_force(x, forms[f], lambda c, k, f=f: normals[f, c, k : k + 8]))
        for i, force in enumerate(forces):
            for c in range(3):
                pairs[pl.ds(c * PAIRS + first + i, 1), :] = force[c]
        return 0

    lax.fori_loop(0, PAIRS // PAIR_STEP, pair_step, 0)
    slot = lax.broadcasted_iota(jnp.int32, (1, PAIRS), 1)
    listed = onehot(DEVICES, jnp.where(slot < count_ref[...], node_row_ref[...], -1))
    listed = jnp.concatenate([listed] * 3, axis=1)
    leaving[...] = jnp.zeros_like(leaving)
    for c in range(3):
        parts = jnp.concatenate(split(pairs[c * PAIRS : (c + 1) * PAIRS, :], 3), axis=0)
        leaving[pl.ds(c, DEVICES, stride=8), :] = dot(listed, parts, NN)
    forces_move = exchange(1, leaving, back, 3)

    sum_ref[...] = jnp.zeros_like(sum_ref)
    last = NODE_DEV // 256 - 1
    scatter_blocks([0, last, *range(1, SPREAD_STEP - 1)], conn_in, spread, sum_ref)
    rims = edges(
        2, sum_ref.at[:, 0:HALO], sum_ref.at[:, HALO + NODE_DEV : 2 * HALO + NODE_DEV], rim_in
    )

    def scatter_step(b, _):
        first = b * SPREAD_STEP - 1
        scatter_blocks([first + i for i in range(SPREAD_STEP)], conn_in, spread, sum_ref)
        return 0

    lax.fori_loop(1, NODE_DEV // (256 * SPREAD_STEP), scatter_step, 0)
    for copy in rims:
        copy.wait()
    sum_ref[:, HALO : 2 * HALO] += rim_in[0]
    sum_ref[:, NODE_DEV : NODE_DEV + HALO] += rim_in[1]
    forces_move.wait()
    totals(back, owner_ref, rank_ref, sum_ref, total, side)
    leave[1].start()
    for copy in leave:
        copy.wait()


def totals(back_ref, owner_ref, rank_ref, sum_ref, out_ref, side):
    for c in range(3):
        turned = back_ref[pl.ds(c, DEVICES, stride=8), :].T
        for i, part in enumerate(split(turned, 2)):
            side[128 * c : 128 * c + 128, 128 * i : 128 * i + 128] = part

    def block(b):
        at = lane_aligned(b, 256)
        own = onehot(DEVICES, owner_ref[0:1, at])
        found = dot(side[...], jnp.concatenate([own, own], axis=0), NN)
        rank = rank_ref[0:1, at].astype(jnp.int32)
        mine = lax.broadcasted_iota(jnp.int32, (128, 256), 0) == rank
        contact = [
            jnp.sum(jnp.where(mine, found[128 * c : 128 * c + 128], 0.0), axis=0, keepdims=True)
            for c in range(3)
        ]
        contact = jnp.concatenate([*contact, jnp.zeros((2, 256), F32)], axis=0)
        return contact - sum_ref[0:5, pl.ds(pl.multiple_of(b * 256 + HALO, HALO), 256)]

    def step(b, _):
        done = [block(b * FINISH_STEP + i) for i in range(FINISH_STEP)]
        for i, value in enumerate(done):
            out_ref[:, lane_aligned(b * FINISH_STEP + i, 256)] = value
        return 0

    lax.fori_loop(0, NODE_DEV // (256 * FINISH_STEP), step, 0)


def finish_kernel(
    total_hbm, vel_hbm, mass_hbm, cells_hbm, out_hbm, new_hbm, total, vel, mass, cells, out, new,
    in_sem, out_sem,
):
    size = 5 * ROWS
    moves = [(total_hbm, total), (vel_hbm, vel), (mass_hbm, mass)]
    moves += [
        (cells_hbm.at[pl.ds(i * size, size)], cells.at[pl.ds(i * size, size)]) for i in range(5)
    ]
    inside = [pltpu.make_async_copy(*move, in_sem.at[i]) for i, move in enumerate(moves)]
    for copy in inside:
        copy.start()
    for copy in inside[:3]:
        copy.wait()
    out[...] = vel[...] + mass[...] * total[...]
    outside = [pltpu.make_async_copy(out, out_hbm, out_sem.at[5])]
    outside[0].start()
    for layer in range(5):
        inside[3 + layer].wait()
        for j in range(ROWS):
            part = cells[pl.ds(layer * size + j, 5, stride=ROWS), :]
            new[layer, :, 128 * j : 128 * j + 128] = part
        copy = pltpu.make_async_copy(new.at[layer], new_hbm.at[layer], out_sem.at[layer])
        copy.start()
        outside.append(copy)
    for copy in outside:
        copy.wait()


def body(
    velocity, position, inv_mass, connectivity, shape_grad, area, thickness, yield_stress, stress,
    contact_owner, face_center, face_angle, face_stiffness, ghost_list, pair_node, pair_face,
    pair_count,
):
    square = (ROWS, 128)
    owner = contact_owner.reshape(1, NODE_DEV)
    hbm = pl.BlockSpec(memory_space=pltpu.HBM)
    args = (
        owner, position, velocity, face_center, face_angle, face_stiffness.reshape(1, FACE_DEV),
        ghost_list.reshape(1, 2 * GHOST), connectivity, shape_grad, stress, area.reshape(square),
        thickness.reshape(square), yield_stress.reshape(square), pair_node, pair_face,
        pair_node.reshape(1, PAIRS), pair_count.reshape(1, 1),
    )
    held = [
        (pltpu.SMEM if len(arg.shape) == 1 else pltpu.VMEM)(arg.shape, arg.dtype) for arg in args
    ]
    dma = pltpu.SemaphoreType.DMA
    scratch = [
        ((DEVICES * 8, 128), F32), ((8, NODE_DEV + 2 * HALO), F32), ((1, NODE_DEV), F32),
        ((25 * ROWS, 128), F32), ((5, NODE_DEV), F32), ((3 * 128, 256), BF),
        ((DEVICES, 128), F32), ((448, 256), F32), ((256, 384), BF),
        ((DEVICES * 8, 128), F32), ((DEVICES * 8, 128), F32), ((FACE_DEV // 64, 128), F32),
        ((FACE_DEV // 16, 128), F32), ((8, FACE_TILES * 128), F32), ((8, 2 * GHOST), F32),
        ((2, 8, GHOST), F32), ((2, 5, HALO), F32), ((5 * EXT, 128), F32),
        ((4 * ROWS, 128), jnp.int32), ((8 * ROWS, 128), F32), ((4, 8 * ROWS, 128), F32),
        ((2, 8, HALO), F32), ((FACE_TILES, 3 * TILE, 48), BF), ((24, 3 * TILE), BF),
        ((FACE_TILES, 3, TILE, TILE), F32), ((3 * PAIRS, 128), F32), ((DEVICES * 8, 128), F32),
    ]
    total, cells = pl.pallas_call(
        step_kernel,
        out_shape=(
            jax.ShapeDtypeStruct((5, NODE_DEV), F32),
            jax.ShapeDtypeStruct((25 * ROWS, 128), F32),
        ),
        in_specs=[hbm] * len(args),
        out_specs=(hbm, hbm),
        scratch_shapes=[
            *held,
            *(pltpu.VMEM(shape, kind) for shape, kind in scratch),
            dma((len(args),)), dma((2,)), dma((2,)), dma((2,)), dma((3, 2)), dma((3, 2)),
        ],
        compiler_params=pltpu.CompilerParams(
            vmem_limit_bytes=56 * 2**20, collective_id=0, has_side_effects=True
        ),
        name="crash_step",
    )(*args)
    last = (total, velocity, inv_mass.reshape(1, NODE_DEV), cells)
    results = (
        jax.ShapeDtypeStruct((5, NODE_DEV), F32),
        jax.ShapeDtypeStruct((5, 5, NODE_DEV), F32),
    )
    return pl.pallas_call(
        finish_kernel,
        out_shape=results,
        in_specs=[hbm] * len(last),
        out_specs=(hbm, hbm),
        scratch_shapes=[
            *(pltpu.VMEM(x.shape, x.dtype) for x in (*last, *results)), dma((8,)), dma((6,)),
        ],
        compiler_params=pltpu.CompilerParams(vmem_limit_bytes=56 * 2**20),
        name="finish",
    )(*last)


def solution(mesh):
    axes = ("dom", "sub")
    nodes, rows, cells = P(axes), P(None, axes), P(None, None, axes)
    in_specs = (
        rows, rows, nodes, rows, cells, nodes, nodes, nodes, cells, P(axes, None), rows, rows,
        nodes, nodes, nodes, nodes, nodes,
    )
    return jax.shard_map(
        body, mesh=mesh, in_specs=in_specs, out_specs=(rows, cells), check_vma=False
    )
```

```python
import itertools

import jax
import jax.numpy as jnp
from jax import lax
from jax.experimental import pallas as pl
from jax.experimental.pallas import tpu as pltpu
from jax.sharding import PartitionSpec as P

TILE = 128
HALO = 128
GHOST = 256
NODE_DEV = 8192
ROWS = NODE_DEV // 128
FACE_DEV = 2048
FACE_TILES = 20
DEVICES = 128
PAIRS = 128
EXT = ROWS + 8

LOBATTO_POINTS = (-1.0, -0.6546536707079771, 0.0, 0.6546536707079771, 1.0)
LOBATTO_WEIGHTS = (0.1, 49.0 / 90.0, 32.0 / 45.0, 49.0 / 90.0, 0.1)
PLANE_MODULUS = 1.0 / 0.91
POISSON = 0.3
SHEAR_MODULUS = 5.0 / 6.0 / 2.6
DAMPING = 0.3
REACH_SQ = 0.5
LOG2E = 1.4426950408889634

BF = jnp.bfloat16
F32 = jnp.float32
NT = (((1,), (1,)), ((), ()))
NN = (((1,), (0,)), ((), ()))


def dot(a, b, dims):
    return lax.dot_general(a, b, dims, preferred_element_type=F32)


def onehot(count, row):
    where = lax.broadcasted_iota(jnp.int32, (count, row.shape[1]), 0)
    return jnp.where(where == row, 1.0, 0.0).astype(BF)


def split(x, parts):
    out = []
    for _ in range(parts - 1):
        head = x.astype(BF)
        out.append(head)
        x = x - head.astype(F32)
    out.append(x.astype(BF))
    return out


def lane_aligned(x, size):
    return pl.ds(pl.multiple_of(x * size, size), size)


MESH = pl.DeviceIdType.MESH
RANK_STEP, PLACE_STEP, SPREAD_STEP, FACE_STEP, PAIR_STEP, FINISH_STEP = 16, 4, 8, 10, 16, 8
PARTS = (2, 2, 2, 2, 2, 2, 1)


def constitutive(corner, grad_x, grad_y, area, thickness, limit, old):
    def over(f):
        total = f(0)
        for a in range(1, 4):
            total = total + f(a)
        return total

    vx, vy, vz, rx, ry = corner
    memb_xx = over(lambda a: grad_x[a] * vx[a])
    bend_xx = over(lambda a: grad_x[a] * ry[a])
    memb_yy = over(lambda a: grad_y[a] * vy[a])
    bend_yy = -over(lambda a: grad_y[a] * rx[a])
    memb_xy = over(lambda a: grad_y[a] * vx[a] + grad_x[a] * vy[a])
    bend_xy = over(lambda a: grad_y[a] * ry[a] - grad_x[a] * rx[a])
    shear_xz = over(lambda a: grad_x[a] * vz[a]) + 0.25 * over(lambda a: ry[a])
    shear_yz = over(lambda a: grad_y[a] * vz[a]) - 0.25 * over(lambda a: rx[a])
    add_xz, add_yz = SHEAR_MODULUS * shear_xz, SHEAR_MODULUS * shear_yz
    half = 0.5 * thickness
    volume = half * area
    new, force, moment = [], [0.0] * 5, [0.0] * 3
    for layer in range(5):
        height = half * LOBATTO_POINTS[layer]
        exx = memb_xx + height * bend_xx
        eyy = memb_yy + height * bend_yy
        exy = memb_xy + height * bend_xy
        t0 = old(layer, 0) + PLANE_MODULUS * (exx + POISSON * eyy)
        t1 = old(layer, 1) + PLANE_MODULUS * (eyy + POISSON * exx)
        t2 = old(layer, 2) + PLANE_MODULUS * 0.5 * (1.0 - POISSON) * exy
        t3 = old(layer, 3) + add_xz
        t4 = old(layer, 4) + add_yz
        plus, minus = t0 + t1, t0 - t1
        mises = jnp.sqrt(
            0.25 * (plus * plus) + 0.75 * (minus * minus) + 3.0 * (t2 * t2 + t3 * t3 + t4 * t4)
        )
        factor = limit / jnp.maximum(mises, limit)
        updated = [t * factor for t in (t0, t1, t2, t3, t4)]
        new.append(updated)
        weight = LOBATTO_WEIGHTS[layer] * volume
        weighted = [weight * u for u in updated]
        force = [f + w for f, w in zip(force, weighted)]
        moment = [m + height * w for m, w in zip(moment, weighted)]
    corners = []
    for a in range(4):
        gx, gy = grad_x[a], grad_y[a]
        corners.append(
            [
                gx * force[0] + gy * force[2],
                gy * force[1] + gx * force[2],
                gx * force[3] + gy * force[4],
                -(gy * moment[1] + gx * moment[2]) - 0.25 * force[4],
                gx * moment[0] + gy * moment[2] + 0.25 * force[3],
            ]
        )
    return new, corners


def ranks(owner_ref, rank_ref, run, tri):
    row = lax.broadcasted_iota(jnp.int32, (256, 384), 0)
    column = lax.broadcasted_iota(jnp.int32, (256, 384), 1)
    tri[...] = jnp.where((row < column) | (column >= 256), 1.0, 0.0).astype(BF)
    run[...] = jnp.zeros_like(run)

    def step(b, _):
        spans = [lane_aligned(b * RANK_STEP + i, 256) for i in range(RANK_STEP)]
        where = lax.broadcasted_iota(jnp.int32, (DEVICES, 256), 0)
        hot = [jnp.where(where == owner_ref[0:1, at], 1.0, 0.0) for at in spans]
        counts = dot(jnp.concatenate([h.astype(BF) for h in hot], axis=0), tri[...], NN)
        base = run[...]
        for i, at in enumerate(spans):
            count = counts[DEVICES * i : DEVICES * i + DEVICES]
            seen = count[:, :256] + jnp.concatenate([base, base], axis=1)
            rank_ref[0:1, at] = jnp.sum(hot[i] * seen, axis=0, keepdims=True)
            base = base + count[:, 256:]
        run[...] = base
        return 0

    lax.fori_loop(0, NODE_DEV // (256 * RANK_STEP), step, 0)


def place(owner_ref, rank_ref, pos_ref, vel_ref, out_ref, acc):
    acc[...] = jnp.zeros_like(acc)

    def block(b):
        at = lane_aligned(b, 1024)
        own = owner_ref[0:1, at]
        hot = onehot(256, (own & 1) * 128 + rank_ref[0:1, at].astype(jnp.int32))
        group = onehot(64, own >> 1)
        rows = []
        for c in range(6):
            value = pos_ref[c : c + 1, at] if c < 3 else vel_ref[c - 3 : c - 2, at]
            rows += [group * part for part in split(value, PARTS[c])]
        return dot(jnp.concatenate([*rows, group], axis=0), hot, NT)

    def step(b, _):
        placed = [block(b * PLACE_STEP + i) for i in range(PLACE_STEP)]
        first = 0
        for c, parts in enumerate(PARTS):
            total = acc[c * 64 : c * 64 + 64, :]
            for _ in range(parts):
                for p in placed:
                    total = total + p[first : first + 64]
                first += 64
            acc[c * 64 : c * 64 + 64, :] = total
        return 0

    lax.fori_loop(0, NODE_DEV // (1024 * PLACE_STEP), step, 0)
    for first in range(0, 64, 8):
        for low in range(2):
            for c in range(8):
                if c < 7:
                    part = acc[c * 64 + first : c * 64 + first + 8, low * 128 : low * 128 + 128]
                else:
                    part = jnp.ones((8, 128), F32)
                out_ref[pl.ds(first * 16 + low * 8 + c, 8, stride=16), :] = part


def face_rows(center_ref, angle_ref, stiff_ref, angles, normals, out_ref):
    tiles = FACE_DEV // 128
    for j in range(tiles):
        angles[pl.ds(j, 2, stride=tiles), :] = angle_ref[:, 128 * j : 128 * j + 128]
    azimuth, elevation = angles[0:tiles, :], angles[tiles : 2 * tiles, :]
    flat = jnp.cos(elevation)
    for c, value in enumerate(
        (jnp.cos(azimuth) * flat, jnp.sin(azimuth) * flat, jnp.sin(elevation))
    ):
        normals[pl.ds(c, tiles, stride=8), :] = value
    for j in range(tiles):
        at = slice(128 * j, 128 * j + 128)
        out_ref[:, GHOST + 128 * j : GHOST + 128 * j + 128] = jnp.concatenate(
            [center_ref[:, at], normals[8 * j : 8 * j + 3, :], stiff_ref[:, at], jnp.zeros((1, 128), F32)],
            axis=0,
        )


def lend(list_ref, faces_ref, out_ref):
    for g in range(2 * GHOST // 128):
        index = jnp.broadcast_to(list_ref[:, 128 * g : 128 * g + 128], (8, 128))
        low, high = index & 127, index >> 7
        found = jnp.zeros((8, 128), F32)
        for t in range(FACE_DEV // 128):
            at = slice(GHOST + 128 * t, GHOST + 128 * t + 128)
            part = jnp.take_along_axis(faces_ref[:, at], low, axis=1)
            found = jnp.where(high == t, part, found)
        out_ref[:, 128 * g : 128 * g + 128] = found


def unpack(vel_ref, conn_ref, grad_ref, stress_ref, vel, conn, grad, stress):
    def step(j, _):
        at = lane_aligned(j, 128)
        vel[pl.ds(j + 1, 5, stride=EXT), :] = vel_ref[:, at]
        conn[pl.ds(j, 4, stride=ROWS), :] = conn_ref[:, at] - 128 * j
        for axis in range(2):
            grad[pl.ds(axis * 4 * ROWS + j, 4, stride=ROWS), :] = grad_ref[axis, :, at]
        for layer in range(5):
            stress[pl.ds(layer * 5 * ROWS + j, 5, stride=ROWS), :] = stress_ref[layer, :, at]
        return 0

    lax.fori_loop(0, ROWS, step, 0, unroll=8)


def elements(vel, conn, grad, area_ref, thick_ref, limit_ref, stress, spread):
    spread[...] = jnp.zeros_like(spread)

    def group(g, _):
        def rows(field):
            return pl.ds(pl.multiple_of(field * ROWS + 8 * g, 8), 8)

        here = pl.ds(pl.multiple_of(8 * g, 8), 8)
        index = [conn[rows(a), :] for a in range(4)]
        low = [i & 127 for i in index]
        part_of = [i >> 7 for i in index]
        corner = []
        for c in range(5):
            window = [vel[pl.ds(c * EXT + 8 * g + k, 8), :] for k in range(3)]
            values = []
            for a in range(4):
                got = [jnp.take_along_axis(w, low[a], axis=1) for w in window]
                values.append(
                    jnp.where(part_of[a] == 0, got[0], jnp.where(part_of[a] == 1, got[1], got[2]))
                )
            corner.append(values)
        grad_x = [grad[rows(a), :] for a in range(4)]
        grad_y = [grad[rows(4 + a), :] for a in range(4)]
        new, forces = constitutive(
            corner, grad_x, grad_y, area_ref[here, :], thick_ref[here, :], limit_ref[here, :],
            lambda layer, c: stress[rows(5 * layer + c), :],
        )
        for layer in range(5):
            for c in range(5):
                stress[rows(5 * layer + c), :] = new[layer][c]
        for a in range(4):
            for c in range(5):
                spread[a, pl.ds(64 * g + c, 8, stride=8), :] = forces[a][c]
        return 0

    lax.fori_loop(0, 8, group, 0)


def scatter(b, conn_ref, spread):
    at = lane_aligned(b, 256)
    index = jnp.concatenate([conn_ref[a : a + 1, at] for a in range(4)], axis=1) - 256 * b
    hot = onehot(128, index & 127)
    window = index >> 7
    value = jnp.concatenate(
        [spread[a, lane_aligned(2 * b + h, 8), :] for a in range(4) for h in range(2)], axis=1
    )
    parts = split(value, 2)
    rows = []
    for h in range(4):
        mine = jnp.where(window == h, 1.0, 0.0).astype(BF)
        rows += [part * mine for part in parts]
    found = dot(hot, jnp.concatenate(rows, axis=0), NT).T
    return [found[16 * h : 16 * h + 8] + found[16 * h + 8 : 16 * h + 16] for h in range(4)]


def scatter_blocks(blocks, conn_ref, spread, sum_ref):
    found = [scatter(b, conn_ref, spread) for b in blocks]
    for b, windows in zip(blocks, found):
        for h, window in enumerate(windows):
            sum_ref[:, lane_aligned(2 * b + h, 128)] += window


def six_terms(x):
    high, mid, low = (part.astype(F32) for part in split(x, 3))
    return jnp.concatenate([high, mid, high, mid, low, high], axis=0)


def face_tables(faces_ref, forms, pick, normals):
    row = lax.broadcasted_iota(jnp.int32, (24, 3 * TILE), 0)
    column = lax.broadcasted_iota(jnp.int32, (24, 3 * TILE), 1)
    pick[...] = jnp.where((row & 7) == (column >> 7), 1.0, 0.0).astype(BF)

    def tile(f):
        x = faces_ref[:, lane_aligned(f, TILE)]
        r, m = [x[i : i + 1] for i in range(3)], [x[i : i + 1] for i in range(3, 6)]
        apart = m[0] * r[0] + m[1] * r[1] + m[2] * r[2]
        square = r[0] * r[0] + r[1] * r[1] + r[2] * r[2]
        strength = x[6:7] * jnp.exp2((-LOG2E / REACH_SQ) * square)
        none = jnp.zeros_like(apart)
        depth = [*(-strength * v for v in m), none, none, none, none, strength * apart]
        along = [none, none, none, *(-DAMPING * v for v in m), none, jnp.ones_like(apart)]
        reach = [*((2.0 / REACH_SQ * LOG2E) * v for v in r), none, none, none, none, none]
        for i, form in enumerate((depth, along, reach)):
            terms = six_terms(jnp.concatenate(form, axis=0))
            forms[f, TILE * i : TILE * i + TILE, :] = terms.T.astype(BF)
        parts = [part.astype(F32) for part in split(jnp.concatenate([*m] + [none] * 5, axis=0), 3)]
        wide = dot(jnp.concatenate(parts, axis=0).T.astype(BF), pick[...], NN)
        for i in range(3):
            normals[f, i] = wide[:, TILE * i : TILE * i + TILE]

    def step(b, _):
        for i in range(FACE_STEP):
            tile(b * FACE_STEP + i)
        return 0

    lax.fori_loop(0, FACE_TILES // FACE_STEP, step, 0)


def pair_force(x, form, normal_of):
    high, mid, low = split(x, 3)
    products = dot(form, jnp.concatenate([high, high, mid, mid, high, low], axis=0), NN)
    square = x[0:1] * x[0:1] + x[1:2] * x[1:2] + x[2:3] * x[2:3]
    scale = x[6:7] * jnp.exp2((-LOG2E / REACH_SQ) * square)
    total = [jnp.zeros((8, TILE), F32) for _ in range(3)]
    for k in range(0, TILE, 8):
        depth = jnp.maximum(products[k : k + 8], 0.0)
        along = products[TILE + k : TILE + k + 8]
        size = depth * along * jnp.exp2(products[2 * TILE + k : 2 * TILE + k + 8])
        total = [t + size * normal_of(i, k) for i, t in enumerate(total)]
    return [scale * jnp.sum(t, axis=0, keepdims=True) for t in total]


def reach(offset):
    z, y, core, x = offset
    return sum(min(d, 4 - d) for d in (z, y, x)) + 0.5 * core


OFFSETS = sorted(itertools.product(range(4), range(4), range(2), range(4)), key=reach)[:0:-1]


def step_kernel(*refs):
    inputs, outputs, held, scratch = refs[:17], refs[17:19], refs[19:36], refs[36:]
    (
        owner_ref, pos_ref, vel_ref, center_ref, angle_ref, stiff_ref, list_ref, conn_in, grad_in,
        stress_in, area_ref, thick_ref, limit_ref, node_ref, face_of_ref, node_row_ref, count_ref,
    ) = held
    total_hbm, cells_hbm = outputs
    (
        back, sum_ref, rank_ref, stress, total, side, run, acc, tri, going, coming, angles, unit,
        faces, lent, ghost_in, vel_in, vel, conn, grad, spread, rim_in, forms, pick, normals, pairs,
        leaving, load_sem, out_sem, send_sem, recv_sem, edge_send, edge_recv,
    ) = scratch
    sub_count = lax.axis_size("sub")
    me = lax.axis_index("dom") * sub_count + lax.axis_index("sub")

    def device(k):
        to = lax.rem(me + k, DEVICES)
        return to, (lax.div(to, sub_count), lax.rem(to, sub_count))

    digits = (lax.div(me, 32), lax.rem(lax.div(me, 8), 4), lax.rem(lax.div(me, 4), 2), lax.rem(me, 4))

    def device_at(offset):
        z, y, core, x = (
            lax.rem(digit + step, size) for digit, step, size in zip(digits, offset, (4, 4, 2, 4))
        )
        group = (z * 4 + y) * 2 + core
        return group * 4 + x, (group, x)

    loads = [
        pltpu.make_async_copy(src, dst, load_sem.at[i])
        for i, (src, dst) in enumerate(zip(inputs, held))
    ]
    for copy in loads:
        copy.start()
    coming[pl.ds(7, DEVICES, stride=8), :] = jnp.ones((DEVICES, 128), F32)
    barrier = pltpu.get_barrier_semaphore()

    def greet(k, _):
        pl.semaphore_signal(barrier, inc=1, device_id=device(k)[1], device_id_type=MESH)
        return 0

    lax.fori_loop(1, DEVICES, greet, 0)
    for copy in loads[:3]:
        copy.wait()
    ranks(owner_ref, rank_ref, run, tri)
    place(owner_ref, rank_ref, pos_ref, vel_ref, going, acc)
    pl.semaphore_wait(barrier, DEVICES - 1)

    def edges(i, first, last, land):
        pair = []
        for end, (src, k) in enumerate(((last, 1), (first, DEVICES - 1))):
            copy = pltpu.make_async_remote_copy(
                src, land.at[end], edge_send.at[i, end], edge_recv.at[i, end],
                device_id=device(k)[1], device_id_type=MESH,
            )
            copy.start()
            pair.append(copy)
        return pair

    def tile(i):
        return pl.ds(pl.multiple_of(8 * i, 8), 8)

    def exchange(i, src, dst, rows):
        def part(t):
            return pl.ds(pl.multiple_of(8 * t, 8), rows)

        for offset in OFFSETS:
            to, where = device_at(offset)
            pltpu.make_async_remote_copy(
                src.at[part(to)], dst.at[part(me)], send_sem.at[i], recv_sem.at[i],
                device_id=where, device_id_type=MESH,
            ).start()

        dst[tile(me), :] = src[tile(me), :]
        others = pl.ds(0, (DEVICES - 1) * rows)
        return pltpu.make_async_remote_copy(
            src.at[others], dst.at[others], send_sem.at[i], recv_sem.at[i],
            device_id=device(1)[1], device_id_type=MESH,
        )

    halo = edges(0, vel_ref.at[:, 0:HALO], vel_ref.at[:, NODE_DEV - HALO : NODE_DEV], vel_in)
    nodes_move = exchange(0, going, coming, 7)
    for copy in loads[3:]:
        copy.wait()
    face_rows(center_ref, angle_ref, stiff_ref, angles, unit, faces)
    lend(list_ref, faces, lent)
    ghosts = edges(1, lent.at[:, 0:GHOST], lent.at[:, GHOST : 2 * GHOST], ghost_in)
    unpack(vel_ref, conn_in, grad_in, stress_in, vel, conn, grad, stress)
    for copy in halo:
        copy.wait()
    vel[pl.ds(0, 5, stride=EXT), :] = vel_in[0]
    vel[pl.ds(ROWS + 1, 5, stride=EXT), :] = vel_in[1]
    elements(vel, conn, grad, area_ref, thick_ref, limit_ref, stress, spread)
    leave = [
        pltpu.make_async_copy(src, dst, out_sem.at[i])
        for i, (src, dst) in enumerate(((stress, cells_hbm), (total, total_hbm)))
    ]
    leave[0].start()
    for copy in ghosts:
        copy.wait()
    faces[:, 0:GHOST] = jnp.where(me > 0, ghost_in[0], 0.0)
    faces[:, GHOST + FACE_DEV :] = jnp.where(me < DEVICES - 1, ghost_in[1], 0.0)
    face_tables(faces, forms, pick, normals)
    nodes_move.wait()

    tiles = coming.reshape(DEVICES, 8, 128)

    def pair_step(b, _):
        first = b * PAIR_STEP
        forces = []
        for i in range(PAIR_STEP):
            x, f = tiles[node_ref[first + i]], face_of_ref[first + i]
            forces.append(pair_force(x, forms[f], lambda c, k, f=f: normals[f, c, k : k + 8]))
        for i, force in enumerate(forces):
            for c in range(3):
                pairs[pl.ds(c * PAIRS + first + i, 1), :] = force[c]
        return 0

    lax.fori_loop(0, PAIRS // PAIR_STEP, pair_step, 0)
    slot = lax.broadcasted_iota(jnp.int32, (1, PAIRS), 1)
    listed = onehot(DEVICES, jnp.where(slot < count_ref[...], node_row_ref[...], -1))
    listed = jnp.concatenate([listed] * 3, axis=1)
    leaving[...] = jnp.zeros_like(leaving)
    for c in range(3):
        parts = jnp.concatenate(split(pairs[c * PAIRS : (c + 1) * PAIRS, :], 3), axis=0)
        leaving[pl.ds(c, DEVICES, stride=8), :] = dot(listed, parts, NN)
    forces_move = exchange(1, leaving, back, 3)

    sum_ref[...] = jnp.zeros_like(sum_ref)
    last = NODE_DEV // 256 - 1
    scatter_blocks([0, last, *range(1, SPREAD_STEP - 1)], conn_in, spread, sum_ref)
    rims = edges(
        2, sum_ref.at[:, 0:HALO], sum_ref.at[:, HALO + NODE_DEV : 2 * HALO + NODE_DEV], rim_in
    )

    def scatter_step(b, _):
        first = b * SPREAD_STEP - 1
        scatter_blocks([first + i for i in range(SPREAD_STEP)], conn_in, spread, sum_ref)
        return 0

    lax.fori_loop(1, NODE_DEV // (256 * SPREAD_STEP), scatter_step, 0)
    for copy in rims:
        copy.wait()
    sum_ref[:, HALO : 2 * HALO] += rim_in[0]
    sum_ref[:, NODE_DEV : NODE_DEV + HALO] += rim_in[1]
    forces_move.wait()
    totals(back, owner_ref, rank_ref, sum_ref, total, side)
    leave[1].start()
    for copy in leave:
        copy.wait()


def totals(back_ref, owner_ref, rank_ref, sum_ref, out_ref, side):
    for c in range(3):
        turned = back_ref[pl.ds(c, DEVICES, stride=8), :].T
        for i, part in enumerate(split(turned, 2)):
            side[128 * c : 128 * c + 128, 128 * i : 128 * i + 128] = part

    def block(b):
        at = lane_aligned(b, 256)
        own = onehot(DEVICES, owner_ref[0:1, at])
        found = dot(side[...], jnp.concatenate([own, own], axis=0), NN)
        rank = rank_ref[0:1, at].astype(jnp.int32)
        mine = lax.broadcasted_iota(jnp.int32, (128, 256), 0) == rank
        contact = [
            jnp.sum(jnp.where(mine, found[128 * c : 128 * c + 128], 0.0), axis=0, keepdims=True)
            for c in range(3)
        ]
        contact = jnp.concatenate([*contact, jnp.zeros((2, 256), F32)], axis=0)
        return contact - sum_ref[0:5, pl.ds(pl.multiple_of(b * 256 + HALO, HALO), 256)]

    def step(b, _):
        done = [block(b * FINISH_STEP + i) for i in range(FINISH_STEP)]
        for i, value in enumerate(done):
            out_ref[:, lane_aligned(b * FINISH_STEP + i, 256)] = value
        return 0

    lax.fori_loop(0, NODE_DEV // (256 * FINISH_STEP), step, 0)


def finish_kernel(
    total_hbm, vel_hbm, mass_hbm, cells_hbm, out_hbm, new_hbm, total, vel, mass, cells, out, new,
    in_sem, out_sem,
):
    size = 5 * ROWS
    moves = [(total_hbm, total), (vel_hbm, vel), (mass_hbm, mass)]
    moves += [
        (cells_hbm.at[pl.ds(i * size, size)], cells.at[pl.ds(i * size, size)]) for i in range(5)
    ]
    inside = [pltpu.make_async_copy(*move, in_sem.at[i]) for i, move in enumerate(moves)]
    for copy in inside:
        copy.start()
    for copy in inside[:3]:
        copy.wait()
    out[...] = vel[...] + mass[...] * total[...]
    outside = [pltpu.make_async_copy(out, out_hbm, out_sem.at[5])]
    outside[0].start()
    for layer in range(5):
        inside[3 + layer].wait()
        for j in range(ROWS):
            part = cells[pl.ds(layer * size + j, 5, stride=ROWS), :]
            new[layer, :, 128 * j : 128 * j + 128] = part
        copy = pltpu.make_async_copy(new.at[layer], new_hbm.at[layer], out_sem.at[layer])
        copy.start()
        outside.append(copy)
    for copy in outside:
        copy.wait()


def body(
    velocity, position, inv_mass, connectivity, shape_grad, area, thickness, yield_stress, stress,
    contact_owner, face_center, face_angle, face_stiffness, ghost_list, pair_node, pair_face,
    pair_count,
):
    square = (ROWS, 128)
    owner = contact_owner.reshape(1, NODE_DEV)
    hbm = pl.BlockSpec(memory_space=pltpu.HBM)
    args = (
        owner, position, velocity, face_center, face_angle, face_stiffness.reshape(1, FACE_DEV),
        ghost_list.reshape(1, 2 * GHOST), connectivity, shape_grad, stress, area.reshape(square),
        thickness.reshape(square), yield_stress.reshape(square), pair_node, pair_face,
        pair_node.reshape(1, PAIRS), pair_count.reshape(1, 1),
    )
    held = [
        (pltpu.SMEM if len(arg.shape) == 1 else pltpu.VMEM)(arg.shape, arg.dtype) for arg in args
    ]
    dma = pltpu.SemaphoreType.DMA
    scratch = [
        ((DEVICES * 8, 128), F32), ((8, NODE_DEV + 2 * HALO), F32), ((1, NODE_DEV), F32),
        ((25 * ROWS, 128), F32), ((5, NODE_DEV), F32), ((3 * 128, 256), BF),
        ((DEVICES, 128), F32), ((448, 256), F32), ((256, 384), BF),
        ((DEVICES * 8, 128), F32), ((DEVICES * 8, 128), F32), ((FACE_DEV // 64, 128), F32),
        ((FACE_DEV // 16, 128), F32), ((8, FACE_TILES * 128), F32), ((8, 2 * GHOST), F32),
        ((2, 8, GHOST), F32), ((2, 5, HALO), F32), ((5 * EXT, 128), F32),
        ((4 * ROWS, 128), jnp.int32), ((8 * ROWS, 128), F32), ((4, 8 * ROWS, 128), F32),
        ((2, 8, HALO), F32), ((FACE_TILES, 3 * TILE, 48), BF), ((24, 3 * TILE), BF),
        ((FACE_TILES, 3, TILE, TILE), F32), ((3 * PAIRS, 128), F32), ((DEVICES * 8, 128), F32),
    ]
    total, cells = pl.pallas_call(
        step_kernel,
        out_shape=(
            jax.ShapeDtypeStruct((5, NODE_DEV), F32),
            jax.ShapeDtypeStruct((25 * ROWS, 128), F32),
        ),
        in_specs=[hbm] * len(args),
        out_specs=(hbm, hbm),
        scratch_shapes=[
            *held,
            *(pltpu.VMEM(shape, kind) for shape, kind in scratch),
            dma((len(args),)), dma((2,)), dma((2,)), dma((2,)), dma((3, 2)), dma((3, 2)),
        ],
        compiler_params=pltpu.CompilerParams(
            vmem_limit_bytes=56 * 2**20, collective_id=0, has_side_effects=True
        ),
        name="crash_step",
    )(*args)
    last = (total, velocity, inv_mass.reshape(1, NODE_DEV), cells)
    results = (
        jax.ShapeDtypeStruct((5, NODE_DEV), F32),
        jax.ShapeDtypeStruct((5, 5, NODE_DEV), F32),
    )
    return pl.pallas_call(
        finish_kernel,
        out_shape=results,
        in_specs=[hbm] * len(last),
        out_specs=(hbm, hbm),
        scratch_shapes=[
            *(pltpu.VMEM(x.shape, x.dtype) for x in (*last, *results)), dma((8,)), dma((6,)),
        ],
        compiler_params=pltpu.CompilerParams(vmem_limit_bytes=56 * 2**20),
        name="finish",
    )(*last)


def solution(mesh):
    axes = ("dom", "sub")
    nodes, rows, cells = P(axes), P(None, axes), P(None, None, axes)
    in_specs = (
        rows, rows, nodes, rows, cells, nodes, nodes, nodes, cells, P(axes, None), rows, rows,
        nodes, nodes, nodes, nodes, nodes,
    )
    return jax.shard_map(
        body, mesh=mesh, in_specs=in_specs, out_specs=(rows, cells), check_vma=False
    )
```

```python
import itertools

import jax
import jax.numpy as jnp
from jax import lax
from jax.experimental import pallas as pl
from jax.experimental.pallas import tpu as pltpu
from jax.sharding import PartitionSpec as P

TILE = 128
HALO = 128
GHOST = 256
NODE_DEV = 8192
ROWS = NODE_DEV // 128
FACE_DEV = 2048
FACE_TILES = 20
DEVICES = 128
PAIRS = 128
EXT = ROWS + 8

LOBATTO_POINTS = (-1.0, -0.6546536707079771, 0.0, 0.6546536707079771, 1.0)
LOBATTO_WEIGHTS = (0.1, 49.0 / 90.0, 32.0 / 45.0, 49.0 / 90.0, 0.1)
PLANE_MODULUS = 1.0 / 0.91
POISSON = 0.3
SHEAR_MODULUS = 5.0 / 6.0 / 2.6
DAMPING = 0.3
REACH_SQ = 0.5
LOG2E = 1.4426950408889634

BF = jnp.bfloat16
F32 = jnp.float32
NT = (((1,), (1,)), ((), ()))
NN = (((1,), (0,)), ((), ()))


def dot(a, b, dims):
    return lax.dot_general(a, b, dims, preferred_element_type=F32)


def onehot(count, row):
    where = lax.broadcasted_iota(jnp.int32, (count, row.shape[1]), 0)
    return jnp.where(where == row, 1.0, 0.0).astype(BF)


def split(x, parts):
    out = []
    for _ in range(parts - 1):
        head = x.astype(BF)
        out.append(head)
        x = x - head.astype(F32)
    out.append(x.astype(BF))
    return out


def lane_aligned(x, size):
    return pl.ds(pl.multiple_of(x * size, size), size)


MESH = pl.DeviceIdType.MESH
RANK_STEP, PLACE_STEP, SPREAD_STEP, FACE_STEP, PAIR_STEP, FINISH_STEP = 16, 4, 8, 10, 16, 8
PARTS = (2, 2, 2, 2, 2, 2, 1)


def constitutive(corner, grad_x, grad_y, area, thickness, limit, old):
    def over(f):
        total = f(0)
        for a in range(1, 4):
            total = total + f(a)
        return total

    vx, vy, vz, rx, ry = corner
    memb_xx = over(lambda a: grad_x[a] * vx[a])
    bend_xx = over(lambda a: grad_x[a] * ry[a])
    memb_yy = over(lambda a: grad_y[a] * vy[a])
    bend_yy = -over(lambda a: grad_y[a] * rx[a])
    memb_xy = over(lambda a: grad_y[a] * vx[a] + grad_x[a] * vy[a])
    bend_xy = over(lambda a: grad_y[a] * ry[a] - grad_x[a] * rx[a])
    shear_xz = over(lambda a: grad_x[a] * vz[a]) + 0.25 * over(lambda a: ry[a])
    shear_yz = over(lambda a: grad_y[a] * vz[a]) - 0.25 * over(lambda a: rx[a])
    add_xz, add_yz = SHEAR_MODULUS * shear_xz, SHEAR_MODULUS * shear_yz
    half = 0.5 * thickness
    volume = half * area
    new, force, moment = [], [0.0] * 5, [0.0] * 3
    for layer in range(5):
        height = half * LOBATTO_POINTS[layer]
        exx = memb_xx + height * bend_xx
        eyy = memb_yy + height * bend_yy
        exy = memb_xy + height * bend_xy
        t0 = old(layer, 0) + PLANE_MODULUS * (exx + POISSON * eyy)
        t1 = old(layer, 1) + PLANE_MODULUS * (eyy + POISSON * exx)
        t2 = old(layer, 2) + PLANE_MODULUS * 0.5 * (1.0 - POISSON) * exy
        t3 = old(layer, 3) + add_xz
        t4 = old(layer, 4) + add_yz
        plus, minus = t0 + t1, t0 - t1
        mises = jnp.sqrt(
            0.25 * (plus * plus) + 0.75 * (minus * minus) + 3.0 * (t2 * t2 + t3 * t3 + t4 * t4)
        )
        factor = limit / jnp.maximum(mises, limit)
        updated = [t * factor for t in (t0, t1, t2, t3, t4)]
        new.append(updated)
        weight = LOBATTO_WEIGHTS[layer] * volume
        weighted = [weight * u for u in updated]
        force = [f + w for f, w in zip(force, weighted)]
        moment = [m + height * w for m, w in zip(moment, weighted)]
    corners = []
    for a in range(4):
        gx, gy = grad_x[a], grad_y[a]
        corners.append(
            [
                gx * force[0] + gy * force[2],
                gy * force[1] + gx * force[2],
                gx * force[3] + gy * force[4],
                -(gy * moment[1] + gx * moment[2]) - 0.25 * force[4],
                gx * moment[0] + gy * moment[2] + 0.25 * force[3],
            ]
        )
    return new, corners


def ranks(owner_ref, rank_ref, run, tri):
    row = lax.broadcasted_iota(jnp.int32, (256, 384), 0)
    column = lax.broadcasted_iota(jnp.int32, (256, 384), 1)
    tri[...] = jnp.where((row < column) | (column >= 256), 1.0, 0.0).astype(BF)
    run[...] = jnp.zeros_like(run)

    def step(b, _):
        spans = [lane_aligned(b * RANK_STEP + i, 256) for i in range(RANK_STEP)]
        where = lax.broadcasted_iota(jnp.int32, (DEVICES, 256), 0)
        hot = [jnp.where(where == owner_ref[0:1, at], 1.0, 0.0) for at in spans]
        counts = dot(jnp.concatenate([h.astype(BF) for h in hot], axis=0), tri[...], NN)
        base = run[...]
        for i, at in enumerate(spans):
            count = counts[DEVICES * i : DEVICES * i + DEVICES]
            seen = count[:, :256] + jnp.concatenate([base, base], axis=1)
            rank_ref[0:1, at] = jnp.sum(hot[i] * seen, axis=0, keepdims=True)
            base = base + count[:, 256:]
        run[...] = base
        return 0

    lax.fori_loop(0, NODE_DEV // (256 * RANK_STEP), step, 0)


def place(owner_ref, rank_ref, pos_ref, vel_ref, out_ref, acc):
    acc[...] = jnp.zeros_like(acc)

    def block(b):
        at = lane_aligned(b, 1024)
        own = owner_ref[0:1, at]
        hot = onehot(256, (own & 1) * 128 + rank_ref[0:1, at].astype(jnp.int32))
        group = onehot(64, own >> 1)
        rows = []
        for c in range(6):
            value = pos_ref[c : c + 1, at] if c < 3 else vel_ref[c - 3 : c - 2, at]
            rows += [group * part for part in split(value, PARTS[c])]
        return dot(jnp.concatenate([*rows, group], axis=0), hot, NT)

    def step(b, _):
        placed = [block(b * PLACE_STEP + i) for i in range(PLACE_STEP)]
        first = 0
        for c, parts in enumerate(PARTS):
            total = acc[c * 64 : c * 64 + 64, :]
            for _ in range(parts):
                for p in placed:
                    total = total + p[first : first + 64]
                first += 64
            acc[c * 64 : c * 64 + 64, :] = total
        return 0

    lax.fori_loop(0, NODE_DEV // (1024 * PLACE_STEP), step, 0)
    for first in range(0, 64, 8):
        for low in range(2):
            for c in range(8):
                if c < 7:
                    part = acc[c * 64 + first : c * 64 + first + 8, low * 128 : low * 128 + 128]
                else:
                    part = jnp.ones((8, 128), F32)
                out_ref[pl.ds(first * 16 + low * 8 + c, 8, stride=16), :] = part


def face_rows(center_ref, angle_ref, stiff_ref, angles, normals, out_ref):
    tiles = FACE_DEV // 128
    for j in range(tiles):
        angles[pl.ds(j, 2, stride=tiles), :] = angle_ref[:, 128 * j : 128 * j + 128]
    azimuth, elevation = angles[0:tiles, :], angles[tiles : 2 * tiles, :]
    flat = jnp.cos(elevation)
    for c, value in enumerate(
        (jnp.cos(azimuth) * flat, jnp.sin(azimuth) * flat, jnp.sin(elevation))
    ):
        normals[pl.ds(c, tiles, stride=8), :] = value
    for j in range(tiles):
        at = slice(128 * j, 128 * j + 128)
        out_ref[:, GHOST + 128 * j : GHOST + 128 * j + 128] = jnp.concatenate(
            [center_ref[:, at], normals[8 * j : 8 * j + 3, :], stiff_ref[:, at], jnp.zeros((1, 128), F32)],
            axis=0,
        )


def lend(list_ref, faces_ref, out_ref):
    for g in range(2 * GHOST // 128):
        index = jnp.broadcast_to(list_ref[:, 128 * g : 128 * g + 128], (8, 128))
        low, high = index & 127, index >> 7
        found = jnp.zeros((8, 128), F32)
        for t in range(FACE_DEV // 128):
            at = slice(GHOST + 128 * t, GHOST + 128 * t + 128)
            part = jnp.take_along_axis(faces_ref[:, at], low, axis=1)
            found = jnp.where(high == t, part, found)
        out_ref[:, 128 * g : 128 * g + 128] = found


def unpack(vel_ref, conn_ref, grad_ref, stress_ref, vel, conn, grad, stress):
    def step(j, _):
        at = lane_aligned(j, 128)
        vel[pl.ds(j + 1, 5, stride=EXT), :] = vel_ref[:, at]
        conn[pl.ds(j, 4, stride=ROWS), :] = conn_ref[:, at] - 128 * j
        for axis in range(2):
            grad[pl.ds(axis * 4 * ROWS + j, 4, stride=ROWS), :] = grad_ref[axis, :, at]
        for layer in range(5):
            stress[pl.ds(layer * 5 * ROWS + j, 5, stride=ROWS), :] = stress_ref[layer, :, at]
        return 0

    lax.fori_loop(0, ROWS, step, 0, unroll=8)


def elements(vel, conn, grad, area_ref, thick_ref, limit_ref, stress, spread):
    spread[...] = jnp.zeros_like(spread)

    def group(g, _):
        def rows(field):
            return pl.ds(pl.multiple_of(field * ROWS + 8 * g, 8), 8)

        here = pl.ds(pl.multiple_of(8 * g, 8), 8)
        index = [conn[rows(a), :] for a in range(4)]
        low = [i & 127 for i in index]
        part_of = [i >> 7 for i in index]
        corner = []
        for c in range(5):
            window = [vel[pl.ds(c * EXT + 8 * g + k, 8), :] for k in range(3)]
            values = []
            for a in range(4):
                got = [jnp.take_along_axis(w, low[a], axis=1) for w in window]
                values.append(
                    jnp.where(part_of[a] == 0, got[0], jnp.where(part_of[a] == 1, got[1], got[2]))
                )
            corner.append(values)
        grad_x = [grad[rows(a), :] for a in range(4)]
        grad_y = [grad[rows(4 + a), :] for a in range(4)]
        new, forces = constitutive(
            corner, grad_x, grad_y, area_ref[here, :], thick_ref[here, :], limit_ref[here, :],
            lambda layer, c: stress[rows(5 * layer + c), :],
        )
        for layer in range(5):
            for c in range(5):
                stress[rows(5 * layer + c), :] = new[layer][c]
        for a in range(4):
            for c in range(5):
                spread[a, pl.ds(64 * g + c, 8, stride=8), :] = forces[a][c]
        return 0

    lax.fori_loop(0, 8, group, 0)


def scatter(b, conn_ref, spread):
    at = lane_aligned(b, 256)
    index = jnp.concatenate([conn_ref[a : a + 1, at] for a in range(4)], axis=1) - 256 * b
    hot = onehot(128, index & 127)
    window = index >> 7
    value = jnp.concatenate(
        [spread[a, lane_aligned(2 * b + h, 8), :] for a in range(4) for h in range(2)], axis=1
    )
    parts = split(value, 2)
    rows = []
    for h in range(4):
        mine = jnp.where(window == h, 1.0, 0.0).astype(BF)
        rows += [part * mine for part in parts]
    found = dot(hot, jnp.concatenate(rows, axis=0), NT).T
    return [found[16 * h : 16 * h + 8] + found[16 * h + 8 : 16 * h + 16] for h in range(4)]


def scatter_blocks(blocks, conn_ref, spread, sum_ref):
    found = [scatter(b, conn_ref, spread) for b in blocks]
    for b, windows in zip(blocks, found):
        for h, window in enumerate(windows):
            sum_ref[:, lane_aligned(2 * b + h, 128)] += window


def six_terms(x):
    high, mid, low = (part.astype(F32) for part in split(x, 3))
    return jnp.concatenate([high, mid, high, mid, low, high], axis=0)


def face_tables(faces_ref, forms, pick, normals):
    row = lax.broadcasted_iota(jnp.int32, (24, 3 * TILE), 0)
    column = lax.broadcasted_iota(jnp.int32, (24, 3 * TILE), 1)
    pick[...] = jnp.where((row & 7) == (column >> 7), 1.0, 0.0).astype(BF)

    def tile(f):
        x = faces_ref[:, lane_aligned(f, TILE)]
        r, m = [x[i : i + 1] for i in range(3)], [x[i : i + 1] for i in range(3, 6)]
        apart = m[0] * r[0] + m[1] * r[1] + m[2] * r[2]
        square = r[0] * r[0] + r[1] * r[1] + r[2] * r[2]
        strength = x[6:7] * jnp.exp2((-LOG2E / REACH_SQ) * square)
        none = jnp.zeros_like(apart)
        depth = [*(-strength * v for v in m), none, none, none, none, strength * apart]
        along = [none, none, none, *(-DAMPING * v for v in m), none, jnp.ones_like(apart)]
        reach = [*((2.0 / REACH_SQ * LOG2E) * v for v in r), none, none, none, none, none]
        terms = [six_terms(jnp.concatenate(form, axis=0)) for form in (depth, along, reach)]
        forms[f, 0:TILE, :] = jnp.concatenate(terms[:2], axis=0).T.astype(BF)
        forms[f, TILE : 2 * TILE, 0:48] = terms[2].T.astype(BF)
        parts = [part.astype(F32) for part in split(jnp.concatenate([*m] + [none] * 5, axis=0), 3)]
        wide = dot(jnp.concatenate(parts, axis=0).T.astype(BF), pick[...], NN)
        for i in range(3):
            normals[f, i] = wide[:, TILE * i : TILE * i + TILE]

    def step(b, _):
        for i in range(FACE_STEP):
            tile(b * FACE_STEP + i)
        return 0

    lax.fori_loop(0, FACE_TILES // FACE_STEP, step, 0)


def pair_force(x, form, normal_of):
    high, mid, low = split(x, 3)
    node = jnp.concatenate([high, high, mid, mid, high, low], axis=0)
    none = jnp.zeros_like(node)
    both = [jnp.concatenate(two, axis=1) for two in ((node, none), (none, node))]
    products = dot(form[0:TILE], jnp.concatenate(both, axis=0), NN)
    reach = dot(form[TILE : 2 * TILE, 0:48], node, NN)
    square = x[0:1] * x[0:1] + x[1:2] * x[1:2] + x[2:3] * x[2:3]
    scale = x[6:7] * jnp.exp2((-LOG2E / REACH_SQ) * square)
    total = [jnp.zeros((8, TILE), F32) for _ in range(3)]
    for k in range(0, TILE, 8):
        depth = jnp.maximum(products[k : k + 8, 0:TILE], 0.0)
        along = products[k : k + 8, TILE : 2 * TILE]
        size = depth * along * jnp.exp2(reach[k : k + 8])
        total = [t + size * normal_of(i, k) for i, t in enumerate(total)]
    return [scale * jnp.sum(t, axis=0, keepdims=True) for t in total]


def reach(offset):
    z, y, core, x = offset
    return sum(min(d, 4 - d) for d in (z, y, x)) + 0.5 * core


OFFSETS = sorted(itertools.product(range(4), range(4), range(2), range(4)), key=reach)[:0:-1]


def step_kernel(*refs):
    inputs, outputs, held, scratch = refs[:17], refs[17:19], refs[19:36], refs[36:]
    (
        owner_ref, pos_ref, vel_ref, center_ref, angle_ref, stiff_ref, list_ref, conn_in, grad_in,
        stress_in, area_ref, thick_ref, limit_ref, node_ref, face_of_ref, node_row_ref, count_ref,
    ) = held
    total_hbm, cells_hbm = outputs
    (
        back, sum_ref, rank_ref, stress, total, side, run, acc, tri, going, coming, angles, unit,
        faces, lent, ghost_in, vel_in, vel, conn, grad, spread, rim_in, forms, pick, normals, pairs,
        leaving, load_sem, out_sem, send_sem, recv_sem, edge_send, edge_recv,
    ) = scratch
    sub_count = lax.axis_size("sub")
    me = lax.axis_index("dom") * sub_count + lax.axis_index("sub")

    def device(k):
        to = lax.rem(me + k, DEVICES)
        return to, (lax.div(to, sub_count), lax.rem(to, sub_count))

    digits = (lax.div(me, 32), lax.rem(lax.div(me, 8), 4), lax.rem(lax.div(me, 4), 2), lax.rem(me, 4))

    def device_at(offset):
        z, y, core, x = (
            lax.rem(digit + step, size) for digit, step, size in zip(digits, offset, (4, 4, 2, 4))
        )
        group = (z * 4 + y) * 2 + core
        return group * 4 + x, (group, x)

    loads = [
        pltpu.make_async_copy(src, dst, load_sem.at[i])
        for i, (src, dst) in enumerate(zip(inputs, held))
    ]
    for copy in loads:
        copy.start()
    coming[pl.ds(7, DEVICES, stride=8), :] = jnp.ones((DEVICES, 128), F32)
    barrier = pltpu.get_barrier_semaphore()

    def greet(k, _):
        pl.semaphore_signal(barrier, inc=1, device_id=device(k)[1], device_id_type=MESH)
        return 0

    lax.fori_loop(1, DEVICES, greet, 0)
    for copy in loads[:3]:
        copy.wait()
    ranks(owner_ref, rank_ref, run, tri)
    place(owner_ref, rank_ref, pos_ref, vel_ref, going, acc)
    pl.semaphore_wait(barrier, DEVICES - 1)

    def edges(i, first, last, land):
        pair = []
        for end, (src, k) in enumerate(((last, 1), (first, DEVICES - 1))):
            copy = pltpu.make_async_remote_copy(
                src, land.at[end], edge_send.at[i, end], edge_recv.at[i, end],
                device_id=device(k)[1], device_id_type=MESH,
            )
            copy.start()
            pair.append(copy)
        return pair

    def tile(i):
        return pl.ds(pl.multiple_of(8 * i, 8), 8)

    def exchange(i, src, dst, rows):
        def part(t):
            return pl.ds(pl.multiple_of(8 * t, 8), rows)

        for offset in OFFSETS:
            to, where = device_at(offset)
            pltpu.make_async_remote_copy(
                src.at[part(to)], dst.at[part(me)], send_sem.at[i], recv_sem.at[i],
                device_id=where, device_id_type=MESH,
            ).start()

        dst[tile(me), :] = src[tile(me), :]
        others = pl.ds(0, (DEVICES - 1) * rows)
        return pltpu.make_async_remote_copy(
            src.at[others], dst.at[others], send_sem.at[i], recv_sem.at[i],
            device_id=device(1)[1], device_id_type=MESH,
        )

    halo = edges(0, vel_ref.at[:, 0:HALO], vel_ref.at[:, NODE_DEV - HALO : NODE_DEV], vel_in)
    nodes_move = exchange(0, going, coming, 7)
    for copy in loads[3:]:
        copy.wait()
    face_rows(center_ref, angle_ref, stiff_ref, angles, unit, faces)
    lend(list_ref, faces, lent)
    ghosts = edges(1, lent.at[:, 0:GHOST], lent.at[:, GHOST : 2 * GHOST], ghost_in)
    unpack(vel_ref, conn_in, grad_in, stress_in, vel, conn, grad, stress)
    for copy in halo:
        copy.wait()
    vel[pl.ds(0, 5, stride=EXT), :] = vel_in[0]
    vel[pl.ds(ROWS + 1, 5, stride=EXT), :] = vel_in[1]
    elements(vel, conn, grad, area_ref, thick_ref, limit_ref, stress, spread)
    leave = [
        pltpu.make_async_copy(src, dst, out_sem.at[i])
        for i, (src, dst) in enumerate(((stress, cells_hbm), (total, total_hbm)))
    ]
    leave[0].start()
    for copy in ghosts:
        copy.wait()
    faces[:, 0:GHOST] = jnp.where(me > 0, ghost_in[0], 0.0)
    faces[:, GHOST + FACE_DEV :] = jnp.where(me < DEVICES - 1, ghost_in[1], 0.0)
    face_tables(faces, forms, pick, normals)
    nodes_move.wait()

    tiles = coming.reshape(DEVICES, 8, 128)

    def pair_step(b, _):
        first = b * PAIR_STEP
        forces = []
        for i in range(PAIR_STEP):
            x, f = tiles[node_ref[first + i]], face_of_ref[first + i]
            forces.append(pair_force(x, forms[f], lambda c, k, f=f: normals[f, c, k : k + 8]))
        for i, force in enumerate(forces):
            for c in range(3):
                pairs[pl.ds(c * PAIRS + first + i, 1), :] = force[c]
        return 0

    lax.fori_loop(0, PAIRS // PAIR_STEP, pair_step, 0)
    slot = lax.broadcasted_iota(jnp.int32, (1, PAIRS), 1)
    listed = onehot(DEVICES, jnp.where(slot < count_ref[...], node_row_ref[...], -1))
    listed = jnp.concatenate([listed] * 3, axis=1)
    leaving[...] = jnp.zeros_like(leaving)
    for c in range(3):
        parts = jnp.concatenate(split(pairs[c * PAIRS : (c + 1) * PAIRS, :], 3), axis=0)
        leaving[pl.ds(c, DEVICES, stride=8), :] = dot(listed, parts, NN)
    forces_move = exchange(1, leaving, back, 3)

    sum_ref[...] = jnp.zeros_like(sum_ref)
    last = NODE_DEV // 256 - 1
    scatter_blocks([0, last, *range(1, SPREAD_STEP - 1)], conn_in, spread, sum_ref)
    rims = edges(
        2, sum_ref.at[:, 0:HALO], sum_ref.at[:, HALO + NODE_DEV : 2 * HALO + NODE_DEV], rim_in
    )

    def scatter_step(b, _):
        first = b * SPREAD_STEP - 1
        scatter_blocks([first + i for i in range(SPREAD_STEP)], conn_in, spread, sum_ref)
        return 0

    lax.fori_loop(1, NODE_DEV // (256 * SPREAD_STEP), scatter_step, 0)
    for copy in rims:
        copy.wait()
    sum_ref[:, HALO : 2 * HALO] += rim_in[0]
    sum_ref[:, NODE_DEV : NODE_DEV + HALO] += rim_in[1]
    forces_move.wait()
    totals(back, owner_ref, rank_ref, sum_ref, total, side)
    leave[1].start()
    for copy in leave:
        copy.wait()


def totals(back_ref, owner_ref, rank_ref, sum_ref, out_ref, side):
    for c in range(3):
        turned = back_ref[pl.ds(c, DEVICES, stride=8), :].T
        for i, part in enumerate(split(turned, 2)):
            side[128 * c : 128 * c + 128, 128 * i : 128 * i + 128] = part

    def block(b):
        at = lane_aligned(b, 256)
        own = onehot(DEVICES, owner_ref[0:1, at])
        found = dot(side[...], jnp.concatenate([own, own], axis=0), NN)
        rank = rank_ref[0:1, at].astype(jnp.int32)
        mine = lax.broadcasted_iota(jnp.int32, (128, 256), 0) == rank
        contact = [
            jnp.sum(jnp.where(mine, found[128 * c : 128 * c + 128], 0.0), axis=0, keepdims=True)
            for c in range(3)
        ]
        contact = jnp.concatenate([*contact, jnp.zeros((2, 256), F32)], axis=0)
        return contact - sum_ref[0:5, pl.ds(pl.multiple_of(b * 256 + HALO, HALO), 256)]

    def step(b, _):
        done = [block(b * FINISH_STEP + i) for i in range(FINISH_STEP)]
        for i, value in enumerate(done):
            out_ref[:, lane_aligned(b * FINISH_STEP + i, 256)] = value
        return 0

    lax.fori_loop(0, NODE_DEV // (256 * FINISH_STEP), step, 0)


def finish_kernel(
    total_hbm, vel_hbm, mass_hbm, cells_hbm, out_hbm, new_hbm, total, vel, mass, cells, out, new,
    in_sem, out_sem,
):
    size = 5 * ROWS
    moves = [(total_hbm, total), (vel_hbm, vel), (mass_hbm, mass)]
    moves += [
        (cells_hbm.at[pl.ds(i * size, size)], cells.at[pl.ds(i * size, size)]) for i in range(5)
    ]
    inside = [pltpu.make_async_copy(*move, in_sem.at[i]) for i, move in enumerate(moves)]
    for copy in inside:
        copy.start()
    for copy in inside[:3]:
        copy.wait()
    out[...] = vel[...] + mass[...] * total[...]
    outside = [pltpu.make_async_copy(out, out_hbm, out_sem.at[5])]
    outside[0].start()
    for layer in range(5):
        inside[3 + layer].wait()
        for j in range(ROWS):
            part = cells[pl.ds(layer * size + j, 5, stride=ROWS), :]
            new[layer, :, 128 * j : 128 * j + 128] = part
        copy = pltpu.make_async_copy(new.at[layer], new_hbm.at[layer], out_sem.at[layer])
        copy.start()
        outside.append(copy)
    for copy in outside:
        copy.wait()


def body(
    velocity, position, inv_mass, connectivity, shape_grad, area, thickness, yield_stress, stress,
    contact_owner, face_center, face_angle, face_stiffness, ghost_list, pair_node, pair_face,
    pair_count,
):
    square = (ROWS, 128)
    owner = contact_owner.reshape(1, NODE_DEV)
    hbm = pl.BlockSpec(memory_space=pltpu.HBM)
    args = (
        owner, position, velocity, face_center, face_angle, face_stiffness.reshape(1, FACE_DEV),
        ghost_list.reshape(1, 2 * GHOST), connectivity, shape_grad, stress, area.reshape(square),
        thickness.reshape(square), yield_stress.reshape(square), pair_node, pair_face,
        pair_node.reshape(1, PAIRS), pair_count.reshape(1, 1),
    )
    held = [
        (pltpu.SMEM if len(arg.shape) == 1 else pltpu.VMEM)(arg.shape, arg.dtype) for arg in args
    ]
    dma = pltpu.SemaphoreType.DMA
    scratch = [
        ((DEVICES * 8, 128), F32), ((8, NODE_DEV + 2 * HALO), F32), ((1, NODE_DEV), F32),
        ((25 * ROWS, 128), F32), ((5, NODE_DEV), F32), ((3 * 128, 256), BF),
        ((DEVICES, 128), F32), ((448, 256), F32), ((256, 384), BF),
        ((DEVICES * 8, 128), F32), ((DEVICES * 8, 128), F32), ((FACE_DEV // 64, 128), F32),
        ((FACE_DEV // 16, 128), F32), ((8, FACE_TILES * 128), F32), ((8, 2 * GHOST), F32),
        ((2, 8, GHOST), F32), ((2, 5, HALO), F32), ((5 * EXT, 128), F32),
        ((4 * ROWS, 128), jnp.int32), ((8 * ROWS, 128), F32), ((4, 8 * ROWS, 128), F32),
        ((2, 8, HALO), F32), ((FACE_TILES, 2 * TILE, 96), BF), ((24, 3 * TILE), BF),
        ((FACE_TILES, 3, TILE, TILE), F32), ((3 * PAIRS, 128), F32), ((DEVICES * 8, 128), F32),
    ]
    total, cells = pl.pallas_call(
        step_kernel,
        out_shape=(
            jax.ShapeDtypeStruct((5, NODE_DEV), F32),
            jax.ShapeDtypeStruct((25 * ROWS, 128), F32),
        ),
        in_specs=[hbm] * len(args),
        out_specs=(hbm, hbm),
        scratch_shapes=[
            *held,
            *(pltpu.VMEM(shape, kind) for shape, kind in scratch),
            dma((len(args),)), dma((2,)), dma((2,)), dma((2,)), dma((3, 2)), dma((3, 2)),
        ],
        compiler_params=pltpu.CompilerParams(
            vmem_limit_bytes=56 * 2**20, collective_id=0, has_side_effects=True
        ),
        name="crash_step",
    )(*args)
    last = (total, velocity, inv_mass.reshape(1, NODE_DEV), cells)
    results = (
        jax.ShapeDtypeStruct((5, NODE_DEV), F32),
        jax.ShapeDtypeStruct((5, 5, NODE_DEV), F32),
    )
    return pl.pallas_call(
        finish_kernel,
        out_shape=results,
        in_specs=[hbm] * len(last),
        out_specs=(hbm, hbm),
        scratch_shapes=[
            *(pltpu.VMEM(x.shape, x.dtype) for x in (*last, *results)), dma((8,)), dma((6,)),
        ],
        compiler_params=pltpu.CompilerParams(vmem_limit_bytes=56 * 2**20),
        name="finish",
    )(*last)


def solution(mesh):
    axes = ("dom", "sub")
    nodes, rows, cells = P(axes), P(None, axes), P(None, None, axes)
    in_specs = (
        rows, rows, nodes, rows, cells, nodes, nodes, nodes, cells, P(axes, None), rows, rows,
        nodes, nodes, nodes, nodes, nodes,
    )
    return jax.shard_map(
        body, mesh=mesh, in_specs=in_specs, out_specs=(rows, cells), check_vma=False
    )
```

```python
import itertools

import jax
import jax.numpy as jnp
from jax import lax
from jax.experimental import pallas as pl
from jax.experimental.pallas import tpu as pltpu
from jax.sharding import PartitionSpec as P

TILE = 128
HALO = 128
GHOST = 256
NODE_DEV = 8192
ROWS = NODE_DEV // 128
FACE_DEV = 2048
FACE_TILES = 20
DEVICES = 128
PAIRS = 128
EXT = ROWS + 8

LOBATTO_POINTS = (-1.0, -0.6546536707079771, 0.0, 0.6546536707079771, 1.0)
LOBATTO_WEIGHTS = (0.1, 49.0 / 90.0, 32.0 / 45.0, 49.0 / 90.0, 0.1)
PLANE_MODULUS = 1.0 / 0.91
POISSON = 0.3
SHEAR_MODULUS = 5.0 / 6.0 / 2.6
DAMPING = 0.3
REACH_SQ = 0.5
LOG2E = 1.4426950408889634

BF = jnp.bfloat16
F32 = jnp.float32
NT = (((1,), (1,)), ((), ()))
NN = (((1,), (0,)), ((), ()))


def dot(a, b, dims):
    return lax.dot_general(a, b, dims, preferred_element_type=F32)


def onehot(count, row):
    where = lax.broadcasted_iota(jnp.int32, (count, row.shape[1]), 0)
    return jnp.where(where == row, 1.0, 0.0).astype(BF)


def split(x, parts):
    out = []
    for _ in range(parts - 1):
        head = x.astype(BF)
        out.append(head)
        x = x - head.astype(F32)
    out.append(x.astype(BF))
    return out


def lane_aligned(x, size):
    return pl.ds(pl.multiple_of(x * size, size), size)


MESH = pl.DeviceIdType.MESH
RANK_STEP, PLACE_STEP, SPREAD_STEP, FACE_STEP, PAIR_STEP, FINISH_STEP = 16, 4, 8, 10, 16, 8
PARTS = (2, 2, 2, 2, 2, 2, 1)


def constitutive(corner, grad_x, grad_y, area, thickness, limit, old):
    def over(f):
        total = f(0)
        for a in range(1, 4):
            total = total + f(a)
        return total

    vx, vy, vz, rx, ry = corner
    memb_xx = over(lambda a: grad_x[a] * vx[a])
    bend_xx = over(lambda a: grad_x[a] * ry[a])
    memb_yy = over(lambda a: grad_y[a] * vy[a])
    bend_yy = -over(lambda a: grad_y[a] * rx[a])
    memb_xy = over(lambda a: grad_y[a] * vx[a] + grad_x[a] * vy[a])
    bend_xy = over(lambda a: grad_y[a] * ry[a] - grad_x[a] * rx[a])
    shear_xz = over(lambda a: grad_x[a] * vz[a]) + 0.25 * over(lambda a: ry[a])
    shear_yz = over(lambda a: grad_y[a] * vz[a]) - 0.25 * over(lambda a: rx[a])
    add_xz, add_yz = SHEAR_MODULUS * shear_xz, SHEAR_MODULUS * shear_yz
    half = 0.5 * thickness
    volume = half * area
    new, force, moment = [], [0.0] * 5, [0.0] * 3
    for layer in range(5):
        height = half * LOBATTO_POINTS[layer]
        exx = memb_xx + height * bend_xx
        eyy = memb_yy + height * bend_yy
        exy = memb_xy + height * bend_xy
        t0 = old(layer, 0) + PLANE_MODULUS * (exx + POISSON * eyy)
        t1 = old(layer, 1) + PLANE_MODULUS * (eyy + POISSON * exx)
        t2 = old(layer, 2) + PLANE_MODULUS * 0.5 * (1.0 - POISSON) * exy
        t3 = old(layer, 3) + add_xz
        t4 = old(layer, 4) + add_yz
        plus, minus = t0 + t1, t0 - t1
        mises = jnp.sqrt(
            0.25 * (plus * plus) + 0.75 * (minus * minus) + 3.0 * (t2 * t2 + t3 * t3 + t4 * t4)
        )
        factor = limit / jnp.maximum(mises, limit)
        updated = [t * factor for t in (t0, t1, t2, t3, t4)]
        new.append(updated)
        weight = LOBATTO_WEIGHTS[layer] * volume
        weighted = [weight * u for u in updated]
        force = [f + w for f, w in zip(force, weighted)]
        moment = [m + height * w for m, w in zip(moment, weighted)]
    corners = []
    for a in range(4):
        gx, gy = grad_x[a], grad_y[a]
        corners.append(
            [
                gx * force[0] + gy * force[2],
                gy * force[1] + gx * force[2],
                gx * force[3] + gy * force[4],
                -(gy * moment[1] + gx * moment[2]) - 0.25 * force[4],
                gx * moment[0] + gy * moment[2] + 0.25 * force[3],
            ]
        )
    return new, corners


def ranks(owner_ref, rank_ref, run, tri):
    row = lax.broadcasted_iota(jnp.int32, (256, 384), 0)
    column = lax.broadcasted_iota(jnp.int32, (256, 384), 1)
    tri[...] = jnp.where((row < column) | (column >= 256), 1.0, 0.0).astype(BF)
    run[...] = jnp.zeros_like(run)

    def step(b, _):
        spans = [lane_aligned(b * RANK_STEP + i, 256) for i in range(RANK_STEP)]
        where = lax.broadcasted_iota(jnp.int32, (DEVICES, 256), 0)
        hot = [jnp.where(where == owner_ref[0:1, at], 1.0, 0.0) for at in spans]
        counts = dot(jnp.concatenate([h.astype(BF) for h in hot], axis=0), tri[...], NN)
        base = run[...]
        for i, at in enumerate(spans):
            count = counts[DEVICES * i : DEVICES * i + DEVICES]
            seen = count[:, :256] + jnp.concatenate([base, base], axis=1)
            rank_ref[0:1, at] = jnp.sum(hot[i] * seen, axis=0, keepdims=True)
            base = base + count[:, 256:]
        run[...] = base
        return 0

    lax.fori_loop(0, NODE_DEV // (256 * RANK_STEP), step, 0)


def place(owner_ref, rank_ref, pos_ref, vel_ref, out_ref, acc):
    acc[...] = jnp.zeros_like(acc)

    def block(b):
        at = lane_aligned(b, 1024)
        own = owner_ref[0:1, at]
        hot = onehot(256, (own & 1) * 128 + rank_ref[0:1, at].astype(jnp.int32))
        group = onehot(64, own >> 1)
        rows = []
        for c in range(6):
            value = pos_ref[c : c + 1, at] if c < 3 else vel_ref[c - 3 : c - 2, at]
            rows += [group * part for part in split(value, PARTS[c])]
        return dot(jnp.concatenate([*rows, group], axis=0), hot, NT)

    def step(b, _):
        placed = [block(b * PLACE_STEP + i) for i in range(PLACE_STEP)]
        first = 0
        for c, parts in enumerate(PARTS):
            total = acc[c * 64 : c * 64 + 64, :]
            for _ in range(parts):
                for p in placed:
                    total = total + p[first : first + 64]
                first += 64
            acc[c * 64 : c * 64 + 64, :] = total
        return 0

    lax.fori_loop(0, NODE_DEV // (1024 * PLACE_STEP), step, 0)
    for first in range(0, 64, 8):
        for low in range(2):
            for c in range(8):
                if c < 7:
                    part = acc[c * 64 + first : c * 64 + first + 8, low * 128 : low * 128 + 128]
                else:
                    part = jnp.ones((8, 128), F32)
                out_ref[pl.ds(first * 16 + low * 8 + c, 8, stride=16), :] = part


def face_rows(center_ref, angle_ref, stiff_ref, angles, normals, out_ref):
    tiles = FACE_DEV // 128
    for j in range(tiles):
        angles[pl.ds(j, 2, stride=tiles), :] = angle_ref[:, 128 * j : 128 * j + 128]
    azimuth, elevation = angles[0:tiles, :], angles[tiles : 2 * tiles, :]
    flat = jnp.cos(elevation)
    for c, value in enumerate(
        (jnp.cos(azimuth) * flat, jnp.sin(azimuth) * flat, jnp.sin(elevation))
    ):
        normals[pl.ds(c, tiles, stride=8), :] = value
    for j in range(tiles):
        at = slice(128 * j, 128 * j + 128)
        out_ref[:, GHOST + 128 * j : GHOST + 128 * j + 128] = jnp.concatenate(
            [center_ref[:, at], normals[8 * j : 8 * j + 3, :], stiff_ref[:, at], jnp.zeros((1, 128), F32)],
            axis=0,
        )


def lend(list_ref, faces_ref, out_ref):
    for g in range(2 * GHOST // 128):
        index = jnp.broadcast_to(list_ref[:, 128 * g : 128 * g + 128], (8, 128))
        low, high = index & 127, index >> 7
        found = jnp.zeros((8, 128), F32)
        for t in range(FACE_DEV // 128):
            at = slice(GHOST + 128 * t, GHOST + 128 * t + 128)
            part = jnp.take_along_axis(faces_ref[:, at], low, axis=1)
            found = jnp.where(high == t, part, found)
        out_ref[:, 128 * g : 128 * g + 128] = found


def unpack(vel_ref, conn_ref, grad_ref, stress_ref, vel, conn, grad, stress):
    def step(j, _):
        at = lane_aligned(j, 128)
        vel[pl.ds(j + 1, 5, stride=EXT), :] = vel_ref[:, at]
        conn[pl.ds(j, 4, stride=ROWS), :] = conn_ref[:, at] - 128 * j
        for axis in range(2):
            grad[pl.ds(axis * 4 * ROWS + j, 4, stride=ROWS), :] = grad_ref[axis, :, at]
        for layer in range(5):
            stress[pl.ds(layer * 5 * ROWS + j, 5, stride=ROWS), :] = stress_ref[layer, :, at]
        return 0

    lax.fori_loop(0, ROWS, step, 0, unroll=8)


def elements(vel, conn, grad, area_ref, thick_ref, limit_ref, stress, spread):
    spread[...] = jnp.zeros_like(spread)

    def group(g, _):
        def rows(field):
            return pl.ds(pl.multiple_of(field * ROWS + 8 * g, 8), 8)

        here = pl.ds(pl.multiple_of(8 * g, 8), 8)
        index = [conn[rows(a), :] for a in range(4)]
        low = [i & 127 for i in index]
        part_of = [i >> 7 for i in index]
        corner = []
        for c in range(5):
            window = [vel[pl.ds(c * EXT + 8 * g + k, 8), :] for k in range(3)]
            values = []
            for a in range(4):
                got = [jnp.take_along_axis(w, low[a], axis=1) for w in window]
                values.append(
                    jnp.where(part_of[a] == 0, got[0], jnp.where(part_of[a] == 1, got[1], got[2]))
                )
            corner.append(values)
        grad_x = [grad[rows(a), :] for a in range(4)]
        grad_y = [grad[rows(4 + a), :] for a in range(4)]
        new, forces = constitutive(
            corner, grad_x, grad_y, area_ref[here, :], thick_ref[here, :], limit_ref[here, :],
            lambda layer, c: stress[rows(5 * layer + c), :],
        )
        for layer in range(5):
            for c in range(5):
                stress[rows(5 * layer + c), :] = new[layer][c]
        for a in range(4):
            for c in range(5):
                spread[a, pl.ds(64 * g + c, 8, stride=8), :] = forces[a][c]
        return 0

    lax.fori_loop(0, 8, group, 0)


def scatter(b, conn_ref, spread):
    at = lane_aligned(b, 256)
    index = jnp.concatenate([conn_ref[a : a + 1, at] for a in range(4)], axis=1) - 256 * b
    hot = onehot(128, index & 127)
    window = index >> 7
    value = jnp.concatenate(
        [spread[a, lane_aligned(2 * b + h, 8), :] for a in range(4) for h in range(2)], axis=1
    )
    parts = split(value, 2)
    rows = []
    for h in range(4):
        mine = jnp.where(window == h, 1.0, 0.0).astype(BF)
        rows += [part * mine for part in parts]
    found = dot(hot, jnp.concatenate(rows, axis=0), NT).T
    return [found[16 * h : 16 * h + 8] + found[16 * h + 8 : 16 * h + 16] for h in range(4)]


def scatter_blocks(blocks, conn_ref, spread, sum_ref):
    found = [scatter(b, conn_ref, spread) for b in blocks]
    for b, windows in zip(blocks, found):
        for h, window in enumerate(windows):
            sum_ref[:, lane_aligned(2 * b + h, 128)] += window


def six_terms(x):
    high, mid, low = (part.astype(F32) for part in split(x, 3))
    return jnp.concatenate([high, mid, high, mid, low, high], axis=0)


def face_tables(faces_ref, forms, pick, normals):
    row = lax.broadcasted_iota(jnp.int32, (24, 3 * TILE), 0)
    column = lax.broadcasted_iota(jnp.int32, (24, 3 * TILE), 1)
    pick[...] = jnp.where((row & 7) == (column >> 7), 1.0, 0.0).astype(BF)

    def tile(f):
        x = faces_ref[:, lane_aligned(f, TILE)]
        r, m = [x[i : i + 1] for i in range(3)], [x[i : i + 1] for i in range(3, 6)]
        apart = m[0] * r[0] + m[1] * r[1] + m[2] * r[2]
        square = r[0] * r[0] + r[1] * r[1] + r[2] * r[2]
        strength = x[6:7] * jnp.exp2((-LOG2E / REACH_SQ) * square)
        none = jnp.zeros_like(apart)
        depth = [*(-strength * v for v in m), none, none, none, none, strength * apart]
        along = [none, none, none, *(-DAMPING * v for v in m), none, jnp.ones_like(apart)]
        reach = [*((2.0 / REACH_SQ * LOG2E) * v for v in r), none, none, none, none, none]
        terms = [six_terms(jnp.concatenate(form, axis=0)) for form in (depth, along, reach)]
        forms[f, 0:TILE, :] = jnp.concatenate(terms[:2], axis=0).T.astype(BF)
        forms[f, TILE : 2 * TILE, 0:48] = terms[2].T.astype(BF)
        parts = [part.astype(F32) for part in split(jnp.concatenate([*m] + [none] * 5, axis=0), 3)]
        wide = dot(jnp.concatenate(parts, axis=0).T.astype(BF), pick[...], NN)
        for i in range(3):
            normals[f, i] = wide[:, TILE * i : TILE * i + TILE]

    def step(b, _):
        for i in range(FACE_STEP):
            tile(b * FACE_STEP + i)
        return 0

    lax.fori_loop(0, FACE_TILES // FACE_STEP, step, 0)


def pair_force(x, form, normal_of):
    high, mid, low = split(x, 3)
    node = jnp.concatenate([high, high, mid, mid, high, low], axis=0)
    none = jnp.zeros_like(node)
    both = [jnp.concatenate(two, axis=1) for two in ((node, none), (none, node))]
    products = dot(form[0:TILE], jnp.concatenate(both, axis=0), NN)
    reach = dot(form[TILE : 2 * TILE, 0:48], node, NN)
    square = x[0:1] * x[0:1] + x[1:2] * x[1:2] + x[2:3] * x[2:3]
    scale = x[6:7] * jnp.exp2((-LOG2E / REACH_SQ) * square)
    total = [jnp.zeros((8, TILE), F32) for _ in range(3)]
    for k in range(0, TILE, 8):
        depth = jnp.maximum(products[k : k + 8, 0:TILE], 0.0)
        along = products[k : k + 8, TILE : 2 * TILE]
        size = depth * along * jnp.exp2(reach[k : k + 8])
        total = [t + size * normal_of(i, k) for i, t in enumerate(total)]
    return [scale * jnp.sum(t, axis=0, keepdims=True) for t in total]


def reach(offset):
    z, y, core, x = offset
    return sum(min(d, 4 - d) for d in (z, y, x)) + 0.5 * core


OFFSETS = sorted(itertools.product(range(4), range(4), range(2), range(4)), key=reach)[:0:-1]


def step_kernel(*refs):
    inputs, outputs, held, scratch = refs[:17], refs[17:19], refs[19:36], refs[36:]
    (
        owner_ref, pos_ref, vel_ref, center_ref, angle_ref, stiff_ref, list_ref, conn_in, grad_in,
        stress_in, area_ref, thick_ref, limit_ref, node_ref, face_of_ref, node_row_ref, count_ref,
    ) = held
    total_hbm, cells_hbm = outputs
    (
        back, sum_ref, rank_ref, stress, total, side, hots, run, acc, tri, going, coming, angles, unit,
        faces, lent, ghost_in, vel_in, vel, conn, grad, spread, rim_in, forms, pick, normals, pairs,
        leaving, load_sem, out_sem, send_sem, recv_sem, edge_send, edge_recv,
    ) = scratch
    sub_count = lax.axis_size("sub")
    me = lax.axis_index("dom") * sub_count + lax.axis_index("sub")

    def device(k):
        to = lax.rem(me + k, DEVICES)
        return to, (lax.div(to, sub_count), lax.rem(to, sub_count))

    digits = (lax.div(me, 32), lax.rem(lax.div(me, 8), 4), lax.rem(lax.div(me, 4), 2), lax.rem(me, 4))

    def device_at(offset):
        z, y, core, x = (
            lax.rem(digit + step, size) for digit, step, size in zip(digits, offset, (4, 4, 2, 4))
        )
        group = (z * 4 + y) * 2 + core
        return group * 4 + x, (group, x)

    loads = [
        pltpu.make_async_copy(src, dst, load_sem.at[i])
        for i, (src, dst) in enumerate(zip(inputs, held))
    ]
    for copy in loads:
        copy.start()
    coming[pl.ds(7, DEVICES, stride=8), :] = jnp.ones((DEVICES, 128), F32)
    barrier = pltpu.get_barrier_semaphore()

    def greet(k, _):
        pl.semaphore_signal(barrier, inc=1, device_id=device(k)[1], device_id_type=MESH)
        return 0

    lax.fori_loop(1, DEVICES, greet, 0)
    for copy in loads[:3]:
        copy.wait()
    ranks(owner_ref, rank_ref, run, tri)
    place(owner_ref, rank_ref, pos_ref, vel_ref, going, acc)
    pl.semaphore_wait(barrier, DEVICES - 1)

    def edges(i, first, last, land):
        pair = []
        for end, (src, k) in enumerate(((last, 1), (first, DEVICES - 1))):
            copy = pltpu.make_async_remote_copy(
                src, land.at[end], edge_send.at[i, end], edge_recv.at[i, end],
                device_id=device(k)[1], device_id_type=MESH,
            )
            copy.start()
            pair.append(copy)
        return pair

    def tile(i):
        return pl.ds(pl.multiple_of(8 * i, 8), 8)

    def exchange(i, src, dst, rows):
        def part(t):
            return pl.ds(pl.multiple_of(8 * t, 8), rows)

        for offset in OFFSETS:
            to, where = device_at(offset)
            pltpu.make_async_remote_copy(
                src.at[part(to)], dst.at[part(me)], send_sem.at[i], recv_sem.at[i],
                device_id=where, device_id_type=MESH,
            ).start()

        dst[tile(me), :] = src[tile(me), :]
        others = pl.ds(0, (DEVICES - 1) * rows)
        return pltpu.make_async_remote_copy(
            src.at[others], dst.at[others], send_sem.at[i], recv_sem.at[i],
            device_id=device(1)[1], device_id_type=MESH,
        )

    halo = edges(0, vel_ref.at[:, 0:HALO], vel_ref.at[:, NODE_DEV - HALO : NODE_DEV], vel_in)
    nodes_move = exchange(0, going, coming, 7)
    for copy in loads[3:]:
        copy.wait()
    face_rows(center_ref, angle_ref, stiff_ref, angles, unit, faces)
    lend(list_ref, faces, lent)
    ghosts = edges(1, lent.at[:, 0:GHOST], lent.at[:, GHOST : 2 * GHOST], ghost_in)
    unpack(vel_ref, conn_in, grad_in, stress_in, vel, conn, grad, stress)
    for copy in halo:
        copy.wait()
    vel[pl.ds(0, 5, stride=EXT), :] = vel_in[0]
    vel[pl.ds(ROWS + 1, 5, stride=EXT), :] = vel_in[1]
    elements(vel, conn, grad, area_ref, thick_ref, limit_ref, stress, spread)
    leave = [
        pltpu.make_async_copy(src, dst, out_sem.at[i])
        for i, (src, dst) in enumerate(((stress, cells_hbm), (total, total_hbm)))
    ]
    leave[0].start()
    for copy in ghosts:
        copy.wait()
    faces[:, 0:GHOST] = jnp.where(me > 0, ghost_in[0], 0.0)
    faces[:, GHOST + FACE_DEV :] = jnp.where(me < DEVICES - 1, ghost_in[1], 0.0)
    face_tables(faces, forms, pick, normals)
    nodes_move.wait()

    tiles = coming.reshape(DEVICES, 8, 128)

    def pair_step(b, _):
        first = b * PAIR_STEP
        forces = []
        for i in range(PAIR_STEP):
            x, f = tiles[node_ref[first + i]], face_of_ref[first + i]
            forces.append(pair_force(x, forms[f], lambda c, k, f=f: normals[f, c, k : k + 8]))
        for i, force in enumerate(forces):
            for c in range(3):
                pairs[pl.ds(c * PAIRS + first + i, 1), :] = force[c]
        return 0

    lax.fori_loop(0, PAIRS // PAIR_STEP, pair_step, 0)
    slot = lax.broadcasted_iota(jnp.int32, (1, PAIRS), 1)
    listed = onehot(DEVICES, jnp.where(slot < count_ref[...], node_row_ref[...], -1))
    listed = jnp.concatenate([listed] * 3, axis=1)
    leaving[...] = jnp.zeros_like(leaving)
    for c in range(3):
        parts = jnp.concatenate(split(pairs[c * PAIRS : (c + 1) * PAIRS, :], 3), axis=0)
        leaving[pl.ds(c, DEVICES, stride=8), :] = dot(listed, parts, NN)
    forces_move = exchange(1, leaving, back, 3)

    sum_ref[...] = jnp.zeros_like(sum_ref)
    last = NODE_DEV // 256 - 1
    scatter_blocks([0, last, *range(1, SPREAD_STEP - 1)], conn_in, spread, sum_ref)
    rims = edges(
        2, sum_ref.at[:, 0:HALO], sum_ref.at[:, HALO + NODE_DEV : 2 * HALO + NODE_DEV], rim_in
    )

    def scatter_step(b, _):
        first = b * SPREAD_STEP - 1
        scatter_blocks([first + i for i in range(SPREAD_STEP)], conn_in, spread, sum_ref)
        return 0

    lax.fori_loop(1, NODE_DEV // (256 * SPREAD_STEP), scatter_step, 0)
    for copy in rims:
        copy.wait()
    sum_ref[:, HALO : 2 * HALO] += rim_in[0]
    sum_ref[:, NODE_DEV : NODE_DEV + HALO] += rim_in[1]
    owner_onehots(owner_ref, hots)
    forces_move.wait()
    totals(back, hots, rank_ref, sum_ref, total, side)
    leave[1].start()
    for copy in leave:
        copy.wait()


def owner_onehots(owner_ref, hots):
    def step(b, _):
        at = lane_aligned(b, 1024)
        hots[:, at] = onehot(DEVICES, owner_ref[0:1, at])
        return 0

    lax.fori_loop(0, NODE_DEV // 1024, step, 0)


def totals(back_ref, hots, rank_ref, sum_ref, out_ref, side):
    for c in range(3):
        turned = back_ref[pl.ds(c, DEVICES, stride=8), :].T
        for i, part in enumerate(split(turned, 2)):
            side[128 * c : 128 * c + 128, 128 * i : 128 * i + 128] = part

    def block(b):
        at = lane_aligned(b, 256)
        own = hots[:, at]
        found = dot(side[...], jnp.concatenate([own, own], axis=0), NN)
        rank = rank_ref[0:1, at].astype(jnp.int32)
        mine = lax.broadcasted_iota(jnp.int32, (128, 256), 0) == rank
        contact = [
            jnp.sum(jnp.where(mine, found[128 * c : 128 * c + 128], 0.0), axis=0, keepdims=True)
            for c in range(3)
        ]
        contact = jnp.concatenate([*contact, jnp.zeros((2, 256), F32)], axis=0)
        return contact - sum_ref[0:5, pl.ds(pl.multiple_of(b * 256 + HALO, HALO), 256)]

    def step(b, _):
        done = [block(b * FINISH_STEP + i) for i in range(FINISH_STEP)]
        for i, value in enumerate(done):
            out_ref[:, lane_aligned(b * FINISH_STEP + i, 256)] = value
        return 0

    lax.fori_loop(0, NODE_DEV // (256 * FINISH_STEP), step, 0)


def finish_kernel(
    total_hbm, vel_hbm, mass_hbm, cells_hbm, out_hbm, new_hbm, total, vel, mass, cells, out, new,
    in_sem, out_sem,
):
    size = 5 * ROWS
    moves = [(total_hbm, total), (vel_hbm, vel), (mass_hbm, mass)]
    moves += [
        (cells_hbm.at[pl.ds(i * size, size)], cells.at[pl.ds(i * size, size)]) for i in range(5)
    ]
    inside = [pltpu.make_async_copy(*move, in_sem.at[i]) for i, move in enumerate(moves)]
    for copy in inside:
        copy.start()
    for copy in inside[:3]:
        copy.wait()
    out[...] = vel[...] + mass[...] * total[...]
    outside = [pltpu.make_async_copy(out, out_hbm, out_sem.at[5])]
    outside[0].start()
    for layer in range(5):
        inside[3 + layer].wait()
        for j in range(ROWS):
            part = cells[pl.ds(layer * size + j, 5, stride=ROWS), :]
            new[layer, :, 128 * j : 128 * j + 128] = part
        copy = pltpu.make_async_copy(new.at[layer], new_hbm.at[layer], out_sem.at[layer])
        copy.start()
        outside.append(copy)
    for copy in outside:
        copy.wait()


def body(
    velocity, position, inv_mass, connectivity, shape_grad, area, thickness, yield_stress, stress,
    contact_owner, face_center, face_angle, face_stiffness, ghost_list, pair_node, pair_face,
    pair_count,
):
    square = (ROWS, 128)
    owner = contact_owner.reshape(1, NODE_DEV)
    hbm = pl.BlockSpec(memory_space=pltpu.HBM)
    args = (
        owner, position, velocity, face_center, face_angle, face_stiffness.reshape(1, FACE_DEV),
        ghost_list.reshape(1, 2 * GHOST), connectivity, shape_grad, stress, area.reshape(square),
        thickness.reshape(square), yield_stress.reshape(square), pair_node, pair_face,
        pair_node.reshape(1, PAIRS), pair_count.reshape(1, 1),
    )
    held = [
        (pltpu.SMEM if len(arg.shape) == 1 else pltpu.VMEM)(arg.shape, arg.dtype) for arg in args
    ]
    dma = pltpu.SemaphoreType.DMA
    scratch = [
        ((DEVICES * 8, 128), F32), ((8, NODE_DEV + 2 * HALO), F32), ((1, NODE_DEV), F32),
        ((25 * ROWS, 128), F32), ((5, NODE_DEV), F32), ((3 * 128, 256), BF), ((DEVICES, NODE_DEV), BF),
        ((DEVICES, 128), F32), ((448, 256), F32), ((256, 384), BF),
        ((DEVICES * 8, 128), F32), ((DEVICES * 8, 128), F32), ((FACE_DEV // 64, 128), F32),
        ((FACE_DEV // 16, 128), F32), ((8, FACE_TILES * 128), F32), ((8, 2 * GHOST), F32),
        ((2, 8, GHOST), F32), ((2, 5, HALO), F32), ((5 * EXT, 128), F32),
        ((4 * ROWS, 128), jnp.int32), ((8 * ROWS, 128), F32), ((4, 8 * ROWS, 128), F32),
        ((2, 8, HALO), F32), ((FACE_TILES, 2 * TILE, 96), BF), ((24, 3 * TILE), BF),
        ((FACE_TILES, 3, TILE, TILE), F32), ((3 * PAIRS, 128), F32), ((DEVICES * 8, 128), F32),
    ]
    total, cells = pl.pallas_call(
        step_kernel,
        out_shape=(
            jax.ShapeDtypeStruct((5, NODE_DEV), F32),
            jax.ShapeDtypeStruct((25 * ROWS, 128), F32),
        ),
        in_specs=[hbm] * len(args),
        out_specs=(hbm, hbm),
        scratch_shapes=[
            *held,
            *(pltpu.VMEM(shape, kind) for shape, kind in scratch),
            dma((len(args),)), dma((2,)), dma((2,)), dma((2,)), dma((3, 2)), dma((3, 2)),
        ],
        compiler_params=pltpu.CompilerParams(
            vmem_limit_bytes=56 * 2**20, collective_id=0, has_side_effects=True
        ),
        name="crash_step",
    )(*args)
    last = (total, velocity, inv_mass.reshape(1, NODE_DEV), cells)
    results = (
        jax.ShapeDtypeStruct((5, NODE_DEV), F32),
        jax.ShapeDtypeStruct((5, 5, NODE_DEV), F32),
    )
    return pl.pallas_call(
        finish_kernel,
        out_shape=results,
        in_specs=[hbm] * len(last),
        out_specs=(hbm, hbm),
        scratch_shapes=[
            *(pltpu.VMEM(x.shape, x.dtype) for x in (*last, *results)), dma((8,)), dma((6,)),
        ],
        compiler_params=pltpu.CompilerParams(vmem_limit_bytes=56 * 2**20),
        name="finish",
    )(*last)


def solution(mesh):
    axes = ("dom", "sub")
    nodes, rows, cells = P(axes), P(None, axes), P(None, None, axes)
    in_specs = (
        rows, rows, nodes, rows, cells, nodes, nodes, nodes, cells, P(axes, None), rows, rows,
        nodes, nodes, nodes, nodes, nodes,
    )
    return jax.shard_map(
        body, mesh=mesh, in_specs=in_specs, out_specs=(rows, cells), check_vma=False
    )
```
